512 devices in a mesh: dp: 32 (over z_hi, y), fsdp: 8 (over x, z_lo), section: 2 (over core).
Axes of the slice: x: 4, y: 8, z: 8 (z_hi: 4, z_lo: 2; z = z_hi * 2 + z_lo), core: 2. Of those that a mesh axis runs over, the one named last changes fastest.
Arguments:
- acts: bfloat16 [32768, 5120], P(('dp', 'section'), 'fsdp'), may hold values from -100 to 100
- output_gradient: bfloat16 [32768, 1024], P(('dp', 'section'), 'fsdp'), may hold values from -40 to 40
- lengths: int32 [128], P(('dp', 'section')), may hold values from 1 to 256
- buckets: int32 [128], P(('dp', 'section')), may hold values from 0 to 3
- frozen_key_weight: bfloat16 [5120, 1024], P('fsdp'), may hold values from -0.078125 to 0.078125
- adapter_down_weight: float32 [5120, 128], P('fsdp'), may hold values from -0.078125 to 0.078125
- adapter_up_weight: float32 [128, 1024], P(None, 'fsdp'), may hold values from -0.5 to 0.5
- prompts: bfloat16 [32768, 5120], P(('dp', 'section'), 'fsdp'), may hold values from -6 to 6
Outputs:
- input_gradient: bfloat16 [32768, 5120], P(('dp', 'section'), 'fsdp')
- next_down_weight: float32 [5120, 128], P('fsdp')
- next_up_weight: float32 [128, 1024], P(None, 'fsdp')
- keys: bfloat16 [32768, 1024], P(('dp', 'section'), 'fsdp')
The draws below stay inside these ranges and needn't reach their ends.
All inputs are finite; a program needn't handle non-finite values.
Results may differ from the reference program's by a relative error of at most 0.0059.
Values may be sent and summed in bfloat16 or wider, within the bound.
No kernel may reach another device: no remote copies, remote signals or barrier semaphores. Data moves between devices by JAX's collectives and lax.ppermute only.
A program may use at most 64 MiB of HBM per device.

```python
import jax
import jax.numpy as jnp
from jax import lax

MODEL_WIDTH = 5120
KEY_CHANNELS = 1024
ADAPTER_RANK = 128
SLOT = 256
SEQS = 128
TOKENS = 32768
PROMPTS = 32768


def rising_scale(key, count, reach, jitter):
    ramp = jnp.arange(count, dtype=jnp.int32).astype(jnp.float32) / jnp.float32(max(count - 1, 1))
    noise = jax.random.uniform(key, (1, count), jnp.float32, -jitter, jitter)
    return jnp.exp(reach * (2.0 * ramp[None, :] - 1.0) + noise)


def draw_acts(key, part):
    key = jax.random.fold_in(key, 11)
    key_rows, key_cols, key_base = jax.random.split(key, 3)
    row_scale = jnp.exp(jax.random.uniform(key_rows, (TOKENS, 1), jnp.float32, -0.8, 0.8))
    col_scale = rising_scale(key_cols, MODEL_WIDTH, 1.0, 0.5)
    base_vals = jnp.clip(jax.random.normal(key_base, (TOKENS, MODEL_WIDTH), jnp.float32), -6.0, 6.0)
    return (base_vals * row_scale * col_scale).astype(jnp.bfloat16)


def draw_output_gradient(key, part):
    key = jax.random.fold_in(key, 23)
    key_cols, key_base = jax.random.split(key, 2)
    col_scale = rising_scale(key_cols, KEY_CHANNELS, 0.9, 0.4)
    base_vals = jnp.clip(jax.random.normal(key_base, (TOKENS, KEY_CHANNELS), jnp.float32), -6.0, 6.0)
    return (base_vals * col_scale).astype(jnp.bfloat16)


def with_ends(values, rng, least, largest):
    dims = values.shape
    index_at = [jax.random.randint(jax.random.fold_in(rng, axis), (), 0, dims[axis]) for axis in range(len(dims))]
    values = values.at[tuple(index_at)].set(least)
    longest = dims.index(max(dims))
    index_at[longest] = (index_at[longest] + 1) % dims[longest]
    return values.at[tuple(index_at)].set(largest)


def shard_levels(key, shape, pieces, smallest, top_value):
    def one(position, parts):
        draws = jax.random.uniform(jax.random.fold_in(jax.random.fold_in(key, 6), position), (parts,), jnp.float32, smallest / len(pieces), top_value / len(pieces))
        return jnp.repeat(jnp.exp(draws), shape[position] // parts).reshape((-1,) + (1,) * (len(shape) - position - 1))

    gain = one(*pieces[0])
    for cut in pieces[1:]:
        gain = gain * one(*cut)
    return gain


def bell_draw(stream_key, shape, deviation, most, cuts=(), kind=jnp.bfloat16):
    drawn = deviation * jax.random.normal(stream_key, shape, jnp.float32)
    if cuts:
        drawn = drawn * shard_levels(stream_key, shape, cuts, -0.22, 0.18)
    return jnp.clip(drawn, -most, most).astype(kind)


def setup_inputs(seed: int = 0) -> dict:
    splits = jax.random.split(jax.random.key(seed), 9)
    acts = draw_acts(jax.random.fold_in(splits[8], 71), 0)
    output_gradient = draw_output_gradient(jax.random.fold_in(splits[8], 71), 0)
    lengths = with_ends(jax.random.randint(splits[2], (SEQS,), 1, SLOT + 1), jax.random.fold_in(splits[2], 1), 1, SLOT).astype(jnp.int32)
    buckets = with_ends(jax.random.randint(splits[3], (SEQS,), 0, 4), jax.random.fold_in(splits[3], 1), 0, 3).astype(jnp.int32)
    frozen_key_weight = bell_draw(splits[4], (MODEL_WIDTH, KEY_CHANNELS), MODEL_WIDTH ** -0.5, 0.078125, ((0, 8),))
    adapter_down_weight = bell_draw(splits[5], (MODEL_WIDTH, ADAPTER_RANK), MODEL_WIDTH ** -0.5, 0.078125, ((0, 8),), jnp.float32)
    adapter_up_weight = bell_draw(splits[6], (ADAPTER_RANK, KEY_CHANNELS), ADAPTER_RANK ** -0.5, 0.5, ((1, 8),), jnp.float32)
    prompts = bell_draw(splits[7], (PROMPTS, MODEL_WIDTH), 1.0, 6.0, ((0, 64), (1, 8)))
    return {"acts": acts, "output_gradient": output_gradient, "lengths": lengths, "buckets": buckets, "frozen_key_weight": frozen_key_weight, "adapter_down_weight": adapter_down_weight, "adapter_up_weight": adapter_up_weight, "prompts": prompts}


adapter_scale = 0.5
step_rate = 16.0
clip_norm = 1.0

def reference(acts, output_gradient, lengths, buckets, frozen_key_weight, adapter_down_weight, adapter_up_weight, prompts):
    slot_pos = jnp.arange(TOKENS, dtype=jnp.int32) % SLOT
    seq_len = jnp.repeat(lengths, SLOT)
    advantage = jnp.repeat(buckets.astype(jnp.float32) - 1.5, SLOT)
    token_weight = jnp.where(slot_pos < seq_len, advantage, jnp.float32(0.0))
    key_gradient = (token_weight[:, None] * output_gradient.astype(jnp.float32)).astype(jnp.bfloat16)
    first_factor_half = adapter_down_weight.astype(jnp.bfloat16)
    second_factor_half = adapter_up_weight.astype(jnp.bfloat16)
    down_acts = jnp.dot(acts, first_factor_half, preferred_element_type=jnp.float32)
    up_grads = jnp.dot(key_gradient, second_factor_half.T, preferred_element_type=jnp.float32)
    down_weight_half = down_acts.astype(jnp.bfloat16)
    up_weight_half = up_grads.astype(jnp.bfloat16)
    up_gradient = adapter_scale * jnp.dot(down_weight_half.T, key_gradient, preferred_element_type=jnp.float32)
    down_gradient = adapter_scale * jnp.dot(acts.T, up_weight_half, preferred_element_type=jnp.float32)
    squares = jnp.sum(down_gradient * down_gradient) + jnp.sum(up_gradient * up_gradient)
    norm = jnp.sqrt(squares + 1e-12)
    scale_factor = step_rate * jnp.minimum(1.0, clip_norm / norm)
    next_down_weight = adapter_down_weight - scale_factor * down_gradient
    next_up_weight = adapter_up_weight - scale_factor * up_gradient
    input_gradient = jnp.dot(key_gradient, frozen_key_weight.T, preferred_element_type=jnp.float32)
    input_gradient = input_gradient + adapter_scale * jnp.dot(up_weight_half, first_factor_half.T, preferred_element_type=jnp.float32)
    weight_change = jnp.dot(next_down_weight, next_up_weight, precision=lax.Precision.HIGHEST)
    combined_weight = (frozen_key_weight.astype(jnp.float32) + adapter_scale * weight_change).astype(jnp.bfloat16)
    keys = jnp.dot(prompts, combined_weight, preferred_element_type=jnp.float32).astype(jnp.bfloat16)
    return (input_gradient.astype(jnp.bfloat16), next_down_weight, next_up_weight, keys)
```

```python
import jax
import jax.numpy as jnp
from jax import lax
from jax.experimental import pallas as pl
from jax.experimental.pallas import tpu as pltpu
from jax.sharding import Mesh
from jax.sharding import PartitionSpec as P

adapter_scale = 0.5
step_rate = 16.0
clip_norm = 1.0

AXES = ("zhi", "y", "x", "zlo", "core")
DP = ("zhi", "y")
FSDP = ("x", "zlo")
ROWS = ("zhi", "y", "core")
bf16 = jnp.bfloat16
f32 = jnp.float32


def swap(v, axis):
    return lax.all_to_all(v, axis, 0, 0, tiled=True)


def spread(v, axis, n):
    return swap(jnp.broadcast_to(v[None], (n,) + v.shape).reshape((n * v.shape[0],) + v.shape[1:]), axis)


def base_kernel(p_ref, w_ref, o_ref):
    o_ref[...] = jnp.dot(p_ref[...], w_ref[...], preferred_element_type=f32).astype(bf16)


def base_partials(prompts, weight, n):
    rows, width = prompts.shape
    cols = weight.shape[1] // n
    return pl.pallas_call(
        base_kernel,
        grid=(n,),
        in_specs=[
            pl.BlockSpec((rows, width), lambda k: (0, 0)),
            pl.BlockSpec((width, cols), lambda k: (0, k)),
        ],
        out_specs=pl.BlockSpec((rows, cols), lambda k: (k, 0)),
        out_shape=jax.ShapeDtypeStruct((n * rows, cols), bf16),
        compiler_params=pltpu.CompilerParams(vmem_limit_bytes=32 * 1024 * 1024),
        cost_estimate=pl.CostEstimate(
            flops=2 * rows * width * cols * n, bytes_accessed=4 * 1024 * 1024, transcendentals=0
        ),
    )(prompts, weight)


def per_device(acts, output_gradient, lengths, buckets, frozen, down_w, up_w, prompts):
    rows = acts.shape[0]
    slot = rows // lengths.shape[0]
    n_f = lax.axis_size(FSDP)
    n_d = lax.axis_size(DP)
    core = lax.axis_index("core")
    width, rank = down_w.shape

    alive = jnp.arange(slot, dtype=jnp.int32)[None, :] < lengths[:, None]
    adv = buckets.astype(f32)[:, None] - 1.5
    token_weight = jnp.where(alive, adv, f32(0.0)).reshape(rows)
    gk = (token_weight[:, None] * output_gradient.astype(f32)).astype(bf16)
    gk_full = lax.all_gather(gk, FSDP, axis=1, tiled=True)

    a_half = down_w.astype(bf16)
    b_half = up_w.astype(bf16)
    parts = jnp.concatenate(
        [
            jnp.dot(gk, b_half.T, preferred_element_type=f32),
            jnp.dot(acts, a_half, preferred_element_type=f32),
            jnp.dot(prompts, a_half, preferred_element_type=f32),
        ],
        axis=1,
    )
    base_parts = base_partials(prompts, frozen, n_f)
    keys_base = lax.psum_scatter(base_parts, FSDP, scatter_dimension=0, tiled=True)

    sums = swap(parts, FSDP).reshape(n_f, rows // n_f, 3 * rank).sum(0).astype(bf16)
    full = spread(sums, FSDP, n_f)
    up_half, down_half, p_a = full[:, :rank], full[:, rank : 2 * rank], full[:, 2 * rank :]

    g_down = adapter_scale * jnp.dot(acts.T, up_half, preferred_element_type=f32)
    g_up = adapter_scale * jnp.dot(down_half.T, gk, preferred_element_type=f32)
    g = jnp.concatenate([g_down, g_up], axis=0)
    half = g.shape[0] // 2
    g2 = g.reshape(2, half, g.shape[1])
    other = lax.ppermute(
        lax.dynamic_index_in_dim(g2, 1 - core, 0, keepdims=False), "core", [(0, 1), (1, 0)]
    )
    mine = lax.dynamic_index_in_dim(g2, core, 0, keepdims=False) + other
    part = swap(mine, DP).reshape(n_d, half // n_d, g.shape[1]).sum(0)
    mine = spread(part, DP, n_d)
    other = lax.ppermute(mine, "core", [(0, 1), (1, 0)])
    first = jnp.where(core == 0, mine, other)
    second = jnp.where(core == 0, other, mine)
    g = jnp.concatenate([first, second], axis=0)
    g_down, g_up = g[:width], g[width:]

    sq = jnp.sum(g * g)
    hi = sq.astype(bf16)
    mid = (sq - hi.astype(f32)).astype(bf16)
    low = (sq - hi.astype(f32) - mid.astype(f32)).astype(bf16)
    lanes = jnp.arange(rank)[None, :]
    tail = jnp.where(lanes == 0, hi, jnp.where(lanes == 1, mid, jnp.where(lanes == 2, low, bf16(0))))
    tail = jnp.broadcast_to(tail, (16, rank))
    p_g = jnp.dot(prompts, g_down.astype(bf16), preferred_element_type=f32).astype(bf16)
    got = spread(jnp.concatenate([p_g, tail], axis=0), FSDP, n_f).reshape(n_f, rows + 16, rank)
    p_g = got[:, :rows].astype(f32).sum(0)
    sq = got[:, rows, :3].astype(f32).sum()
    factor = step_rate * jnp.minimum(1.0, clip_norm / jnp.sqrt(sq + 1e-12))
    next_down = down_w - factor * g_down
    next_up = up_w - factor * g_up
    proj = p_a.astype(f32) - factor * p_g
    keys = keys_base.astype(f32) + adapter_scale * jnp.dot(
        proj.astype(bf16), next_up.astype(bf16), preferred_element_type=f32
    )

    input_gradient = adapter_scale * jnp.dot(
        up_half, a_half.T, preferred_element_type=f32
    ) + jnp.dot(gk_full, frozen.T, preferred_element_type=f32)
    return input_gradient.astype(bf16), next_down, next_up, keys.astype(bf16)


def solution(mesh):
    dp, fsdp, section = mesh.devices.shape
    fine = Mesh(mesh.devices.reshape(4, dp // 4, fsdp // 2, 2, section), AXES)
    rows_by_width = P(ROWS, FSDP)
    return jax.shard_map(
        per_device,
        mesh=fine,
        in_specs=(
            rows_by_width,
            rows_by_width,
            P(ROWS),
            P(ROWS),
            P(FSDP, None),
            P(FSDP, None),
            P(None, FSDP),
            rows_by_width,
        ),
        out_specs=(rows_by_width, P(FSDP, None), P(None, FSDP), rows_by_width),
        check_vma=False,
    )
```

```python
import jax
import jax.numpy as jnp
from jax import lax
from jax.experimental import pallas as pl
from jax.experimental.pallas import tpu as pltpu
from jax.sharding import Mesh
from jax.sharding import PartitionSpec as P

adapter_scale = 0.5
step_rate = 16.0
clip_norm = 1.0

AXES = ("zhi", "y", "x", "zlo", "core")
FSDP = ("x", "zlo")
ROWS = ("zhi", "y", "core")
NEAR = ("y", "core")
FAR = "zhi"
TAIL = 16
bf16 = jnp.bfloat16
f32 = jnp.float32

NT = (((1,), (1,)), ((), ()))
TN = (((0,), (0,)), ((), ()))


def dot(a, b, dims=(((1,), (0,)), ((), ()))):
    return lax.dot_general(a, b, dims, preferred_element_type=f32)


def swap(v, axis):
    return lax.all_to_all(v, axis, 0, 0, tiled=True)


VMEM = None
SMEM = pl.BlockSpec(memory_space=pltpu.SMEM)
ANY = pl.BlockSpec(memory_space=pl.ANY)


def block(v):
    zeros = (0,) * len(v.shape)
    return pl.BlockSpec(v.shape, lambda i: zeros)


def call(kernel, outs, ins, args, flops=0, out_specs=None, **more):
    moved = sum(a.size * a.dtype.itemsize for a in args) + sum(
        o.size * o.dtype.itemsize for o in outs
    )
    return pl.pallas_call(
        kernel,
        grid=(1,),
        in_specs=[spec or block(a) for spec, a in zip(ins, args, strict=True)],
        out_specs=out_specs or tuple(block(o) for o in outs),
        out_shape=tuple(outs),
        compiler_params=pltpu.CompilerParams(vmem_limit_bytes=40 * 1024 * 1024),
        cost_estimate=pl.CostEstimate(flops=flops, bytes_accessed=moved, transcendentals=0),
        **more,
    )(*args)


def shape(dims, kind):
    return jax.ShapeDtypeStruct(dims, kind)


def parts_kernel(lens, buckets, acts, og, down_w, up_w, prompts, gk_ref, pay_ref):
    rows = acts.shape[0]
    seqs = lens.shape[0]
    slot = rows // seqs
    peers = pay_ref.shape[0]
    piece = rows // peers
    place = lax.broadcasted_iota(jnp.int32, (slot, 1), 0)
    for s in range(seqs):
        here = pl.ds(s * slot, slot)
        weight = jnp.where(place < lens[s], buckets[s].astype(f32) - 1.5, f32(0.0))
        gk_ref[here, :] = (weight * og[here, :].astype(f32)).astype(bf16)
    gk = gk_ref[...]
    a_half = down_w[...].astype(bf16)
    up = dot(gk, up_w[...].astype(bf16), NT).astype(bf16)
    down = dot(acts[...], a_half).astype(bf16)
    proj = dot(prompts[...], a_half).astype(bf16)
    for j in range(peers):
        here = slice(j * piece, (j + 1) * piece)
        pay_ref[j, 0:piece, :] = up[here]
        pay_ref[j, piece : 2 * piece, :] = down[here]
        pay_ref[j, 2 * piece : 3 * piece, :] = proj[here]
        pay_ref[j, 3 * piece :, :] = gk


def base_kernel(prompts, frozen, pay_ref):
    peers, long, cols = pay_ref.shape
    rows = prompts.shape[0]
    base = dot(prompts[...], frozen[...]).astype(bf16)
    for j in range(peers):
        pay_ref[j, long - rows :, :] = base[:, j * cols : (j + 1) * cols]


def sums_kernel(got_ref, pay_in, pay_ref, sums_ref, sems):
    del pay_in
    peers = got_ref.shape[0]
    part = sums_ref.shape[0]
    total = got_ref[0, :part, :].astype(f32)
    for j in range(1, peers):
        total += got_ref[j, :part, :].astype(f32)
    sums_ref[...] = total.astype(bf16)
    copies = [
        pltpu.make_async_copy(sums_ref, pay_ref.at[j, pl.ds(0, part), :], sems.at[j])
        for j in range(peers)
    ]
    for c in copies:
        c.start()
    for c in copies:
        c.wait()


def rejoin(got_ref, first, piece):
    return jnp.concatenate(
        [got_ref[j, first : first + piece, :] for j in range(got_ref.shape[0])], axis=0
    )


def grads_kernel(got_ref, acts, gk, pay_ref):
    rows = acts.shape[0]
    piece = rows // got_ref.shape[0]
    lanes = gk.shape[1]
    up = rejoin(got_ref, 0, piece)
    down = rejoin(got_ref, piece, piece)
    g = adapter_scale * jnp.concatenate([dot(up, acts[...], TN), dot(down, gk[...], TN)], axis=1)
    peers = pay_ref.shape[0]
    step = g.shape[0] // peers
    for j in range(peers):
        pay_ref[j] = jnp.concatenate(
            [
                g[j * step : (j + 1) * step, c * lanes : (c + 1) * lanes]
                for c in range(g.shape[1] // lanes)
            ],
            axis=0,
        ).astype(pay_ref.dtype)


def add_kernel(got_ref, pay_ref):
    total = got_ref[0].astype(f32)
    for j in range(1, got_ref.shape[0]):
        total += got_ref[j].astype(f32)
    total = total.astype(pay_ref.dtype)
    for j in range(pay_ref.shape[0]):
        pay_ref[j] = total


def whole_gradient(got_ref, rank):
    peers, long, _ = got_ref.shape
    step = rank // peers
    got = [got_ref[j].astype(f32) for j in range(peers)]
    return [
        jnp.concatenate([v[c * step : (c + 1) * step] for v in got], axis=0)
        for c in range(long // step)
    ]


def project_kernel(got_ref, prompts, pay_ref):
    rank = pay_ref.shape[2]
    rows = prompts.shape[0]
    blocks = whole_gradient(got_ref, rank)
    squares = sum(b * b for b in blocks)
    total = jnp.sum(squares, keepdims=True)
    high = total.astype(bf16)
    rest = total - high.astype(f32)
    middle = rest.astype(bf16)
    low = (rest - middle.astype(f32)).astype(bf16)
    lane = lax.broadcasted_iota(jnp.int32, (TAIL, rank), 1)
    tail = jnp.where(
        lane == 0,
        high.astype(f32),
        jnp.where(lane == 1, middle.astype(f32), jnp.where(lane == 2, low.astype(f32), 0.0)),
    ).astype(bf16)
    g_down = jnp.concatenate(blocks[:-1], axis=1).astype(bf16)
    proj = dot(prompts[...], g_down, NT).astype(bf16)
    for j in range(pay_ref.shape[0]):
        pay_ref[j, :rows, :] = proj
        pay_ref[j, rows:, :] = tail


def finish_kernel(got, got_base, got_g, down_w, up_w, next_down, next_up, keys):
    rows = keys.shape[0]
    rank = down_w.shape[1]
    peers = got.shape[0]
    piece = rows // peers
    lane = lax.broadcasted_iota(jnp.int32, (TAIL, rank), 1)
    place = lax.broadcasted_iota(jnp.int32, (TAIL, rank), 0)
    p_g = got[0, :rows, :].astype(f32)
    tail = got[0, rows:, :].astype(f32)
    base = got_base[0, 3 * piece :, :].astype(f32)
    for j in range(1, peers):
        p_g += got[j, :rows, :].astype(f32)
        tail += got[j, rows:, :].astype(f32)
        base += got_base[j, 3 * piece :, :].astype(f32)
    squares = jnp.sum(jnp.where((place == 0) & (lane < 3), tail, 0.0), keepdims=True)
    factor = step_rate * jnp.minimum(1.0, clip_norm / jnp.sqrt(squares + 1e-12))
    blocks = whole_gradient(got_g, rank)
    for c, block in enumerate(blocks[:-1]):
        here = pl.ds(c * rank, rank)
        next_down[here, :] = down_w[here, :] - factor * block.T
    new_up = up_w[...] - factor * blocks[-1]
    next_up[...] = new_up
    proj = rejoin(got_base, 2 * piece, piece).astype(f32) - factor * p_g
    keys[...] = (base + adapter_scale * dot(proj.astype(bf16), new_up.astype(bf16))).astype(bf16)


def input_kernel(got_gk, got_up, down_w, frozen, out):
    rows = out.shape[0]
    piece = rows // got_up.shape[0]
    gk = jnp.concatenate([got_gk[j, 3 * piece :, :] for j in range(got_gk.shape[0])], axis=1)
    up = rejoin(got_up, 0, piece)
    a_half = down_w[...].astype(bf16)
    out[...] = (dot(gk, frozen[...], NT) + adapter_scale * dot(up, a_half, NT)).astype(bf16)


def per_device(acts, output_gradient, lengths, buckets, frozen, down_w, up_w, prompts):
    rows = acts.shape[0]
    width, rank = down_w.shape
    cols = up_w.shape[1]
    n_f = lax.axis_size(FSDP)
    n_near = lax.axis_size(NEAR)
    n_far = lax.axis_size(FAR)
    piece = rows // n_f
    long = 3 * piece + rows
    slab = (width + cols) // n_near

    gk, pay = call(
        parts_kernel,
        [shape((rows, cols), bf16), shape((n_f, long, rank), bf16)],
        [SMEM, SMEM] + [VMEM] * 5,
        (lengths, buckets, acts, output_gradient, down_w, up_w, prompts),
        flops=2 * rows * rank * (2 * width + cols),
    )
    got_gk = swap(pay, FSDP)
    (pay,) = call(
        base_kernel,
        [shape((n_f, long, cols), bf16)],
        [VMEM, VMEM],
        (prompts, frozen),
        flops=2 * rows * width * cols * n_f,
    )
    (pay,) = call(
        sums_kernel,
        [shape((n_f, long, cols), bf16)],
        [VMEM, ANY],
        (got_gk, pay),
        input_output_aliases={1: 0},
        out_specs=(ANY,),
        scratch_shapes=[pltpu.VMEM((3 * piece, rank), bf16), pltpu.SemaphoreType.DMA((n_f,))],
    )
    got_base = swap(pay, FSDP)

    (pay,) = call(
        grads_kernel,
        [shape((n_near, slab, rank), bf16)],
        [VMEM] * 3,
        (got_base, acts, gk),
        flops=2 * rows * rank * (width + cols),
    )
    got = swap(pay, NEAR)
    (input_gradient,) = call(
        input_kernel,
        [shape((rows, width), bf16)],
        [VMEM] * 4,
        (got_gk, got_base, down_w, frozen),
        flops=2 * rows * width * (cols * n_f + rank),
    )
    (pay,) = call(add_kernel, [shape((n_far, slab, rank), bf16)], [VMEM], (got,))
    got = swap(pay, FAR)
    (pay,) = call(add_kernel, [shape((n_near, slab, rank), bf16)], [VMEM], (got,))
    got_g = swap(pay, NEAR)
    (pay,) = call(
        project_kernel,
        [shape((n_f, rows + TAIL, rank), bf16)],
        [VMEM] * 2,
        (got_g, prompts),
        flops=2 * rows * width * rank,
    )
    got = swap(pay, FSDP)
    next_down, next_up, keys = call(
        finish_kernel,
        [shape((width, rank), f32), shape((rank, cols), f32), shape((rows, cols), bf16)],
        [VMEM] * 5,
        (got, got_base, got_g, down_w, up_w),
        flops=2 * rows * rank * cols,
    )
    return input_gradient, next_down, next_up, keys


def solution(mesh):
    dp, fsdp, section = mesh.devices.shape
    fine = Mesh(mesh.devices.reshape(4, dp // 4, fsdp // 2, 2, section), AXES)
    rows_by_width = P(ROWS, FSDP)
    return jax.shard_map(
        per_device,
        mesh=fine,
        in_specs=(
            rows_by_width,
            rows_by_width,
            P(ROWS),
            P(ROWS),
            P(FSDP, None),
            P(FSDP, None),
            P(None, FSDP),
            rows_by_width,
        ),
        out_specs=(rows_by_width, P(FSDP, None), P(None, FSDP), rows_by_width),
        check_vma=False,
    )
```

```python
import jax
import jax.numpy as jnp
from jax import lax
from jax.experimental import pallas as pl
from jax.experimental.pallas import tpu as pltpu
from jax.sharding import Mesh
from jax.sharding import PartitionSpec as P

adapter_scale = 0.5
step_rate = 16.0
clip_norm = 1.0

AXES = ("zhi", "y", "x", "zlo", "core")
FSDP = ("x", "zlo")
ROWS = ("zhi", "y", "core")
NEAR = ("y", "core")
FAR = "zhi"
TAIL = 16
bf16 = jnp.bfloat16
f32 = jnp.float32

NT = (((1,), (1,)), ((), ()))
TN = (((0,), (0,)), ((), ()))


def dot(a, b, dims=(((1,), (0,)), ((), ()))):
    return lax.dot_general(a, b, dims, preferred_element_type=f32)


def swap(v, axis):
    return lax.all_to_all(v, axis, 0, 0, tiled=True)


VMEM = None
SMEM = pl.BlockSpec(memory_space=pltpu.SMEM)
ANY = pl.BlockSpec(memory_space=pl.ANY)


def block(v):
    zeros = (0,) * len(v.shape)
    return pl.BlockSpec(v.shape, lambda i: zeros)


def call(kernel, outs, ins, args, flops=0, out_specs=None, limit=24, **more):
    moved = sum(a.size * a.dtype.itemsize for a in args) + sum(
        o.size * o.dtype.itemsize for o in outs
    )
    return pl.pallas_call(
        kernel,
        grid=(1,),
        in_specs=[spec or block(a) for spec, a in zip(ins, args, strict=True)],
        out_specs=out_specs or tuple(block(o) for o in outs),
        out_shape=tuple(outs),
        compiler_params=pltpu.CompilerParams(vmem_limit_bytes=limit * 1024 * 1024),
        cost_estimate=pl.CostEstimate(flops=flops, bytes_accessed=moved, transcendentals=0),
        **more,
    )(*args)


def shape(dims, kind):
    return jax.ShapeDtypeStruct(dims, kind)


def parts_kernel(
    lens, buckets, acts, og, down_w, up_w, prompts, gk_out, pay,
    acts_v, og_v, down_v, up_v, prompts_v, gk, parts, sems,
):
    rows = acts.shape[0]
    seqs = lens.shape[0]
    slot = rows // seqs
    peers = pay.shape[0]
    piece = rows // peers
    pairs = ((og, og_v), (up_w, up_v), (down_w, down_v), (acts, acts_v), (prompts, prompts_v))
    loads = [pltpu.make_async_copy(a, b, sems.at[i]) for i, (a, b) in enumerate(pairs)]
    for c in loads:
        c.start()
    loads[0].wait()
    place = lax.broadcasted_iota(jnp.int32, (slot, 1), 0)
    for s in range(seqs):
        here = pl.ds(s * slot, slot)
        weight = jnp.where(place < lens[s], buckets[s].astype(f32) - 1.5, f32(0.0))
        gk[here, :] = (weight * og_v[here, :].astype(f32)).astype(bf16)
    first = len(pairs)
    stores = [pltpu.make_async_copy(gk, gk_out, sems.at[first])] + [
        pltpu.make_async_copy(gk, pay.at[j, pl.ds(3 * piece, rows), :], sems.at[first + 1 + j])
        for j in range(peers)
    ]
    for c in stores:
        c.start()

    def put(k, v):
        v = v.astype(bf16)
        for j in range(peers):
            parts[j, k * piece : (k + 1) * piece, :] = v[j * piece : (j + 1) * piece]

    loads[1].wait()
    put(0, dot(gk[...], up_v[...].astype(bf16), NT))
    loads[2].wait()
    a_half = down_v[...].astype(bf16)
    loads[3].wait()
    put(1, dot(acts_v[...], a_half))
    loads[4].wait()
    put(2, dot(prompts_v[...], a_half))
    last = pltpu.make_async_copy(
        parts, pay.at[:, pl.ds(0, 3 * piece), :], sems.at[first + 1 + peers]
    )
    last.start()
    for c in stores:
        c.wait()
    last.wait()


def base_kernel(prompts, frozen, pay_ref):
    peers, long, cols = pay_ref.shape
    rows = prompts.shape[0]
    base = dot(prompts[...], frozen[...]).astype(bf16)
    for j in range(peers):
        pay_ref[j, long - rows :, :] = base[:, j * cols : (j + 1) * cols]


def sums_kernel(got_ref, pay_in, pay_ref, sums_ref, sems):
    del pay_in
    peers = got_ref.shape[0]
    part = sums_ref.shape[0]
    total = got_ref[0, :part, :].astype(f32)
    for j in range(1, peers):
        total += got_ref[j, :part, :].astype(f32)
    sums_ref[...] = total.astype(bf16)
    copies = [
        pltpu.make_async_copy(sums_ref, pay_ref.at[j, pl.ds(0, part), :], sems.at[j])
        for j in range(peers)
    ]
    for c in copies:
        c.start()
    for c in copies:
        c.wait()


def rejoin(got_ref, first, piece):
    return jnp.concatenate(
        [got_ref[j, first : first + piece, :] for j in range(got_ref.shape[0])], axis=0
    )


def grads_kernel(got_ref, acts, gk, pay_ref):
    rows = acts.shape[0]
    piece = rows // got_ref.shape[0]
    lanes = gk.shape[1]
    up = rejoin(got_ref, 0, piece)
    down = rejoin(got_ref, piece, piece)
    g = adapter_scale * jnp.concatenate([dot(up, acts[...], TN), dot(down, gk[...], TN)], axis=1)
    peers = pay_ref.shape[0]
    step = g.shape[0] // peers
    for j in range(peers):
        pay_ref[j] = jnp.concatenate(
            [
                g[j * step : (j + 1) * step, c * lanes : (c + 1) * lanes]
                for c in range(g.shape[1] // lanes)
            ],
            axis=0,
        ).astype(pay_ref.dtype)


def add_kernel(got_ref, pay_ref):
    total = got_ref[0].astype(f32)
    for j in range(1, got_ref.shape[0]):
        total += got_ref[j].astype(f32)
    total = total.astype(pay_ref.dtype)
    for j in range(pay_ref.shape[0]):
        pay_ref[j] = total


def whole_gradient(got_ref, rank):
    peers, long, _ = got_ref.shape
    step = rank // peers
    got = [got_ref[j].astype(f32) for j in range(peers)]
    return [
        jnp.concatenate([v[c * step : (c + 1) * step] for v in got], axis=0)
        for c in range(long // step)
    ]


def project_kernel(got_ref, prompts, pay_ref):
    rank = pay_ref.shape[2]
    rows = prompts.shape[0]
    blocks = whole_gradient(got_ref, rank)
    squares = sum(b * b for b in blocks)
    total = jnp.sum(squares, keepdims=True)
    high = total.astype(bf16)
    rest = total - high.astype(f32)
    middle = rest.astype(bf16)
    low = (rest - middle.astype(f32)).astype(bf16)
    lane = lax.broadcasted_iota(jnp.int32, (TAIL, rank), 1)
    tail = jnp.where(
        lane == 0,
        high.astype(f32),
        jnp.where(lane == 1, middle.astype(f32), jnp.where(lane == 2, low.astype(f32), 0.0)),
    ).astype(bf16)
    g_down = jnp.concatenate(blocks[:-1], axis=1).astype(bf16)
    proj = dot(prompts[...], g_down, NT).astype(bf16)
    for j in range(pay_ref.shape[0]):
        pay_ref[j, :rows, :] = proj
        pay_ref[j, rows:, :] = tail


def finish_kernel(got, got_base, base, got_g, down_w, up_w, next_down, next_up, keys):
    rows = keys.shape[0]
    rank = down_w.shape[1]
    peers = got.shape[0]
    piece = rows // peers
    lane = lax.broadcasted_iota(jnp.int32, (TAIL, rank), 1)
    place = lax.broadcasted_iota(jnp.int32, (TAIL, rank), 0)
    p_g = got[0, :rows, :].astype(f32)
    tail = got[0, rows:, :].astype(f32)
    for j in range(1, peers):
        p_g += got[j, :rows, :].astype(f32)
        tail += got[j, rows:, :].astype(f32)
    squares = jnp.sum(jnp.where((place == 0) & (lane < 3), tail, 0.0), keepdims=True)
    factor = step_rate * jnp.minimum(1.0, clip_norm / jnp.sqrt(squares + 1e-12))
    blocks = whole_gradient(got_g, rank)
    for c, block in enumerate(blocks[:-1]):
        here = pl.ds(c * rank, rank)
        next_down[here, :] = down_w[here, :] - factor * block.T
    new_up = up_w[...] - factor * blocks[-1]
    next_up[...] = new_up
    proj = rejoin(got_base, 2 * piece, piece).astype(f32) - factor * p_g
    keys[...] = (base[...] + adapter_scale * dot(proj.astype(bf16), new_up.astype(bf16))).astype(bf16)


def input_kernel(got_gk, got_up, down_w, frozen, out, base_out):
    rows = out.shape[0]
    first = got_up.shape[1] - rows
    base = got_up[0, first:, :].astype(f32)
    for j in range(1, got_up.shape[0]):
        base += got_up[j, first:, :].astype(f32)
    base_out[...] = base
    piece = rows // got_up.shape[0]
    gk = jnp.concatenate([got_gk[j, 3 * piece :, :] for j in range(got_gk.shape[0])], axis=1)
    up = rejoin(got_up, 0, piece)
    a_half = down_w[...].astype(bf16)
    out[...] = (dot(gk, frozen[...], NT) + adapter_scale * dot(up, a_half, NT)).astype(bf16)


def per_device(acts, output_gradient, lengths, buckets, frozen, down_w, up_w, prompts):
    rows = acts.shape[0]
    width, rank = down_w.shape
    cols = up_w.shape[1]
    n_f = lax.axis_size(FSDP)
    n_near = lax.axis_size(NEAR)
    n_far = lax.axis_size(FAR)
    piece = rows // n_f
    long = 3 * piece + rows
    slab = (width + cols) // n_near

    gk, pay = call(
        parts_kernel,
        [shape((rows, cols), bf16), shape((n_f, long, rank), bf16)],
        [SMEM, SMEM] + [ANY] * 5,
        (lengths, buckets, acts, output_gradient, down_w, up_w, prompts),
        out_specs=(ANY, ANY),
        limit=60,
        scratch_shapes=[
            pltpu.VMEM((rows, width), bf16),
            pltpu.VMEM((rows, cols), bf16),
            pltpu.VMEM((width, rank), f32),
            pltpu.VMEM((rank, cols), f32),
            pltpu.VMEM((rows, width), bf16),
            pltpu.VMEM((rows, cols), bf16),
            pltpu.VMEM((n_f, 3 * piece, rank), bf16),
            pltpu.SemaphoreType.DMA((7 + n_f,)),
        ],
        flops=2 * rows * rank * (2 * width + cols),
    )
    got_gk = swap(pay, FSDP)
    (pay,) = call(
        base_kernel,
        [shape((n_f, long, cols), bf16)],
        [VMEM, VMEM],
        (prompts, frozen),
        flops=2 * rows * width * cols * n_f,
    )
    (pay,) = call(
        sums_kernel,
        [shape((n_f, long, cols), bf16)],
        [VMEM, ANY],
        (got_gk, pay),
        input_output_aliases={1: 0},
        out_specs=(ANY,),
        scratch_shapes=[pltpu.VMEM((3 * piece, rank), bf16), pltpu.SemaphoreType.DMA((n_f,))],
    )
    got_base = swap(pay, FSDP)

    (pay,) = call(
        grads_kernel,
        [shape((n_near, slab, rank), bf16)],
        [VMEM] * 3,
        (got_base, acts, gk),
        flops=2 * rows * rank * (width + cols),
    )
    got = swap(pay, NEAR)
    input_gradient, base = call(
        input_kernel,
        [shape((rows, width), bf16), shape((rows, cols), f32)],
        [VMEM] * 4,
        (got_gk, got_base, down_w, frozen),
        flops=2 * rows * width * (cols * n_f + rank),
    )
    got, input_gradient, base = lax.optimization_barrier((got, input_gradient, base))
    (pay,) = call(add_kernel, [shape((n_far, slab, rank), bf16)], [VMEM], (got,))
    got = swap(pay, FAR)
    (pay,) = call(add_kernel, [shape((n_near, slab, rank), bf16)], [VMEM], (got,))
    got_g = swap(pay, NEAR)
    (pay,) = call(
        project_kernel,
        [shape((n_f, rows + TAIL, rank), bf16)],
        [VMEM] * 2,
        (got_g, prompts),
        flops=2 * rows * width * rank,
    )
    got = swap(pay, FSDP)
    next_down, next_up, keys = call(
        finish_kernel,
        [shape((width, rank), f32), shape((rank, cols), f32), shape((rows, cols), bf16)],
        [VMEM] * 6,
        (got, got_base, base, got_g, down_w, up_w),
        flops=2 * rows * rank * cols,
    )
    return input_gradient, next_down, next_up, keys


def solution(mesh):
    dp, fsdp, section = mesh.devices.shape
    fine = Mesh(mesh.devices.reshape(4, dp // 4, fsdp // 2, 2, section), AXES)
    rows_by_width = P(ROWS, FSDP)
    return jax.shard_map(
        per_device,
        mesh=fine,
        in_specs=(
            rows_by_width,
            rows_by_width,
            P(ROWS),
            P(ROWS),
            P(FSDP, None),
            P(FSDP, None),
            P(None, FSDP),
            rows_by_width,
        ),
        out_specs=(rows_by_width, P(FSDP, None), P(None, FSDP), rows_by_width),
        check_vma=False,
    )
```

```python
import jax
import jax.numpy as jnp
from jax import lax
from jax.experimental import pallas as pl
from jax.experimental.pallas import tpu as pltpu
from jax.sharding import Mesh
from jax.sharding import PartitionSpec as P

adapter_scale = 0.5
step_rate = 16.0
clip_norm = 1.0

AXES = ("zhi", "y", "x", "zlo", "core")
FSDP = ("x", "zlo")
ROWS = ("zhi", "y", "core")
NEAR = ("y", "core")
FAR = "zhi"
TAIL = 16
bf16 = jnp.bfloat16
f32 = jnp.float32

NT = (((1,), (1,)), ((), ()))
TN = (((0,), (0,)), ((), ()))


def dot(a, b, dims=(((1,), (0,)), ((), ()))):
    return lax.dot_general(a, b, dims, preferred_element_type=f32)


def swap(v, axis):
    return lax.all_to_all(v, axis, 0, 0, tiled=True)


VMEM = None
SMEM = pl.BlockSpec(memory_space=pltpu.SMEM)
ANY = pl.BlockSpec(memory_space=pl.ANY)
HBM = pl.BlockSpec(memory_space=pltpu.HBM)


def block(v):
    zeros = (0,) * len(v.shape)
    return pl.BlockSpec(v.shape, lambda i: zeros)


def call(kernel, outs, ins, args, flops=0, out_specs=None, limit=24, **more):
    moved = sum(a.size * a.dtype.itemsize for a in args) + sum(
        o.size * o.dtype.itemsize for o in outs
    )
    return pl.pallas_call(
        kernel,
        grid=(1,),
        in_specs=[spec or block(a) for spec, a in zip(ins, args, strict=True)],
        out_specs=out_specs or tuple(block(o) for o in outs),
        out_shape=tuple(outs),
        compiler_params=pltpu.CompilerParams(vmem_limit_bytes=limit * 1024 * 1024),
        cost_estimate=pl.CostEstimate(flops=flops, bytes_accessed=moved, transcendentals=0),
        **more,
    )(*args)


def shape(dims, kind):
    return jax.ShapeDtypeStruct(dims, kind)


def parts_kernel(
    lens, buckets, acts, og, down_w, up_w, gk_out, pay,
    acts_v, og_v, down_v, up_v, gk, parts, sems,
):
    rows = acts.shape[0]
    seqs = lens.shape[0]
    slot = rows // seqs
    peers = pay.shape[0]
    piece = rows // peers
    pairs = ((og, og_v), (up_w, up_v), (down_w, down_v), (acts, acts_v))
    loads = [pltpu.make_async_copy(a, b, sems.at[i]) for i, (a, b) in enumerate(pairs)]
    for c in loads:
        c.start()
    loads[0].wait()
    place = lax.broadcasted_iota(jnp.int32, (slot, 1), 0)
    for s in range(seqs):
        here = pl.ds(s * slot, slot)
        weight = jnp.where(place < lens[s], buckets[s].astype(f32) - 1.5, f32(0.0))
        gk[here, :] = (weight * og_v[here, :].astype(f32)).astype(bf16)
    first = len(pairs)
    stores = [pltpu.make_async_copy(gk, gk_out, sems.at[first])] + [
        pltpu.make_async_copy(gk, pay.at[j, pl.ds(2 * piece, rows), :], sems.at[first + 1 + j])
        for j in range(peers)
    ]
    for c in stores:
        c.start()

    def put(k, v):
        v = v.astype(bf16)
        for j in range(peers):
            parts[j, k * piece : (k + 1) * piece, :] = v[j * piece : (j + 1) * piece]

    loads[1].wait()
    put(0, dot(gk[...], up_v[...].astype(bf16), NT))
    loads[2].wait()
    a_half = down_v[...].astype(bf16)
    loads[3].wait()
    put(1, dot(acts_v[...], a_half))
    last = pltpu.make_async_copy(
        parts, pay.at[:, pl.ds(0, 2 * piece), :], sems.at[first + 1 + peers]
    )
    last.start()
    for c in stores:
        c.wait()
    last.wait()


def prompts_kernel(prompts, frozen, down_w, pay, base_v, proj_v, sems):
    peers, long, cols = pay.shape
    rows = prompts.shape[0]
    piece = rows // peers
    proj = dot(prompts[...], down_w[...].astype(bf16)).astype(bf16)
    base = dot(prompts[...], frozen[...]).astype(bf16)
    for j in range(peers):
        proj_v[j] = proj[j * piece : (j + 1) * piece]
        base_v[j] = base[:, j * cols : (j + 1) * cols]
    copies = [
        pltpu.make_async_copy(proj_v, pay.at[:, pl.ds(2 * piece, piece), :], sems.at[0]),
        pltpu.make_async_copy(base_v, pay.at[:, pl.ds(3 * piece, rows), :], sems.at[1]),
    ]
    for c in copies:
        c.start()
    for c in copies:
        c.wait()


def sums_kernel(got_ref, pay_in, pay_ref, sums_ref, sems):
    del pay_in
    peers = got_ref.shape[0]
    part = sums_ref.shape[0]
    total = got_ref[0, :part, :].astype(f32)
    for j in range(1, peers):
        total += got_ref[j, :part, :].astype(f32)
    sums_ref[...] = total.astype(bf16)
    copies = [
        pltpu.make_async_copy(sums_ref, pay_ref.at[j, pl.ds(0, part), :], sems.at[j])
        for j in range(peers)
    ]
    for c in copies:
        c.start()
    for c in copies:
        c.wait()


def rejoin(got_ref, first, piece):
    return jnp.concatenate(
        [got_ref[j, first : first + piece, :] for j in range(got_ref.shape[0])], axis=0
    )


def grads_kernel(got_ref, acts, gk, pay, pay_v, sem):
    rows = acts.shape[0]
    piece = rows // got_ref.shape[0]
    lanes = gk.shape[1]
    up = rejoin(got_ref, 0, piece)
    down = rejoin(got_ref, piece, piece)
    g = adapter_scale * jnp.concatenate([dot(up, acts[...], TN), dot(down, gk[...], TN)], axis=1)
    peers = pay.shape[0]
    step = g.shape[0] // peers
    for j in range(peers):
        pay_v[j] = jnp.concatenate(
            [
                g[j * step : (j + 1) * step, c * lanes : (c + 1) * lanes]
                for c in range(g.shape[1] // lanes)
            ],
            axis=0,
        ).astype(pay.dtype)
    copy = pltpu.make_async_copy(pay_v, pay, sem)
    copy.start()
    copy.wait()


def add_kernel(got_ref, pay_ref):
    total = got_ref[0].astype(f32)
    for j in range(1, got_ref.shape[0]):
        total += got_ref[j].astype(f32)
    total = total.astype(pay_ref.dtype)
    for j in range(pay_ref.shape[0]):
        pay_ref[j] = total


def whole_gradient(got_ref, rank):
    peers, long, _ = got_ref.shape
    step = rank // peers
    got = [got_ref[j].astype(f32) for j in range(peers)]
    return [
        jnp.concatenate([v[c * step : (c + 1) * step] for v in got], axis=0)
        for c in range(long // step)
    ]


def project_kernel(got_ref, prompts, pa_rows, pay_ref):
    rank = pay_ref.shape[2]
    rows = prompts.shape[0]
    blocks = whole_gradient(got_ref, rank)
    squares = sum(b * b for b in blocks)
    total = jnp.sum(squares, keepdims=True)
    high = total.astype(bf16)
    rest = total - high.astype(f32)
    middle = rest.astype(bf16)
    low = (rest - middle.astype(f32)).astype(bf16)
    lane = lax.broadcasted_iota(jnp.int32, (TAIL, rank), 1)
    tail = jnp.where(
        lane == 0,
        high.astype(f32),
        jnp.where(lane == 1, middle.astype(f32), jnp.where(lane == 2, low.astype(f32), 0.0)),
    ).astype(bf16)
    g_down = jnp.concatenate(blocks[:-1], axis=1).astype(bf16)
    proj = dot(prompts[...], g_down, NT).astype(bf16)
    for j in range(pay_ref.shape[0]):
        pay_ref[j, :rows, :] = proj
        pay_ref[j, rows : rows + TAIL, :] = tail
        pay_ref[j, rows + TAIL :, :] = pa_rows[...]


def finish_kernel(got, base, got_g, down_w, up_w, next_down, next_up, keys):
    rows = keys.shape[0]
    rank = down_w.shape[1]
    peers = got.shape[0]
    lane = lax.broadcasted_iota(jnp.int32, (TAIL, rank), 1)
    place = lax.broadcasted_iota(jnp.int32, (TAIL, rank), 0)
    p_g = got[0, :rows, :].astype(f32)
    tail = got[0, rows : rows + TAIL, :].astype(f32)
    for j in range(1, peers):
        p_g += got[j, :rows, :].astype(f32)
        tail += got[j, rows : rows + TAIL, :].astype(f32)
    squares = jnp.sum(jnp.where((place == 0) & (lane < 3), tail, 0.0), keepdims=True)
    factor = step_rate * jnp.minimum(1.0, clip_norm / jnp.sqrt(squares + 1e-12))
    blocks = whole_gradient(got_g, rank)
    for c, block in enumerate(blocks[:-1]):
        here = pl.ds(c * rank, rank)
        next_down[here, :] = down_w[here, :] - factor * block.T
    new_up = up_w[...] - factor * blocks[-1]
    next_up[...] = new_up
    proj = rejoin(got, rows + TAIL, rows // peers).astype(f32) - factor * p_g
    keys[...] = (
        base[...] + adapter_scale * dot(proj.astype(bf16), new_up.astype(bf16))
    ).astype(bf16)


def frozen_kernel(got_gk, frozen, acts, out):
    del acts
    rows = out.shape[0]
    peers, long, _ = got_gk.shape
    gk = jnp.concatenate([got_gk[j, long - rows :, :] for j in range(peers)], axis=1)
    out[...] = dot(gk, frozen[...], NT)


def beside_kernel(got, down_w, part, out, base_out, pa_out):
    rows = out.shape[0]
    peers, long, _ = got.shape
    piece = rows // peers
    first = long - rows
    a_half = down_w[...].astype(bf16)
    up = rejoin(got, 0, piece)
    out[...] = (part[...] + adapter_scale * dot(up, a_half, NT)).astype(bf16)
    total = got[0, first - piece :, :].astype(f32)
    for j in range(1, peers):
        total += got[j, first - piece :, :].astype(f32)
    pa_out[...] = total[:piece].astype(bf16)
    base_out[...] = total[piece:]


def per_device(acts, output_gradient, lengths, buckets, frozen, down_w, up_w, prompts):
    rows = acts.shape[0]
    width, rank = down_w.shape
    cols = up_w.shape[1]
    n_f = lax.axis_size(FSDP)
    n_near = lax.axis_size(NEAR)
    n_far = lax.axis_size(FAR)
    piece = rows // n_f
    slab = (width + cols) // n_near
    long = 3 * piece + rows

    gk, pay = call(
        parts_kernel,
        [shape((rows, cols), bf16), shape((n_f, 2 * piece + rows, rank), bf16)],
        [SMEM, SMEM] + [ANY] * 4,
        (lengths, buckets, acts, output_gradient, down_w, up_w),
        flops=2 * rows * rank * (width + cols),
        out_specs=(HBM, HBM),
        limit=60,
        scratch_shapes=[
            pltpu.VMEM((rows, width), bf16),
            pltpu.VMEM((rows, cols), bf16),
            pltpu.VMEM((width, rank), f32),
            pltpu.VMEM((rank, cols), f32),
            pltpu.VMEM((rows, cols), bf16),
            pltpu.VMEM((n_f, 2 * piece, rank), bf16),
            pltpu.SemaphoreType.DMA((6 + n_f,)),
        ],
    )
    got_gk = swap(pay, FSDP)
    (pay,) = call(
        prompts_kernel,
        [shape((n_f, long, cols), bf16)],
        [VMEM] * 3,
        (prompts, frozen, down_w),
        flops=2 * rows * width * (cols * n_f + rank),
        out_specs=(HBM,),
        scratch_shapes=[
            pltpu.VMEM((n_f, rows, cols), bf16),
            pltpu.VMEM((n_f, piece, rank), bf16),
            pltpu.SemaphoreType.DMA((2,)),
        ],
    )
    (pay,) = call(
        sums_kernel,
        [shape((n_f, long, cols), bf16)],
        [VMEM, HBM],
        (got_gk, pay),
        input_output_aliases={1: 0},
        out_specs=(HBM,),
        scratch_shapes=[pltpu.VMEM((2 * piece, rank), bf16), pltpu.SemaphoreType.DMA((n_f,))],
    )
    got = swap(pay, FSDP)
    (input_part,) = call(
        frozen_kernel,
        [shape((rows, width), f32)],
        [VMEM] * 3,
        (got_gk, frozen, acts),
        flops=2 * rows * width * cols * n_f,
    )
    got, input_part = lax.optimization_barrier((got, input_part))

    (pay,) = call(
        grads_kernel,
        [shape((n_near, slab, rank), bf16)],
        [VMEM] * 3,
        (got, acts, gk),
        flops=2 * rows * rank * (width + cols),
        out_specs=(HBM,),
        scratch_shapes=[pltpu.VMEM((n_near, slab, rank), bf16), pltpu.SemaphoreType.DMA],
    )
    got_g = swap(pay, NEAR)
    input_gradient, base, pa_rows = call(
        beside_kernel,
        [shape((rows, width), bf16), shape((rows, cols), f32), shape((piece, rank), bf16)],
        [VMEM] * 3,
        (got, down_w, input_part),
        flops=2 * rows * width * rank,
    )
    got_g, input_gradient, base, pa_rows = lax.optimization_barrier(
        (got_g, input_gradient, base, pa_rows)
    )
    (pay,) = call(add_kernel, [shape((n_far, slab, rank), bf16)], [VMEM], (got_g,))
    got = swap(pay, FAR)
    (pay,) = call(add_kernel, [shape((n_near, slab, rank), bf16)], [VMEM], (got,))
    got_g = swap(pay, NEAR)
    (pay,) = call(
        project_kernel,
        [shape((n_f, rows + TAIL + piece, rank), bf16)],
        [VMEM] * 3,
        (got_g, prompts, pa_rows),
        flops=2 * rows * width * rank,
    )
    got = swap(pay, FSDP)
    next_down, next_up, keys = call(
        finish_kernel,
        [shape((width, rank), f32), shape((rank, cols), f32), shape((rows, cols), bf16)],
        [VMEM] * 5,
        (got, base, got_g, down_w, up_w),
        flops=2 * rows * rank * cols,
    )
    return input_gradient, next_down, next_up, keys


def solution(mesh):
    dp, fsdp, section = mesh.devices.shape
    fine = Mesh(mesh.devices.reshape(4, dp // 4, fsdp // 2, 2, section), AXES)
    rows_by_width = P(ROWS, FSDP)
    return jax.shard_map(
        per_device,
        mesh=fine,
        in_specs=(
            rows_by_width,
            rows_by_width,
            P(ROWS),
            P(ROWS),
            P(FSDP, None),
            P(FSDP, None),
            P(None, FSDP),
            rows_by_width,
        ),
        out_specs=(rows_by_width, P(FSDP, None), P(None, FSDP), rows_by_width),
        check_vma=False,
    )
```

```python
import jax
import jax.numpy as jnp
from jax import lax
from jax.experimental import pallas as pl
from jax.experimental.pallas import tpu as pltpu
from jax.sharding import Mesh
from jax.sharding import PartitionSpec as P

adapter_scale = 0.5
step_rate = 16.0
clip_norm = 1.0

AXES = ("zhi", "y", "x", "zlo", "core")
FSDP = ("x", "zlo")
ROWS = ("zhi", "y", "core")
NEAR = ("y", "core")
FAR = "zhi"
TAIL = 16
bf16 = jnp.bfloat16
f32 = jnp.float32

NT = (((1,), (1,)), ((), ()))
TN = (((0,), (0,)), ((), ()))


def dot(a, b, dims=(((1,), (0,)), ((), ()))):
    return lax.dot_general(a, b, dims, preferred_element_type=f32)


Z_PAIRS = ((0, 1), (1, 0))
X_NEAR = ((0, 1), (1, 0), (2, 3), (3, 2))
X_FAR = ((0, 3), (3, 0), (1, 2), (2, 1))


def owner_mask(i):
    return (i & 1) ^ (2 if i & 2 else 0) ^ (6 if i & 4 else 0)


def swap(v, axis):
    return lax.all_to_all(v, axis, 0, 0, tiled=True)


VMEM = None
SMEM = pl.BlockSpec(memory_space=pltpu.SMEM)
ANY = pl.BlockSpec(memory_space=pl.ANY)
HBM = pl.BlockSpec(memory_space=pltpu.HBM)


def block(v):
    zeros = (0,) * len(v.shape)
    return pl.BlockSpec(v.shape, lambda i: zeros)


def call(kernel, outs, ins, args, flops=0, out_specs=None, limit=24, **more):
    moved = sum(a.size * a.dtype.itemsize for a in args) + sum(
        o.size * o.dtype.itemsize for o in outs
    )
    return pl.pallas_call(
        kernel,
        grid=(1,),
        in_specs=[spec or block(a) for spec, a in zip(ins, args, strict=True)],
        out_specs=out_specs or tuple(block(o) for o in outs),
        out_shape=tuple(outs),
        compiler_params=pltpu.CompilerParams(vmem_limit_bytes=limit * 1024 * 1024),
        cost_estimate=pl.CostEstimate(flops=flops, bytes_accessed=moved, transcendentals=0),
        **more,
    )(*args)


def shape(dims, kind):
    return jax.ShapeDtypeStruct(dims, kind)


def parts_kernel(
    lens, buckets, acts, og, down_w, up_w, gk_out, pay,
    acts_v, og_v, down_v, up_v, gk, parts, sems,
):
    rows = acts.shape[0]
    seqs = lens.shape[0]
    slot = rows // seqs
    peers = pay.shape[0]
    piece = rows // peers
    pairs = ((og, og_v), (up_w, up_v), (down_w, down_v), (acts, acts_v))
    loads = [pltpu.make_async_copy(a, b, sems.at[i]) for i, (a, b) in enumerate(pairs)]
    for c in loads:
        c.start()
    loads[0].wait()
    place = lax.broadcasted_iota(jnp.int32, (slot, 1), 0)
    for s in range(seqs):
        here = pl.ds(s * slot, slot)
        weight = jnp.where(place < lens[s], buckets[s].astype(f32) - 1.5, f32(0.0))
        gk[here, :] = (weight * og_v[here, :].astype(f32)).astype(bf16)
    first = len(pairs)
    store = pltpu.make_async_copy(gk, gk_out, sems.at[first])
    store.start()

    def put(k, v):
        v = v.astype(bf16)
        for j in range(peers):
            parts[j, k * piece : (k + 1) * piece, :] = v[j * piece : (j + 1) * piece]

    loads[1].wait()
    put(0, dot(gk[...], up_v[...].astype(bf16), NT))
    loads[2].wait()
    a_half = down_v[...].astype(bf16)
    loads[3].wait()
    put(1, dot(acts_v[...], a_half))
    last = pltpu.make_async_copy(parts, pay, sems.at[first + 1])
    last.start()
    store.wait()
    last.wait()


def prompts_kernel(prompts, frozen, down_w, acts, pay, base_v, proj_v, sems):
    del acts
    peers, long, cols = pay.shape
    rows = prompts.shape[0]
    piece = rows // peers
    proj = dot(prompts[...], down_w[...].astype(bf16)).astype(bf16)
    base = dot(prompts[...], frozen[...]).astype(bf16)
    for j in range(peers):
        proj_v[j] = proj[j * piece : (j + 1) * piece]
        base_v[j] = base[:, j * cols : (j + 1) * cols]
    copies = [
        pltpu.make_async_copy(proj_v, pay.at[:, pl.ds(2 * piece, piece), :], sems.at[0]),
        pltpu.make_async_copy(base_v, pay.at[:, pl.ds(3 * piece, rows), :], sems.at[1]),
    ]
    for c in copies:
        c.start()
    for c in copies:
        c.wait()


def sums_kernel(got_ref, pay_in, pay_ref, sums_ref, sems):
    del pay_in
    peers = got_ref.shape[0]
    part = sums_ref.shape[0]
    total = got_ref[0, :part, :].astype(f32)
    for j in range(1, peers):
        total += got_ref[j, :part, :].astype(f32)
    sums_ref[...] = total.astype(bf16)
    copies = [
        pltpu.make_async_copy(sums_ref, pay_ref.at[j, pl.ds(0, part), :], sems.at[j])
        for j in range(peers)
    ]
    for c in copies:
        c.start()
    for c in copies:
        c.wait()


def rejoin(got_ref, first, piece):
    return jnp.concatenate(
        [got_ref[j, first : first + piece, :] for j in range(got_ref.shape[0])], axis=0
    )


def grads_kernel(got_ref, acts, gk, pay, pay_v, sem):
    rows = acts.shape[0]
    piece = rows // got_ref.shape[0]
    lanes = gk.shape[1]
    up = rejoin(got_ref, 0, piece)
    down = rejoin(got_ref, piece, piece)
    g = adapter_scale * jnp.concatenate([dot(up, acts[...], TN), dot(down, gk[...], TN)], axis=1)
    peers = pay.shape[0]
    step = g.shape[0] // peers
    for j in range(peers):
        pay_v[j] = jnp.concatenate(
            [
                g[j * step : (j + 1) * step, c * lanes : (c + 1) * lanes]
                for c in range(g.shape[1] // lanes)
            ],
            axis=0,
        ).astype(pay.dtype)
    copy = pltpu.make_async_copy(pay_v, pay, sem)
    copy.start()
    copy.wait()


def add_kernel(got_ref, pay, total_v, sems):
    total = got_ref[0].astype(f32)
    for j in range(1, got_ref.shape[0]):
        total += got_ref[j].astype(f32)
    total_v[...] = total.astype(pay.dtype)
    copies = [
        pltpu.make_async_copy(total_v, pay.at[j], sems.at[j]) for j in range(pay.shape[0])
    ]
    for c in copies:
        c.start()
    for c in copies:
        c.wait()


def add(got, peers):
    dims = got.shape[1:]
    (pay,) = call(
        add_kernel,
        [shape((peers,) + dims, bf16)],
        [VMEM],
        (got,),
        out_specs=(HBM,),
        scratch_shapes=[pltpu.VMEM(dims, bf16), pltpu.SemaphoreType.DMA((peers,))],
    )
    return pay


def whole_gradient(got_ref, rank):
    peers, long, _ = got_ref.shape
    step = rank // peers
    got = [got_ref[j].astype(f32) for j in range(peers)]
    return [
        jnp.concatenate([v[c * step : (c + 1) * step] for v in got], axis=0)
        for c in range(long // step)
    ]


def project_kernel(got_ref, prompts, pa_rows, pay_ref):
    rank = pay_ref.shape[2]
    rows = prompts.shape[0]
    blocks = whole_gradient(got_ref, rank)
    squares = sum(b * b for b in blocks)
    total = jnp.sum(squares, keepdims=True)
    high = total.astype(bf16)
    rest = total - high.astype(f32)
    middle = rest.astype(bf16)
    low = (rest - middle.astype(f32)).astype(bf16)
    lane = lax.broadcasted_iota(jnp.int32, (TAIL, rank), 1)
    tail = jnp.where(
        lane == 0,
        high.astype(f32),
        jnp.where(lane == 1, middle.astype(f32), jnp.where(lane == 2, low.astype(f32), 0.0)),
    ).astype(bf16)
    g_down = jnp.concatenate(blocks[:-1], axis=1).astype(bf16)
    proj = dot(prompts[...], g_down, NT).astype(bf16)
    for j in range(pay_ref.shape[0]):
        pay_ref[j, :rows, :] = proj
        pay_ref[j, rows : rows + TAIL, :] = tail
        pay_ref[j, rows + TAIL :, :] = pa_rows[...]


def finish_kernel(got, base, got_g, down_w, up_w, next_down, next_up, keys):
    rows = keys.shape[0]
    rank = down_w.shape[1]
    peers = got.shape[0]
    lane = lax.broadcasted_iota(jnp.int32, (TAIL, rank), 1)
    place = lax.broadcasted_iota(jnp.int32, (TAIL, rank), 0)
    p_g = got[0, :rows, :].astype(f32)
    tail = got[0, rows : rows + TAIL, :].astype(f32)
    for j in range(1, peers):
        p_g += got[j, :rows, :].astype(f32)
        tail += got[j, rows : rows + TAIL, :].astype(f32)
    squares = jnp.sum(jnp.where((place == 0) & (lane < 3), tail, 0.0), keepdims=True)
    factor = step_rate * jnp.minimum(1.0, clip_norm / jnp.sqrt(squares + 1e-12))
    blocks = whole_gradient(got_g, rank)
    for c, block in enumerate(blocks[:-1]):
        here = pl.ds(c * rank, rank)
        next_down[here, :] = down_w[here, :] - factor * block.T
    new_up = up_w[...] - factor * blocks[-1]
    next_up[...] = new_up
    proj = rejoin(got, rows + TAIL, rows // peers).astype(f32) - factor * p_g
    keys[...] = (
        base[...] + adapter_scale * dot(proj.astype(bf16), new_up.astype(bf16))
    ).astype(bf16)


def input_kernel(place, near, far, up, down_w, frozen, out, gk):
    rows = out.shape[0]
    lanes = near.shape[1]
    count = near.shape[0] // rows
    for i in range(2 * count):
        ref = near if i < count else far
        block = ref[(i % count) * rows : (i % count + 1) * rows, :]
        owner = place[0] ^ owner_mask(i)
        gk[:, pl.ds(pl.multiple_of(owner * lanes, lanes), lanes)] = block
    a_half = down_w[...].astype(bf16)
    out[...] = (
        dot(gk[...], frozen[...], NT) + adapter_scale * dot(up[...], a_half, NT)
    ).astype(bf16)


def beside_kernel(got, two, other, base_out, pa_out, up_out, four):
    count = two.shape[0]
    four[:count, :] = two[...]
    four[count:, :] = other[...]
    rows = base_out.shape[0]
    peers, long, _ = got.shape
    piece = rows // peers
    first = long - rows
    up_out[...] = rejoin(got, 0, piece)
    total = got[0, first - piece :, :].astype(f32)
    for j in range(1, peers):
        total += got[j, first - piece :, :].astype(f32)
    pa_out[...] = total[:piece].astype(bf16)
    base_out[...] = total[piece:]


def per_device(acts, output_gradient, lengths, buckets, frozen, down_w, up_w, prompts):
    rows = acts.shape[0]
    width, rank = down_w.shape
    cols = up_w.shape[1]
    n_f = lax.axis_size(FSDP)
    n_near = lax.axis_size(NEAR)
    n_far = lax.axis_size(FAR)
    piece = rows // n_f
    slab = (width + cols) // n_near
    long = 3 * piece + rows

    gk, pay = call(
        parts_kernel,
        [shape((rows, cols), bf16), shape((n_f, 2 * piece, rank), bf16)],
        [SMEM, SMEM] + [ANY] * 4,
        (lengths, buckets, acts, output_gradient, down_w, up_w),
        flops=2 * rows * rank * (width + cols),
        out_specs=(HBM, HBM),
        limit=60,
        scratch_shapes=[
            pltpu.VMEM((rows, width), bf16),
            pltpu.VMEM((rows, cols), bf16),
            pltpu.VMEM((width, rank), f32),
            pltpu.VMEM((rank, cols), f32),
            pltpu.VMEM((rows, cols), bf16),
            pltpu.VMEM((n_f, 2 * piece, rank), bf16),
            pltpu.SemaphoreType.DMA((6,)),
        ],
    )
    got = swap(pay, FSDP)
    other = lax.ppermute(gk, "zlo", Z_PAIRS)
    (pay,) = call(
        prompts_kernel,
        [shape((n_f, long, cols), bf16)],
        [VMEM] * 4,
        (prompts, frozen, down_w, acts),
        flops=2 * rows * width * (cols * n_f + rank),
        out_specs=(HBM,),
        scratch_shapes=[
            pltpu.VMEM((n_f, rows, cols), bf16),
            pltpu.VMEM((n_f, piece, rank), bf16),
            pltpu.SemaphoreType.DMA((2,)),
        ],
    )
    got, pay, other = lax.optimization_barrier((got, pay, other))
    (pay,) = call(
        sums_kernel,
        [shape((n_f, long, cols), bf16)],
        [VMEM, HBM],
        (got, pay),
        input_output_aliases={1: 0},
        out_specs=(HBM,),
        scratch_shapes=[pltpu.VMEM((2 * piece, rank), bf16), pltpu.SemaphoreType.DMA((n_f,))],
    )
    got = swap(pay, FSDP)
    two = jnp.concatenate([gk, other], axis=0)
    other = lax.ppermute(two, "x", X_NEAR)
    got, two, other = lax.optimization_barrier((got, two, other))

    (pay,) = call(
        grads_kernel,
        [shape((n_near, slab, rank), bf16)],
        [VMEM] * 3,
        (got, acts, gk),
        flops=2 * rows * rank * (width + cols),
        out_specs=(HBM,),
        scratch_shapes=[pltpu.VMEM((n_near, slab, rank), bf16), pltpu.SemaphoreType.DMA],
    )
    got_g = swap(pay, NEAR)
    base, pa_rows, up, four = call(
        beside_kernel,
        [
            shape((rows, cols), f32),
            shape((piece, rank), bf16),
            shape((rows, rank), bf16),
            shape((4 * rows, cols), bf16),
        ],
        [VMEM] * 3,
        (got, two, other),
    )
    other = lax.ppermute(four, "x", X_FAR)
    got_g, base, pa_rows, up = lax.optimization_barrier((got_g, base, pa_rows, up))
    got = swap(add(got_g, n_far), FAR)
    got_g = swap(add(got, n_near), NEAR)
    (input_gradient,) = call(
        input_kernel,
        [shape((rows, width), bf16)],
        [SMEM] + [VMEM] * 5,
        (lax.axis_index(FSDP).reshape(1), four, other, up, down_w, frozen),
        flops=2 * rows * width * (cols * n_f + rank),
        scratch_shapes=[pltpu.VMEM((rows, cols * n_f), bf16)],
    )
    got_g, input_gradient = lax.optimization_barrier((got_g, input_gradient))
    (pay,) = call(
        project_kernel,
        [shape((n_f, rows + TAIL + piece, rank), bf16)],
        [VMEM] * 3,
        (got_g, prompts, pa_rows),
        flops=2 * rows * width * rank,
    )
    got = swap(pay, FSDP)
    next_down, next_up, keys = call(
        finish_kernel,
        [shape((width, rank), f32), shape((rank, cols), f32), shape((rows, cols), bf16)],
        [VMEM] * 5,
        (got, base, got_g, down_w, up_w),
        flops=2 * rows * rank * cols,
    )
    return input_gradient, next_down, next_up, keys


def solution(mesh):
    dp, fsdp, section = mesh.devices.shape
    fine = Mesh(mesh.devices.reshape(4, dp // 4, fsdp // 2, 2, section), AXES)
    rows_by_width = P(ROWS, FSDP)
    return jax.shard_map(
        per_device,
        mesh=fine,
        in_specs=(
            rows_by_width,
            rows_by_width,
            P(ROWS),
            P(ROWS),
            P(FSDP, None),
            P(FSDP, None),
            P(None, FSDP),
            rows_by_width,
        ),
        out_specs=(rows_by_width, P(FSDP, None), P(None, FSDP), rows_by_width),
        check_vma=False,
    )
```

```python
import jax
import jax.numpy as jnp
from jax import lax
from jax.experimental import pallas as pl
from jax.experimental.pallas import tpu as pltpu
from jax.sharding import Mesh
from jax.sharding import PartitionSpec as P

adapter_scale = 0.5
step_rate = 16.0
clip_norm = 1.0

AXES = ("zhi", "y", "x", "zlo", "core")
FSDP = ("x", "zlo")
ROWS = ("zhi", "y", "core")
NEAR = ("y", "core")
FAR = "zhi"
TAIL = 16
bf16 = jnp.bfloat16
f32 = jnp.float32

NT = (((1,), (1,)), ((), ()))
TN = (((0,), (0,)), ((), ()))


def dot(a, b, dims=(((1,), (0,)), ((), ()))):
    return lax.dot_general(a, b, dims, preferred_element_type=f32)


Z_PAIRS = ((0, 1), (1, 0))
X_NEAR = ((0, 1), (1, 0), (2, 3), (3, 2))
X_FAR = ((0, 3), (3, 0), (1, 2), (2, 1))


def owner_mask(i):
    return (i & 1) ^ (2 if i & 2 else 0) ^ (6 if i & 4 else 0)


def swap(v, axis):
    return lax.all_to_all(v, axis, 0, 0, tiled=True)


VMEM = None
SMEM = pl.BlockSpec(memory_space=pltpu.SMEM)
ANY = pl.BlockSpec(memory_space=pl.ANY)
HBM = pl.BlockSpec(memory_space=pltpu.HBM)


def block(v):
    zeros = (0,) * len(v.shape)
    return pl.BlockSpec(v.shape, lambda i: zeros)


def call(kernel, outs, ins, args, flops=0, out_specs=None, limit=24, **more):
    moved = sum(a.size * a.dtype.itemsize for a in args) + sum(
        o.size * o.dtype.itemsize for o in outs
    )
    return pl.pallas_call(
        kernel,
        grid=(1,),
        in_specs=[spec or block(a) for spec, a in zip(ins, args, strict=True)],
        out_specs=out_specs or tuple(block(o) for o in outs),
        out_shape=tuple(outs),
        compiler_params=pltpu.CompilerParams(vmem_limit_bytes=limit * 1024 * 1024),
        cost_estimate=pl.CostEstimate(flops=flops, bytes_accessed=moved, transcendentals=0),
        **more,
    )(*args)


def shape(dims, kind):
    return jax.ShapeDtypeStruct(dims, kind)


def parts_kernel(
    lens, buckets, acts, og, down_w, up_w, gk_out, pay,
    acts_v, og_v, down_v, up_v, gk, parts, sems,
):
    rows = acts.shape[0]
    seqs = lens.shape[0]
    slot = rows // seqs
    peers = pay.shape[0]
    piece = rows // peers
    pairs = ((og, og_v), (up_w, up_v), (down_w, down_v), (acts, acts_v))
    loads = [pltpu.make_async_copy(a, b, sems.at[i]) for i, (a, b) in enumerate(pairs)]
    for c in loads:
        c.start()
    loads[0].wait()
    place = lax.broadcasted_iota(jnp.int32, (slot, 1), 0)
    for s in range(seqs):
        here = pl.ds(s * slot, slot)
        weight = jnp.where(place < lens[s], buckets[s].astype(f32) - 1.5, f32(0.0))
        gk[here, :] = (weight * og_v[here, :].astype(f32)).astype(bf16)
    first = len(pairs)
    store = pltpu.make_async_copy(gk, gk_out, sems.at[first])
    store.start()

    def put(k, v):
        v = v.astype(bf16)
        for j in range(peers):
            parts[j, k * piece : (k + 1) * piece, :] = v[j * piece : (j + 1) * piece]

    loads[1].wait()
    put(0, dot(gk[...], up_v[...].astype(bf16), NT))
    loads[2].wait()
    a_half = down_v[...].astype(bf16)
    loads[3].wait()
    put(1, dot(acts_v[...], a_half))
    last = pltpu.make_async_copy(parts, pay, sems.at[first + 1])
    last.start()
    store.wait()
    last.wait()


def prompts_kernel(place, prompts, frozen, down_w, acts, proj_out, keep, send, base):
    del acts
    rows = prompts.shape[0]
    cols = keep.shape[1]
    count = keep.shape[0] // rows
    proj_out[...] = dot(prompts[...], down_w[...].astype(bf16)).astype(bf16)
    base[...] = dot(prompts[...], frozen[...])
    for i in range(2 * count):
        owner = place[0] ^ owner_mask(i)
        part = base[:, pl.ds(pl.multiple_of(owner * cols, cols), cols)]
        here = pl.ds((i % count) * rows, rows)
        if i < count:
            keep[here, :] = part
        else:
            send[here, :] = part.astype(bf16)


def halve_kernel(held, got, keep, send):
    half = keep.shape[0]
    keep[...] = held[:half, :] + got[:half, :].astype(f32)
    send[...] = (held[half:, :] + got[half:, :].astype(f32)).astype(bf16)


def halve(held, got):
    half = held.shape[0] // 2
    dims = (half, held.shape[1])
    return call(halve_kernel, [shape(dims, f32), shape(dims, bf16)], [VMEM] * 2, (held, got))


def sums_kernel(got_ref, proj, pay, pay_v, sem):
    peers, long, _ = pay.shape
    part = got_ref.shape[1]
    piece = long - part
    total = got_ref[0].astype(f32)
    for j in range(1, peers):
        total += got_ref[j].astype(f32)
    total = total.astype(bf16)
    for j in range(peers):
        pay_v[j, :part, :] = total
        pay_v[j, part:, :] = proj[j * piece : (j + 1) * piece, :]
    copy = pltpu.make_async_copy(pay_v, pay, sem)
    copy.start()
    copy.wait()


def rejoin(got_ref, first, piece):
    return jnp.concatenate(
        [got_ref[j, first : first + piece, :] for j in range(got_ref.shape[0])], axis=0
    )


def grads_kernel(got_ref, acts, gk, pay, pay_v, sem):
    rows = acts.shape[0]
    piece = rows // got_ref.shape[0]
    lanes = gk.shape[1]
    up = rejoin(got_ref, 0, piece)
    down = rejoin(got_ref, piece, piece)
    g = adapter_scale * jnp.concatenate([dot(up, acts[...], TN), dot(down, gk[...], TN)], axis=1)
    peers = pay.shape[0]
    step = g.shape[0] // peers
    for j in range(peers):
        pay_v[j] = jnp.concatenate(
            [
                g[j * step : (j + 1) * step, c * lanes : (c + 1) * lanes]
                for c in range(g.shape[1] // lanes)
            ],
            axis=0,
        ).astype(pay.dtype)
    copy = pltpu.make_async_copy(pay_v, pay, sem)
    copy.start()
    copy.wait()


def add_kernel(got_ref, pay, total_v, sems):
    total = got_ref[0].astype(f32)
    for j in range(1, got_ref.shape[0]):
        total += got_ref[j].astype(f32)
    total_v[...] = total.astype(pay.dtype)
    copies = [
        pltpu.make_async_copy(total_v, pay.at[j], sems.at[j]) for j in range(pay.shape[0])
    ]
    for c in copies:
        c.start()
    for c in copies:
        c.wait()


def add(got, peers):
    dims = got.shape[1:]
    (pay,) = call(
        add_kernel,
        [shape((peers,) + dims, bf16)],
        [VMEM],
        (got,),
        out_specs=(HBM,),
        scratch_shapes=[pltpu.VMEM(dims, bf16), pltpu.SemaphoreType.DMA((peers,))],
    )
    return pay


def whole_gradient(got_ref, rank):
    peers, long, _ = got_ref.shape
    step = rank // peers
    got = [got_ref[j].astype(f32) for j in range(peers)]
    return [
        jnp.concatenate([v[c * step : (c + 1) * step] for v in got], axis=0)
        for c in range(long // step)
    ]


def project_kernel(got_ref, prompts, pa_rows, pay_ref):
    rank = pay_ref.shape[2]
    rows = prompts.shape[0]
    blocks = whole_gradient(got_ref, rank)
    squares = sum(b * b for b in blocks)
    total = jnp.sum(squares, keepdims=True)
    high = total.astype(bf16)
    rest = total - high.astype(f32)
    middle = rest.astype(bf16)
    low = (rest - middle.astype(f32)).astype(bf16)
    lane = lax.broadcasted_iota(jnp.int32, (TAIL, rank), 1)
    tail = jnp.where(
        lane == 0,
        high.astype(f32),
        jnp.where(lane == 1, middle.astype(f32), jnp.where(lane == 2, low.astype(f32), 0.0)),
    ).astype(bf16)
    g_down = jnp.concatenate(blocks[:-1], axis=1).astype(bf16)
    proj = dot(prompts[...], g_down, NT).astype(bf16)
    for j in range(pay_ref.shape[0]):
        pay_ref[j, :rows, :] = proj
        pay_ref[j, rows : rows + TAIL, :] = tail
        pay_ref[j, rows + TAIL :, :] = pa_rows[...]


def finish_kernel(got, base, base_got, got_g, down_w, up_w, next_down, next_up, keys):
    rows = keys.shape[0]
    rank = down_w.shape[1]
    peers = got.shape[0]
    lane = lax.broadcasted_iota(jnp.int32, (TAIL, rank), 1)
    place = lax.broadcasted_iota(jnp.int32, (TAIL, rank), 0)
    p_g = got[0, :rows, :].astype(f32)
    tail = got[0, rows : rows + TAIL, :].astype(f32)
    for j in range(1, peers):
        p_g += got[j, :rows, :].astype(f32)
        tail += got[j, rows : rows + TAIL, :].astype(f32)
    squares = jnp.sum(jnp.where((place == 0) & (lane < 3), tail, 0.0), keepdims=True)
    factor = step_rate * jnp.minimum(1.0, clip_norm / jnp.sqrt(squares + 1e-12))
    blocks = whole_gradient(got_g, rank)
    for c, block in enumerate(blocks[:-1]):
        here = pl.ds(c * rank, rank)
        next_down[here, :] = down_w[here, :] - factor * block.T
    new_up = up_w[...] - factor * blocks[-1]
    next_up[...] = new_up
    proj = rejoin(got, rows + TAIL, rows // peers).astype(f32) - factor * p_g
    keys[...] = (
        base[...] + base_got[...].astype(f32) + adapter_scale * dot(proj.astype(bf16), new_up.astype(bf16))
    ).astype(bf16)


def input_kernel(place, near, far, up, down_w, frozen, out, gk):
    rows = out.shape[0]
    lanes = near.shape[1]
    count = near.shape[0] // rows
    for i in range(2 * count):
        ref = near if i < count else far
        block = ref[(i % count) * rows : (i % count + 1) * rows, :]
        owner = place[0] ^ owner_mask(i)
        gk[:, pl.ds(pl.multiple_of(owner * lanes, lanes), lanes)] = block
    a_half = down_w[...].astype(bf16)
    out[...] = (
        dot(gk[...], frozen[...], NT) + adapter_scale * dot(up[...], a_half, NT)
    ).astype(bf16)


def beside_kernel(got, two, other, pa_out, up_out, four):
    count = two.shape[0]
    four[:count, :] = two[...]
    four[count:, :] = other[...]
    peers = got.shape[0]
    piece = pa_out.shape[0]
    up_out[...] = rejoin(got, 0, piece)
    total = got[0, 2 * piece :, :].astype(f32)
    for j in range(1, peers):
        total += got[j, 2 * piece :, :].astype(f32)
    pa_out[...] = total.astype(bf16)


def per_device(acts, output_gradient, lengths, buckets, frozen, down_w, up_w, prompts):
    rows = acts.shape[0]
    width, rank = down_w.shape
    cols = up_w.shape[1]
    n_f = lax.axis_size(FSDP)
    n_near = lax.axis_size(NEAR)
    n_far = lax.axis_size(FAR)
    piece = rows // n_f
    slab = (width + cols) // n_near

    gk, pay = call(
        parts_kernel,
        [shape((rows, cols), bf16), shape((n_f, 2 * piece, rank), bf16)],
        [SMEM, SMEM] + [ANY] * 4,
        (lengths, buckets, acts, output_gradient, down_w, up_w),
        flops=2 * rows * rank * (width + cols),
        out_specs=(HBM, HBM),
        limit=60,
        scratch_shapes=[
            pltpu.VMEM((rows, width), bf16),
            pltpu.VMEM((rows, cols), bf16),
            pltpu.VMEM((width, rank), f32),
            pltpu.VMEM((rank, cols), f32),
            pltpu.VMEM((rows, cols), bf16),
            pltpu.VMEM((n_f, 2 * piece, rank), bf16),
            pltpu.SemaphoreType.DMA((6,)),
        ],
    )
    got = swap(pay, FSDP)
    other = lax.ppermute(gk, "zlo", Z_PAIRS)
    place = lax.axis_index(FSDP).reshape(1)
    proj, held, send = call(
        prompts_kernel,
        [
            shape((rows, rank), bf16),
            shape((n_f // 2 * rows, cols), f32),
            shape((n_f // 2 * rows, cols), bf16),
        ],
        [SMEM] + [VMEM] * 4,
        (place, prompts, frozen, down_w, acts),
        flops=2 * rows * width * (cols * n_f + rank),
        scratch_shapes=[pltpu.VMEM((rows, cols * n_f), f32)],
    )
    got, proj, held, send, other = lax.optimization_barrier((got, proj, held, send, other))
    (pay,) = call(
        sums_kernel,
        [shape((n_f, 3 * piece, rank), bf16)],
        [VMEM] * 2,
        (got, proj),
        out_specs=(HBM,),
        scratch_shapes=[pltpu.VMEM((n_f, 3 * piece, rank), bf16), pltpu.SemaphoreType.DMA],
    )
    got = swap(pay, FSDP)
    two = jnp.concatenate([gk, other], axis=0)
    other = lax.ppermute(two, "x", X_NEAR)
    base_got = lax.ppermute(send, "x", X_FAR)
    got, two = lax.optimization_barrier((got, two))

    (pay,) = call(
        grads_kernel,
        [shape((n_near, slab, rank), bf16)],
        [VMEM] * 3,
        (got, acts, gk),
        flops=2 * rows * rank * (width + cols),
        out_specs=(HBM,),
        scratch_shapes=[pltpu.VMEM((n_near, slab, rank), bf16), pltpu.SemaphoreType.DMA],
    )
    got_g = swap(pay, NEAR)
    pa_rows, up, four = call(
        beside_kernel,
        [
            shape((piece, rank), bf16),
            shape((rows, rank), bf16),
            shape((n_f // 2 * rows, cols), bf16),
        ],
        [VMEM] * 3,
        (got, two, other),
    )
    other = lax.ppermute(four, "x", X_FAR)
    held, send = halve(held, base_got)
    got_g, pa_rows, up, held, send = lax.optimization_barrier((got_g, pa_rows, up, held, send))
    base_got = lax.ppermute(send, "x", X_NEAR)
    got = swap(add(got_g, n_far), FAR)
    got_g = swap(add(got, n_near), NEAR)
    (input_gradient,) = call(
        input_kernel,
        [shape((rows, width), bf16)],
        [SMEM] + [VMEM] * 5,
        (place, four, other, up, down_w, frozen),
        flops=2 * rows * width * (cols * n_f + rank),
        scratch_shapes=[pltpu.VMEM((rows, cols * n_f), bf16)],
    )
    base, send = halve(held, base_got)
    base_got = lax.ppermute(send, "zlo", Z_PAIRS)
    got_g, input_gradient, base, base_got = lax.optimization_barrier(
        (got_g, input_gradient, base, base_got)
    )
    (pay,) = call(
        project_kernel,
        [shape((n_f, rows + TAIL + piece, rank), bf16)],
        [VMEM] * 3,
        (got_g, prompts, pa_rows),
        flops=2 * rows * width * rank,
    )
    got = swap(pay, FSDP)
    next_down, next_up, keys = call(
        finish_kernel,
        [shape((width, rank), f32), shape((rank, cols), f32), shape((rows, cols), bf16)],
        [VMEM] * 6,
        (got, base, base_got, got_g, down_w, up_w),
        flops=2 * rows * rank * cols,
    )
    return input_gradient, next_down, next_up, keys


def solution(mesh):
    dp, fsdp, section = mesh.devices.shape
    fine = Mesh(mesh.devices.reshape(4, dp // 4, fsdp // 2, 2, section), AXES)
    rows_by_width = P(ROWS, FSDP)
    return jax.shard_map(
        per_device,
        mesh=fine,
        in_specs=(
            rows_by_width,
            rows_by_width,
            P(ROWS),
            P(ROWS),
            P(FSDP, None),
            P(FSDP, None),
            P(None, FSDP),
            rows_by_width,
        ),
        out_specs=(rows_by_width, P(FSDP, None), P(None, FSDP), rows_by_width),
        check_vma=False,
    )
```

```python
import jax
import jax.numpy as jnp
from jax import lax
from jax.experimental import pallas as pl
from jax.experimental.pallas import tpu as pltpu
from jax.sharding import Mesh
from jax.sharding import PartitionSpec as P

adapter_scale = 0.5
step_rate = 16.0
clip_norm = 1.0

AXES = ("zhi", "y", "x", "zlo", "core")
FSDP = ("x", "zlo")
ROWS = ("zhi", "y", "core")
NEAR = ("y", "core")
FAR = "zhi"
TAIL = 16
bf16 = jnp.bfloat16
f32 = jnp.float32

NT = (((1,), (1,)), ((), ()))
TN = (((0,), (0,)), ((), ()))


def dot(a, b, dims=(((1,), (0,)), ((), ()))):
    return lax.dot_general(a, b, dims, preferred_element_type=f32)


Z_PAIRS = ((0, 1), (1, 0))
X_NEAR = ((0, 1), (1, 0), (2, 3), (3, 2))
X_FAR = ((0, 3), (3, 0), (1, 2), (2, 1))


def owner_mask(i):
    return (i & 1) ^ (2 if i & 2 else 0) ^ (6 if i & 4 else 0)


def swap(v, axis):
    return lax.all_to_all(v, axis, 0, 0, tiled=True)


VMEM = None
SMEM = pl.BlockSpec(memory_space=pltpu.SMEM)
ANY = pl.BlockSpec(memory_space=pl.ANY)
HBM = pl.BlockSpec(memory_space=pltpu.HBM)


def block(v):
    zeros = (0,) * len(v.shape)
    return pl.BlockSpec(v.shape, lambda i: zeros)


def call(kernel, outs, ins, args, flops=0, out_specs=None, limit=24, **more):
    moved = sum(a.size * a.dtype.itemsize for a in args) + sum(
        o.size * o.dtype.itemsize for o in outs
    )
    return pl.pallas_call(
        kernel,
        grid=(1,),
        in_specs=[spec or block(a) for spec, a in zip(ins, args, strict=True)],
        out_specs=out_specs or tuple(block(o) for o in outs),
        out_shape=tuple(outs),
        compiler_params=pltpu.CompilerParams(vmem_limit_bytes=limit * 1024 * 1024),
        cost_estimate=pl.CostEstimate(flops=flops, bytes_accessed=moved, transcendentals=0),
        **more,
    )(*args)


def shape(dims, kind):
    return jax.ShapeDtypeStruct(dims, kind)


def parts_kernel(
    lens, buckets, acts, og, down_w, up_w, gk_out, pay,
    acts_v, og_v, down_v, up_v, gk, parts, sems,
):
    rows = acts.shape[0]
    seqs = lens.shape[0]
    slot = rows // seqs
    peers = pay.shape[0]
    piece = rows // peers
    pairs = ((og, og_v), (up_w, up_v), (down_w, down_v), (acts, acts_v))
    loads = [pltpu.make_async_copy(a, b, sems.at[i]) for i, (a, b) in enumerate(pairs)]
    for c in loads:
        c.start()
    loads[0].wait()
    place = lax.broadcasted_iota(jnp.int32, (slot, 1), 0)
    for s in range(seqs):
        here = pl.ds(s * slot, slot)
        weight = jnp.where(place < lens[s], buckets[s].astype(f32) - 1.5, f32(0.0))
        gk[here, :] = (weight * og_v[here, :].astype(f32)).astype(bf16)
    first = len(pairs)
    store = pltpu.make_async_copy(gk, gk_out, sems.at[first])
    store.start()

    def put(k, v):
        v = v.astype(bf16)
        for j in range(peers):
            parts[j, k * piece : (k + 1) * piece, :] = v[j * piece : (j + 1) * piece]

    loads[1].wait()
    put(0, dot(gk[...], up_v[...].astype(bf16), NT))
    loads[2].wait()
    a_half = down_v[...].astype(bf16)
    loads[3].wait()
    put(1, dot(acts_v[...], a_half))
    last = pltpu.make_async_copy(parts, pay, sems.at[first + 1])
    last.start()
    store.wait()
    last.wait()


def prompts_kernel(
    place, prompts, frozen, down_w, acts, pay, keep, send, base, proj_v, keep_v, send_v, sems
):
    del acts
    rows = prompts.shape[0]
    peers, long, cols = pay.shape
    piece = rows // peers
    count = keep.shape[0] // rows
    base[...] = dot(prompts[...], frozen[...])

    def part(i):
        owner = place[0] ^ owner_mask(i)
        return base[:, pl.ds(pl.multiple_of(owner * cols, cols), cols)]

    for i in range(count):
        send_v[i * rows : (i + 1) * rows, :] = part(count + i).astype(bf16)
    copies = [pltpu.make_async_copy(send_v, send, sems.at[0])]
    copies[0].start()
    for i in range(count):
        keep_v[i * rows : (i + 1) * rows, :] = part(i)
    copies.append(pltpu.make_async_copy(keep_v, keep, sems.at[1]))
    copies[1].start()
    proj = dot(prompts[...], down_w[...].astype(bf16)).astype(bf16)
    for j in range(peers):
        proj_v[j] = proj[j * piece : (j + 1) * piece]
    copies.append(
        pltpu.make_async_copy(proj_v, pay.at[:, pl.ds(long - piece, piece), :], sems.at[2])
    )
    copies[2].start()
    for c in copies:
        c.wait()


def halve_kernel(held, got, keep, send, keep_v, send_v, sems):
    half = keep.shape[0]
    send_v[...] = (held[half:, :] + got[half:, :].astype(f32)).astype(bf16)
    copies = [pltpu.make_async_copy(send_v, send, sems.at[0])]
    copies[0].start()
    keep_v[...] = held[:half, :] + got[:half, :].astype(f32)
    copies.append(pltpu.make_async_copy(keep_v, keep, sems.at[1]))
    copies[1].start()
    for c in copies:
        c.wait()


def halve(held, got):
    dims = (held.shape[0] // 2, held.shape[1])
    return call(
        halve_kernel,
        [shape(dims, f32), shape(dims, bf16)],
        [VMEM] * 2,
        (held, got),
        out_specs=(HBM, HBM),
        limit=60,
        scratch_shapes=[
            pltpu.VMEM(dims, f32),
            pltpu.VMEM(dims, bf16),
            pltpu.SemaphoreType.DMA((2,)),
        ],
    )


def send_copies(value, pay, sems, first=0):
    copies = [
        pltpu.make_async_copy(value, pay.at[j, pl.ds(first, value.shape[0]), :], sems.at[j])
        for j in range(pay.shape[0])
    ]
    for c in copies:
        c.start()
    for c in copies:
        c.wait()


def sums_kernel(got_ref, pay_in, pay, sums_v, sems):
    del pay_in
    total = got_ref[0].astype(f32)
    for j in range(1, got_ref.shape[0]):
        total += got_ref[j].astype(f32)
    sums_v[...] = total.astype(bf16)
    send_copies(sums_v, pay, sems)


def rejoin(got_ref, first, piece):
    return jnp.concatenate(
        [got_ref[j, first : first + piece, :] for j in range(got_ref.shape[0])], axis=0
    )


def grads_kernel(got_ref, acts, gk, pay, pay_v, sem):
    rows = acts.shape[0]
    piece = rows // got_ref.shape[0]
    lanes = gk.shape[1]
    up = rejoin(got_ref, 0, piece)
    down = rejoin(got_ref, piece, piece)
    g = adapter_scale * jnp.concatenate([dot(up, acts[...], TN), dot(down, gk[...], TN)], axis=1)
    peers = pay.shape[0]
    step = g.shape[0] // peers
    for j in range(peers):
        pay_v[j] = jnp.concatenate(
            [
                g[j * step : (j + 1) * step, c * lanes : (c + 1) * lanes]
                for c in range(g.shape[1] // lanes)
            ],
            axis=0,
        ).astype(pay.dtype)
    copy = pltpu.make_async_copy(pay_v, pay, sem)
    copy.start()
    copy.wait()


def add_kernel(got_ref, pay, total_v, sems):
    total = got_ref[0].astype(f32)
    for j in range(1, got_ref.shape[0]):
        total += got_ref[j].astype(f32)
    total_v[...] = total.astype(pay.dtype)
    copies = [
        pltpu.make_async_copy(total_v, pay.at[j], sems.at[j]) for j in range(pay.shape[0])
    ]
    for c in copies:
        c.start()
    for c in copies:
        c.wait()


def add(got, peers):
    dims = got.shape[1:]
    (pay,) = call(
        add_kernel,
        [shape((peers,) + dims, bf16)],
        [VMEM],
        (got,),
        out_specs=(HBM,),
        scratch_shapes=[pltpu.VMEM(dims, bf16), pltpu.SemaphoreType.DMA((peers,))],
    )
    return pay


def whole_gradient(got_ref, rank):
    peers, long, _ = got_ref.shape
    step = rank // peers
    got = [got_ref[j].astype(f32) for j in range(peers)]
    return [
        jnp.concatenate([v[c * step : (c + 1) * step] for v in got], axis=0)
        for c in range(long // step)
    ]


def project_kernel(got_ref, prompts, pay):
    peers, long, rank = pay.shape
    piece = long - TAIL
    blocks = whole_gradient(got_ref, rank)
    squares = sum(b * b for b in blocks)
    total = jnp.sum(squares, keepdims=True)
    high = total.astype(bf16)
    rest = total - high.astype(f32)
    middle = rest.astype(bf16)
    low = (rest - middle.astype(f32)).astype(bf16)
    lane = lax.broadcasted_iota(jnp.int32, (TAIL, rank), 1)
    tail = jnp.where(
        lane == 0,
        high.astype(f32),
        jnp.where(lane == 1, middle.astype(f32), jnp.where(lane == 2, low.astype(f32), 0.0)),
    ).astype(bf16)
    g_down = jnp.concatenate(blocks[:-1], axis=1).astype(bf16)
    proj = dot(prompts[...], g_down, NT).astype(bf16)
    for j in range(peers):
        pay[j, :piece, :] = proj[j * piece : (j + 1) * piece]
        pay[j, piece:, :] = tail


def step_factor(got):
    peers, long, rank = got.shape
    piece = long - TAIL
    lane = lax.broadcasted_iota(jnp.int32, (TAIL, rank), 1)
    row = lax.broadcasted_iota(jnp.int32, (TAIL, rank), 0)
    tail = got[0, piece:, :].astype(f32)
    for j in range(1, peers):
        tail += got[j, piece:, :].astype(f32)
    squares = jnp.sum(jnp.where((row == 0) & (lane < 3), tail, 0.0), keepdims=True)
    return step_rate * jnp.minimum(1.0, clip_norm / jnp.sqrt(squares + 1e-12))


def rows_kernel(got, pa_rows, pay, rows_v, sems):
    peers, long, _ = got.shape
    piece = long - TAIL
    p_g = got[0, :piece, :].astype(f32)
    for j in range(1, peers):
        p_g += got[j, :piece, :].astype(f32)
    rows_v[...] = (pa_rows[...] - step_factor(got) * p_g).astype(bf16)
    send_copies(rows_v, pay, sems)


def weights_kernel(got, got_g, down_w, up_w, base, base_got, next_down, next_up):
    del base, base_got
    rank = down_w.shape[1]
    factor = step_factor(got)
    blocks = whole_gradient(got_g, rank)
    for c, part in enumerate(blocks[:-1]):
        here = pl.ds(c * rank, rank)
        next_down[here, :] = down_w[here, :] - factor * part.T
    next_up[...] = up_w[...] - factor * blocks[-1]


def keys_kernel(got, base, base_got, sums, got_g, up_w, keys):
    proj = rejoin(got, 0, got.shape[1])
    new_up = up_w[...] - step_factor(sums) * whole_gradient(got_g, up_w.shape[0])[-1]
    keys[...] = (
        base[...]
        + base_got[...].astype(f32)
        + adapter_scale * dot(proj, new_up.astype(bf16))
    ).astype(bf16)


def input_kernel(place, near, far, up, down_w, frozen, out, gk):
    rows = out.shape[0]
    lanes = near.shape[1]
    count = near.shape[0] // rows
    for i in range(2 * count):
        ref = near if i < count else far
        block = ref[(i % count) * rows : (i % count + 1) * rows, :]
        owner = place[0] ^ owner_mask(i)
        gk[:, pl.ds(pl.multiple_of(owner * lanes, lanes), lanes)] = block
    a_half = down_w[...].astype(bf16)
    out[...] = (
        dot(gk[...], frozen[...], NT) + adapter_scale * dot(up[...], a_half, NT)
    ).astype(bf16)


def beside_kernel(got, two, other, pa_out, up_out, four):
    count = two.shape[0]
    four[:count, :] = two[...]
    four[count:, :] = other[...]
    peers = got.shape[0]
    piece = pa_out.shape[0]
    up_out[...] = rejoin(got, 0, piece)
    total = got[0, 2 * piece :, :].astype(f32)
    for j in range(1, peers):
        total += got[j, 2 * piece :, :].astype(f32)
    pa_out[...] = total


def per_device(acts, output_gradient, lengths, buckets, frozen, down_w, up_w, prompts):
    rows = acts.shape[0]
    width, rank = down_w.shape
    cols = up_w.shape[1]
    n_f = lax.axis_size(FSDP)
    n_near = lax.axis_size(NEAR)
    n_far = lax.axis_size(FAR)
    piece = rows // n_f
    slab = (width + cols) // n_near

    gk, pay = call(
        parts_kernel,
        [shape((rows, cols), bf16), shape((n_f, 2 * piece, rank), bf16)],
        [SMEM, SMEM] + [ANY] * 4,
        (lengths, buckets, acts, output_gradient, down_w, up_w),
        flops=2 * rows * rank * (width + cols),
        out_specs=(HBM, HBM),
        limit=60,
        scratch_shapes=[
            pltpu.VMEM((rows, width), bf16),
            pltpu.VMEM((rows, cols), bf16),
            pltpu.VMEM((width, rank), f32),
            pltpu.VMEM((rank, cols), f32),
            pltpu.VMEM((rows, cols), bf16),
            pltpu.VMEM((n_f, 2 * piece, rank), bf16),
            pltpu.SemaphoreType.DMA((6,)),
        ],
    )
    got = swap(pay, FSDP)
    other = lax.ppermute(gk, "zlo", Z_PAIRS)
    place = lax.axis_index(FSDP).reshape(1)
    half = n_f // 2 * rows
    pay, held, send = call(
        prompts_kernel,
        [shape((n_f, 3 * piece, rank), bf16), shape((half, cols), f32), shape((half, cols), bf16)],
        [SMEM] + [VMEM] * 4,
        (place, prompts, frozen, down_w, acts),
        flops=2 * rows * width * (cols * n_f + rank),
        out_specs=(HBM, HBM, HBM),
        limit=60,
        scratch_shapes=[
            pltpu.VMEM((rows, cols * n_f), f32),
            pltpu.VMEM((n_f, piece, rank), bf16),
            pltpu.VMEM((half, cols), f32),
            pltpu.VMEM((half, cols), bf16),
            pltpu.SemaphoreType.DMA((3,)),
        ],
    )
    got, pay, held, send, other = lax.optimization_barrier((got, pay, held, send, other))
    (pay,) = call(
        sums_kernel,
        [shape(pay.shape, bf16)],
        [VMEM, HBM],
        (got, pay),
        input_output_aliases={1: 0},
        out_specs=(HBM,),
        limit=60,
        scratch_shapes=[pltpu.VMEM((2 * piece, rank), bf16), pltpu.SemaphoreType.DMA((n_f,))],
    )
    got = swap(pay, FSDP)
    two = jnp.concatenate([gk, other], axis=0)
    other = lax.ppermute(two, "x", X_NEAR)
    base_got = lax.ppermute(send, "x", X_FAR)
    got, two = lax.optimization_barrier((got, two))

    (pay,) = call(
        grads_kernel,
        [shape((n_near, slab, rank), bf16)],
        [VMEM] * 3,
        (got, acts, gk),
        flops=2 * rows * rank * (width + cols),
        out_specs=(HBM,),
        scratch_shapes=[pltpu.VMEM((n_near, slab, rank), bf16), pltpu.SemaphoreType.DMA],
    )
    got_g = swap(pay, NEAR)
    pa_rows, up, four = call(
        beside_kernel,
        [
            shape((piece, rank), f32),
            shape((rows, rank), bf16),
            shape((n_f // 2 * rows, cols), bf16),
        ],
        [VMEM] * 3,
        (got, two, other),
        limit=60,
    )
    other = lax.ppermute(four, "x", X_FAR)
    held, send = halve(held, base_got)
    got_g, pa_rows, up, held, send = lax.optimization_barrier((got_g, pa_rows, up, held, send))
    base_got = lax.ppermute(send, "x", X_NEAR)
    got = swap(add(got_g, n_far), FAR)
    got_g = swap(add(got, n_near), NEAR)
    base, send = halve(held, base_got)
    base_got = lax.ppermute(send, "zlo", Z_PAIRS)
    got_g, base, base_got = lax.optimization_barrier((got_g, base, base_got))

    (pay,) = call(
        project_kernel,
        [shape((n_f, piece + TAIL, rank), bf16)],
        [VMEM] * 2,
        (got_g, prompts),
        flops=2 * rows * width * rank,
    )
    sums = swap(pay, FSDP)
    (pay,) = call(
        rows_kernel,
        [shape((n_f, piece, rank), bf16)],
        [VMEM] * 2,
        (sums, pa_rows),
        out_specs=(HBM,),
        scratch_shapes=[pltpu.VMEM((piece, rank), bf16), pltpu.SemaphoreType.DMA((n_f,))],
    )
    got = swap(pay, FSDP)
    next_down, next_up = call(
        weights_kernel,
        [shape((width, rank), f32), shape((rank, cols), f32)],
        [VMEM] * 6,
        (sums, got_g, down_w, up_w, base, base_got),
    )
    (input_gradient,) = call(
        input_kernel,
        [shape((rows, width), bf16)],
        [SMEM] + [VMEM] * 5,
        (place, four, other, up, down_w, frozen),
        flops=2 * rows * width * (cols * n_f + rank),
        scratch_shapes=[pltpu.VMEM((rows, cols * n_f), bf16)],
    )
    got, next_down, next_up, input_gradient = lax.optimization_barrier(
        (got, next_down, next_up, input_gradient)
    )
    (keys,) = call(
        keys_kernel,
        [shape((rows, cols), bf16)],
        [VMEM] * 6,
        (got, base, base_got, sums, got_g, up_w),
        flops=2 * rows * rank * cols,
    )
    return input_gradient, next_down, next_up, keys


def solution(mesh):
    dp, fsdp, section = mesh.devices.shape
    fine = Mesh(mesh.devices.reshape(4, dp // 4, fsdp // 2, 2, section), AXES)
    rows_by_width = P(ROWS, FSDP)
    return jax.shard_map(
        per_device,
        mesh=fine,
        in_specs=(
            rows_by_width,
            rows_by_width,
            P(ROWS),
            P(ROWS),
            P(FSDP, None),
            P(FSDP, None),
            P(None, FSDP),
            rows_by_width,
        ),
        out_specs=(rows_by_width, P(FSDP, None), P(None, FSDP), rows_by_width),
        check_vma=False,
    )
```

```python
import jax
import jax.numpy as jnp
from jax import lax
from jax.experimental import pallas as pl
from jax.experimental.pallas import tpu as pltpu
from jax.sharding import Mesh
from jax.sharding import PartitionSpec as P

adapter_scale = 0.5
step_rate = 16.0
clip_norm = 1.0

AXES = ("zhi", "y", "x", "zlo", "core")
FSDP = ("x", "zlo")
ROWS = ("zhi", "y", "core")
NEAR = ("y", "core")
FAR = "zhi"
TAIL = 16
bf16 = jnp.bfloat16
f32 = jnp.float32

NT = (((1,), (1,)), ((), ()))
TN = (((0,), (0,)), ((), ()))


def dot(a, b, dims=(((1,), (0,)), ((), ()))):
    return lax.dot_general(a, b, dims, preferred_element_type=f32)


Z_PAIRS = ((0, 1), (1, 0))
X_NEAR = ((0, 1), (1, 0), (2, 3), (3, 2))
X_FAR = ((0, 3), (3, 0), (1, 2), (2, 1))


def owner_mask(i):
    return (i & 1) ^ (2 if i & 2 else 0) ^ (6 if i & 4 else 0)


def swap(v, axis):
    return lax.all_to_all(v, axis, 0, 0, tiled=True)


VMEM = None
SMEM = pl.BlockSpec(memory_space=pltpu.SMEM)
ANY = pl.BlockSpec(memory_space=pl.ANY)
HBM = pl.BlockSpec(memory_space=pltpu.HBM)


def block(v):
    zeros = (0,) * len(v.shape)
    return pl.BlockSpec(v.shape, lambda i: zeros)


def call(kernel, outs, ins, args, flops=0, out_specs=None, limit=24, **more):
    moved = sum(a.size * a.dtype.itemsize for a in args) + sum(
        o.size * o.dtype.itemsize for o in outs
    )
    return pl.pallas_call(
        kernel,
        grid=(1,),
        in_specs=[spec or block(a) for spec, a in zip(ins, args, strict=True)],
        out_specs=out_specs or tuple(block(o) for o in outs),
        out_shape=tuple(outs),
        compiler_params=pltpu.CompilerParams(vmem_limit_bytes=limit * 1024 * 1024),
        cost_estimate=pl.CostEstimate(flops=flops, bytes_accessed=moved, transcendentals=0),
        **more,
    )(*args)


def shape(dims, kind):
    return jax.ShapeDtypeStruct(dims, kind)


def parts_kernel(
    lens, buckets, acts, og, down_w, up_w, gk_out, two_out, pay,
    acts_v, og_v, down_v, up_v, gk, parts, sems,
):
    rows = acts.shape[0]
    seqs = lens.shape[0]
    slot = rows // seqs
    peers = pay.shape[0]
    piece = rows // peers
    pairs = ((og, og_v), (up_w, up_v), (down_w, down_v), (acts, acts_v))
    loads = [pltpu.make_async_copy(a, b, sems.at[i]) for i, (a, b) in enumerate(pairs)]
    for c in loads:
        c.start()
    loads[0].wait()
    place = lax.broadcasted_iota(jnp.int32, (slot, 1), 0)
    for s in range(seqs):
        here = pl.ds(s * slot, slot)
        weight = jnp.where(place < lens[s], buckets[s].astype(f32) - 1.5, f32(0.0))
        gk[here, :] = (weight * og_v[here, :].astype(f32)).astype(bf16)
    first = len(pairs)
    stores = [
        pltpu.make_async_copy(gk, gk_out, sems.at[first]),
        pltpu.make_async_copy(gk, two_out.at[pl.ds(0, rows), :], sems.at[first + 1]),
    ]
    for c in stores:
        c.start()

    def put(k, v):
        v = v.astype(bf16)
        for j in range(peers):
            parts[j, k * piece : (k + 1) * piece, :] = v[j * piece : (j + 1) * piece]

    loads[1].wait()
    put(0, dot(gk[...], up_v[...].astype(bf16), NT))
    loads[2].wait()
    a_half = down_v[...].astype(bf16)
    loads[3].wait()
    put(1, dot(acts_v[...], a_half))
    last = pltpu.make_async_copy(parts, pay, sems.at[first + 2])
    last.start()
    for c in stores:
        c.wait()
    last.wait()


def base_part(place, prompts, frozen, i, cols):
    owner = place[0] ^ owner_mask(i)
    return dot(prompts[...], frozen[:, pl.ds(pl.multiple_of(owner * cols, cols), cols)])


def prompts_kernel(place, prompts, frozen, down_w, proj_out, send):
    rows = prompts.shape[0]
    cols = send.shape[1]
    count = send.shape[0] // rows
    for i in range(count):
        send[i * rows : (i + 1) * rows, :] = base_part(
            place, prompts, frozen, count + i, cols
        ).astype(bf16)
    proj_out[...] = dot(prompts[...], down_w[...].astype(bf16)).astype(bf16)


def own_half_kernel(place, prompts, frozen, got, keep, send):
    rows = prompts.shape[0]
    cols = send.shape[1]
    count = send.shape[0] // rows
    for i in range(2 * count):
        part = base_part(place, prompts, frozen, i, cols)
        part += got[i * rows : (i + 1) * rows, :].astype(f32)
        if i < count:
            keep[i * rows : (i + 1) * rows, :] = part
        else:
            send[(i - count) * rows : (i - count + 1) * rows, :] = part.astype(bf16)


def halve_kernel(held, got, keep, send):
    half = keep.shape[0]
    keep[...] = held[:half, :] + got[:half, :].astype(f32)
    send[...] = (held[half:, :] + got[half:, :].astype(f32)).astype(bf16)


def halve(held, got):
    half = held.shape[0] // 2
    dims = (half, held.shape[1])
    return call(halve_kernel, [shape(dims, f32), shape(dims, bf16)], [VMEM] * 2, (held, got))


def sums_kernel(got_ref, proj, pay, pay_v, sem):
    peers, long, _ = pay.shape
    part = got_ref.shape[1]
    piece = long - part
    total = got_ref[0].astype(f32)
    for j in range(1, peers):
        total += got_ref[j].astype(f32)
    total = total.astype(bf16)
    for j in range(peers):
        pay_v[j, :part, :] = total
        pay_v[j, part:, :] = proj[j * piece : (j + 1) * piece, :]
    copy = pltpu.make_async_copy(pay_v, pay, sem)
    copy.start()
    copy.wait()


def rejoin(got_ref, first, piece):
    return jnp.concatenate(
        [got_ref[j, first : first + piece, :] for j in range(got_ref.shape[0])], axis=0
    )


def grads_kernel(got_ref, acts, gk, pay, pay_v, sem):
    rows = acts.shape[0]
    piece = rows // got_ref.shape[0]
    lanes = gk.shape[1]
    up = rejoin(got_ref, 0, piece)
    down = rejoin(got_ref, piece, piece)
    g = adapter_scale * jnp.concatenate([dot(up, acts[...], TN), dot(down, gk[...], TN)], axis=1)
    peers = pay.shape[0]
    step = g.shape[0] // peers
    for j in range(peers):
        pay_v[j] = jnp.concatenate(
            [
                g[j * step : (j + 1) * step, c * lanes : (c + 1) * lanes]
                for c in range(g.shape[1] // lanes)
            ],
            axis=0,
        ).astype(pay.dtype)
    copy = pltpu.make_async_copy(pay_v, pay, sem)
    copy.start()
    copy.wait()


def add_kernel(got_ref, pay, total_v, sems):
    total = got_ref[0].astype(f32)
    for j in range(1, got_ref.shape[0]):
        total += got_ref[j].astype(f32)
    total_v[...] = total.astype(pay.dtype)
    copies = [
        pltpu.make_async_copy(total_v, pay.at[j], sems.at[j]) for j in range(pay.shape[0])
    ]
    for c in copies:
        c.start()
    for c in copies:
        c.wait()


def add(got, peers):
    dims = got.shape[1:]
    (pay,) = call(
        add_kernel,
        [shape((peers,) + dims, bf16)],
        [VMEM],
        (got,),
        out_specs=(HBM,),
        scratch_shapes=[pltpu.VMEM(dims, bf16), pltpu.SemaphoreType.DMA((peers,))],
    )
    return pay


def whole_gradient(got_ref, rank):
    peers, long, _ = got_ref.shape
    step = rank // peers
    got = [got_ref[j].astype(f32) for j in range(peers)]
    return [
        jnp.concatenate([v[c * step : (c + 1) * step] for v in got], axis=0)
        for c in range(long // step)
    ]


def pieces(total):
    high = total.astype(bf16)
    rest = total - high.astype(f32)
    middle = rest.astype(bf16)
    low = (rest - middle.astype(f32)).astype(bf16)
    return high.astype(f32), middle.astype(f32), low.astype(f32)


def make_tail(total, rank):
    lane = lax.broadcasted_iota(jnp.int32, (TAIL, rank), 1)
    high, middle, low = pieces(total)
    return jnp.where(
        lane == 0, high, jnp.where(lane == 1, middle, jnp.where(lane == 2, low, 0.0))
    ).astype(bf16)


def read_tail(tail):
    lane = lax.broadcasted_iota(jnp.int32, tail.shape, 1)
    row = lax.broadcasted_iota(jnp.int32, tail.shape, 0)
    return jnp.sum(jnp.where((row == 0) & (lane < 3), tail, 0.0), keepdims=True)


def project_kernel(got_ref, prompts, pa_rows, out):
    rank = out.shape[1]
    rows = prompts.shape[0]
    blocks = whole_gradient(got_ref, rank)
    total = jnp.sum(sum(b * b for b in blocks), keepdims=True)
    out[rows : rows + TAIL, :] = make_tail(total, rank)
    out[rows + TAIL :, :] = pa_rows[...]
    g_down = jnp.concatenate(blocks[:-1], axis=1).astype(bf16)
    out[:rows, :] = dot(prompts[...], g_down, NT).astype(bf16)


def pair_kernel(place, mine, got, pay):
    peers, long, rank = pay.shape
    piece = long - mine.shape[0]
    rows = mine.shape[0] - TAIL - piece
    proj = (mine[:rows, :].astype(f32) + got[:rows, :].astype(f32)).astype(bf16)
    here = slice(rows, rows + TAIL)
    total = read_tail(mine[here, :].astype(f32) + got[here, :].astype(f32))
    tail = make_tail(total, rank)
    first = rows + TAIL
    side = place[0] & 1
    own = pl.ds(pl.multiple_of(first + side * piece, 16), piece)
    theirs = pl.ds(pl.multiple_of(first + (1 - side) * piece, 16), piece)
    for j in range(peers):
        pay[j, :rows, :] = proj
        pay[j, here, :] = tail
        pay[j, own, :] = mine[first:, :]
        pay[j, theirs, :] = got[first:, :]


def finish_kernel(got, base, base_got, got_g, down_w, up_w, next_down, next_up, keys):
    rows = keys.shape[0]
    rank = down_w.shape[1]
    peers = got.shape[0]
    p_g = got[0, :rows, :].astype(f32)
    tail = got[0, rows : rows + TAIL, :].astype(f32)
    for j in range(1, peers):
        p_g += got[j, :rows, :].astype(f32)
        tail += got[j, rows : rows + TAIL, :].astype(f32)
    squares = read_tail(tail)
    factor = step_rate * jnp.minimum(1.0, clip_norm / jnp.sqrt(squares + 1e-12))
    blocks = whole_gradient(got_g, rank)
    for c, block in enumerate(blocks[:-1]):
        here = pl.ds(c * rank, rank)
        next_down[here, :] = down_w[here, :] - factor * block.T
    new_up = up_w[...] - factor * blocks[-1]
    next_up[...] = new_up
    proj = rejoin(got, rows + TAIL, rows // peers).astype(f32) - factor * p_g
    keys[...] = (
        base[...] + base_got[...].astype(f32) + adapter_scale * dot(proj.astype(bf16), new_up.astype(bf16))
    ).astype(bf16)


def input_kernel(place, near, far, up, down_w, frozen, out, gk):
    rows = out.shape[0]
    lanes = near.shape[1]
    count = near.shape[0] // rows
    for i in range(2 * count):
        ref = near if i < count else far
        block = ref[(i % count) * rows : (i % count + 1) * rows, :]
        owner = place[0] ^ owner_mask(i)
        gk[:, pl.ds(pl.multiple_of(owner * lanes, lanes), lanes)] = block
    a_half = down_w[...].astype(bf16)
    out[...] = (
        dot(gk[...], frozen[...], NT) + adapter_scale * dot(up[...], a_half, NT)
    ).astype(bf16)


def beside_kernel(got, two, other, pa_out, up_out, four):
    count = two.shape[0]
    four[:count, :] = two[...]
    four[count:, :] = other[...]
    peers = got.shape[0]
    piece = pa_out.shape[0]
    up_out[...] = rejoin(got, 0, piece)
    total = got[0, 2 * piece :, :].astype(f32)
    for j in range(1, peers):
        total += got[j, 2 * piece :, :].astype(f32)
    pa_out[...] = total.astype(bf16)


def per_device(acts, output_gradient, lengths, buckets, frozen, down_w, up_w, prompts):
    rows = acts.shape[0]
    width, rank = down_w.shape
    cols = up_w.shape[1]
    n_f = lax.axis_size(FSDP)
    n_near = lax.axis_size(NEAR)
    n_far = lax.axis_size(FAR)
    piece = rows // n_f
    slab = (width + cols) // n_near

    gk, two, pay = call(
        parts_kernel,
        [shape((rows, cols), bf16), shape((2 * rows, cols), bf16), shape((n_f, 2 * piece, rank), bf16)],
        [SMEM, SMEM] + [ANY] * 4,
        (lengths, buckets, acts, output_gradient, down_w, up_w),
        flops=2 * rows * rank * (width + cols),
        out_specs=(HBM, HBM, HBM),
        limit=60,
        scratch_shapes=[
            pltpu.VMEM((rows, width), bf16),
            pltpu.VMEM((rows, cols), bf16),
            pltpu.VMEM((width, rank), f32),
            pltpu.VMEM((rank, cols), f32),
            pltpu.VMEM((rows, cols), bf16),
            pltpu.VMEM((n_f, 2 * piece, rank), bf16),
            pltpu.SemaphoreType.DMA((7,)),
        ],
    )
    got = swap(pay, FSDP)
    other = lax.ppermute(gk, "zlo", Z_PAIRS)
    place = lax.axis_index(FSDP).reshape(1)
    proj, send = call(
        prompts_kernel,
        [shape((rows, rank), bf16), shape((n_f // 2 * rows, cols), bf16)],
        [SMEM] + [VMEM] * 3,
        (place, prompts, frozen, down_w),
        flops=rows * width * (cols * n_f + 2 * rank),
    )
    got, proj, send, other = lax.optimization_barrier((got, proj, send, other))
    (pay,) = call(
        sums_kernel,
        [shape((n_f, 3 * piece, rank), bf16)],
        [VMEM] * 2,
        (got, proj),
        out_specs=(HBM,),
        scratch_shapes=[pltpu.VMEM((n_f, 3 * piece, rank), bf16), pltpu.SemaphoreType.DMA],
    )
    got = swap(pay, FSDP)
    two = lax.dynamic_update_slice(two, other, (rows, 0))
    other = lax.ppermute(two, "x", X_NEAR)
    base_got = lax.ppermute(send, "x", X_FAR)
    got, two = lax.optimization_barrier((got, two))

    (pay,) = call(
        grads_kernel,
        [shape((n_near, slab, rank), bf16)],
        [VMEM] * 3,
        (got, acts, gk),
        flops=2 * rows * rank * (width + cols),
        out_specs=(HBM,),
        scratch_shapes=[pltpu.VMEM((n_near, slab, rank), bf16), pltpu.SemaphoreType.DMA],
    )
    got_g = swap(pay, NEAR)
    pa_rows, up, four = call(
        beside_kernel,
        [
            shape((piece, rank), bf16),
            shape((rows, rank), bf16),
            shape((n_f // 2 * rows, cols), bf16),
        ],
        [VMEM] * 3,
        (got, two, other),
    )
    other = lax.ppermute(four, "x", X_FAR)
    held, send = call(
        own_half_kernel,
        [shape((n_f // 4 * rows, cols), f32), shape((n_f // 4 * rows, cols), bf16)],
        [SMEM] + [VMEM] * 3,
        (place, prompts, frozen, base_got),
        flops=rows * width * cols * n_f,
    )
    got_g, pa_rows, up, held, send = lax.optimization_barrier((got_g, pa_rows, up, held, send))
    base_got = lax.ppermute(send, "x", X_NEAR)
    got = swap(add(got_g, n_far), FAR)
    got_g = swap(add(got, n_near), NEAR)
    (input_gradient,) = call(
        input_kernel,
        [shape((rows, width), bf16)],
        [SMEM] + [VMEM] * 5,
        (place, four, other, up, down_w, frozen),
        flops=2 * rows * width * (cols * n_f + rank),
        scratch_shapes=[pltpu.VMEM((rows, cols * n_f), bf16)],
    )
    base, send = halve(held, base_got)
    base_got = lax.ppermute(send, "zlo", Z_PAIRS)
    got_g, input_gradient, base, base_got = lax.optimization_barrier(
        (got_g, input_gradient, base, base_got)
    )
    (mine,) = call(
        project_kernel,
        [shape((rows + TAIL + piece, rank), bf16)],
        [VMEM] * 3,
        (got_g, prompts, pa_rows),
        flops=2 * rows * width * rank,
    )
    got = lax.ppermute(mine, "zlo", Z_PAIRS)
    n_x = lax.axis_size("x")
    (pay,) = call(
        pair_kernel,
        [shape((n_x, rows + TAIL + 2 * piece, rank), bf16)],
        [SMEM] + [VMEM] * 2,
        (place, mine, got),
    )
    got = swap(pay, "x")
    next_down, next_up, keys = call(
        finish_kernel,
        [shape((width, rank), f32), shape((rank, cols), f32), shape((rows, cols), bf16)],
        [VMEM] * 6,
        (got, base, base_got, got_g, down_w, up_w),
        flops=2 * rows * rank * cols,
    )
    return input_gradient, next_down, next_up, keys


def solution(mesh):
    dp, fsdp, section = mesh.devices.shape
    fine = Mesh(mesh.devices.reshape(4, dp // 4, fsdp // 2, 2, section), AXES)
    rows_by_width = P(ROWS, FSDP)
    return jax.shard_map(
        per_device,
        mesh=fine,
        in_specs=(
            rows_by_width,
            rows_by_width,
            P(ROWS),
            P(ROWS),
            P(FSDP, None),
            P(FSDP, None),
            P(None, FSDP),
            rows_by_width,
        ),
        out_specs=(rows_by_width, P(FSDP, None), P(None, FSDP), rows_by_width),
        check_vma=False,
    )
```

```python
import jax
import jax.numpy as jnp
from jax import lax
from jax.experimental import pallas as pl
from jax.experimental.pallas import tpu as pltpu
from jax.sharding import Mesh
from jax.sharding import PartitionSpec as P

adapter_scale = 0.5
step_rate = 16.0
clip_norm = 1.0

AXES = ("zhi", "y", "x", "zlo", "core")
FSDP = ("x", "zlo")
ROWS = ("zhi", "y", "core")
NEAR = ("y", "core")
FAR = "zhi"
TAIL = 16
bf16 = jnp.bfloat16
f32 = jnp.float32

NT = (((1,), (1,)), ((), ()))
TN = (((0,), (0,)), ((), ()))


def dot(a, b, dims=(((1,), (0,)), ((), ()))):
    return lax.dot_general(a, b, dims, preferred_element_type=f32)


Z_PAIRS = ((0, 1), (1, 0))
X_NEAR = ((0, 1), (1, 0), (2, 3), (3, 2))
X_FAR = ((0, 3), (3, 0), (1, 2), (2, 1))


def owner_mask(i):
    return (i & 1) ^ (2 if i & 2 else 0) ^ (6 if i & 4 else 0)


def swap(v, axis):
    return lax.all_to_all(v, axis, 0, 0, tiled=True)


VMEM = None
SMEM = pl.BlockSpec(memory_space=pltpu.SMEM)
ANY = pl.BlockSpec(memory_space=pl.ANY)
HBM = pl.BlockSpec(memory_space=pltpu.HBM)


def block(v):
    zeros = (0,) * len(v.shape)
    return pl.BlockSpec(v.shape, lambda i: zeros)


def call(kernel, outs, ins, args, flops=0, out_specs=None, limit=24, **more):
    moved = sum(a.size * a.dtype.itemsize for a in args) + sum(
        o.size * o.dtype.itemsize for o in outs
    )
    return pl.pallas_call(
        kernel,
        grid=(1,),
        in_specs=[spec or block(a) for spec, a in zip(ins, args, strict=True)],
        out_specs=out_specs or tuple(block(o) for o in outs),
        out_shape=tuple(outs),
        compiler_params=pltpu.CompilerParams(vmem_limit_bytes=limit * 1024 * 1024),
        cost_estimate=pl.CostEstimate(flops=flops, bytes_accessed=moved, transcendentals=0),
        **more,
    )(*args)


def shape(dims, kind):
    return jax.ShapeDtypeStruct(dims, kind)


def parts_kernel(
    lens, buckets, acts, og, down_w, up_w, gk_out, two_out, pay,
    acts_v, og_v, down_v, up_v, gk, parts, sems,
):
    rows = acts.shape[0]
    seqs = lens.shape[0]
    slot = rows // seqs
    peers = pay.shape[0]
    piece = rows // peers
    pairs = ((og, og_v), (up_w, up_v), (down_w, down_v), (acts, acts_v))
    loads = [pltpu.make_async_copy(a, b, sems.at[i]) for i, (a, b) in enumerate(pairs)]
    for c in loads:
        c.start()
    loads[0].wait()
    place = lax.broadcasted_iota(jnp.int32, (slot, 1), 0)
    for s in range(seqs):
        here = pl.ds(s * slot, slot)
        weight = jnp.where(place < lens[s], buckets[s].astype(f32) - 1.5, f32(0.0))
        gk[here, :] = (weight * og_v[here, :].astype(f32)).astype(bf16)
    first = len(pairs)
    stores = [
        pltpu.make_async_copy(gk, gk_out, sems.at[first]),
        pltpu.make_async_copy(gk, two_out.at[pl.ds(0, rows), :], sems.at[first + 1]),
    ]
    for c in stores:
        c.start()

    def put(k, v):
        v = v.astype(bf16)
        for j in range(peers):
            parts[j, k * piece : (k + 1) * piece, :] = v[j * piece : (j + 1) * piece]

    loads[1].wait()
    put(0, dot(gk[...], up_v[...].astype(bf16), NT))
    loads[2].wait()
    a_half = down_v[...].astype(bf16)
    loads[3].wait()
    put(1, dot(acts_v[...], a_half))
    last = pltpu.make_async_copy(parts, pay, sems.at[first + 2])
    last.start()
    for c in stores:
        c.wait()
    last.wait()


def base_part(place, prompts, frozen, i, cols):
    owner = place[0] ^ owner_mask(i)
    return dot(prompts[...], frozen[:, pl.ds(pl.multiple_of(owner * cols, cols), cols)])


def prompts_kernel(place, prompts, frozen, down_w, proj_out, send):
    rows = prompts.shape[0]
    cols = send.shape[1]
    count = send.shape[0] // rows
    for i in range(count):
        send[i * rows : (i + 1) * rows, :] = base_part(
            place, prompts, frozen, count + i, cols
        ).astype(bf16)
    proj_out[...] = dot(prompts[...], down_w[...].astype(bf16)).astype(bf16)


def own_half_kernel(place, prompts, frozen, got, keep, send):
    rows = prompts.shape[0]
    cols = send.shape[1]
    count = send.shape[0] // rows
    for i in range(2 * count):
        part = base_part(place, prompts, frozen, i, cols)
        part += got[i * rows : (i + 1) * rows, :].astype(f32)
        if i < count:
            keep[i * rows : (i + 1) * rows, :] = part
        else:
            send[(i - count) * rows : (i - count + 1) * rows, :] = part.astype(bf16)


def halve_kernel(held, got, keep, send):
    half = keep.shape[0]
    keep[...] = held[:half, :] + got[:half, :].astype(f32)
    send[...] = (held[half:, :] + got[half:, :].astype(f32)).astype(bf16)


def halve(held, got):
    half = held.shape[0] // 2
    dims = (half, held.shape[1])
    return call(halve_kernel, [shape(dims, f32), shape(dims, bf16)], [VMEM] * 2, (held, got))


def sums_kernel(got_ref, proj, pay, pay_v, sem):
    peers, long, _ = pay.shape
    part = got_ref.shape[1]
    piece = long - part
    total = got_ref[0].astype(f32)
    for j in range(1, peers):
        total += got_ref[j].astype(f32)
    total = total.astype(bf16)
    for j in range(peers):
        pay_v[j, :part, :] = total
        pay_v[j, part:, :] = proj[j * piece : (j + 1) * piece, :]
    copy = pltpu.make_async_copy(pay_v, pay, sem)
    copy.start()
    copy.wait()


def rejoin(got_ref, first, piece):
    return jnp.concatenate(
        [got_ref[j, first : first + piece, :] for j in range(got_ref.shape[0])], axis=0
    )


def grads_kernel(got_ref, acts, gk, pay, pay_v, sem):
    rows = acts.shape[0]
    piece = rows // got_ref.shape[0]
    lanes = gk.shape[1]
    up = rejoin(got_ref, 0, piece)
    down = rejoin(got_ref, piece, piece)
    g = adapter_scale * jnp.concatenate([dot(up, acts[...], TN), dot(down, gk[...], TN)], axis=1)
    peers = pay.shape[0]
    step = g.shape[0] // peers
    for j in range(peers):
        pay_v[j] = jnp.concatenate(
            [
                g[j * step : (j + 1) * step, c * lanes : (c + 1) * lanes]
                for c in range(g.shape[1] // lanes)
            ],
            axis=0,
        ).astype(pay.dtype)
    copy = pltpu.make_async_copy(pay_v, pay, sem)
    copy.start()
    copy.wait()


def add_kernel(got_ref, pay, total_v, sems):
    total = got_ref[0].astype(f32)
    for j in range(1, got_ref.shape[0]):
        total += got_ref[j].astype(f32)
    total_v[...] = total.astype(pay.dtype)
    copies = [
        pltpu.make_async_copy(total_v, pay.at[j], sems.at[j]) for j in range(pay.shape[0])
    ]
    for c in copies:
        c.start()
    for c in copies:
        c.wait()


def add(got, peers):
    dims = got.shape[1:]
    (pay,) = call(
        add_kernel,
        [shape((peers,) + dims, bf16)],
        [VMEM],
        (got,),
        out_specs=(HBM,),
        scratch_shapes=[pltpu.VMEM(dims, bf16), pltpu.SemaphoreType.DMA((peers,))],
    )
    return pay


def whole_gradient(got_ref, rank):
    peers, long, _ = got_ref.shape
    step = rank // peers
    got = [got_ref[j].astype(f32) for j in range(peers)]
    return [
        jnp.concatenate([v[c * step : (c + 1) * step] for v in got], axis=0)
        for c in range(long // step)
    ]


def make_tail(total, rank):
    lane = lax.broadcasted_iota(jnp.int32, (TAIL, rank), 1)
    high = total.astype(bf16).astype(f32)
    middle = (total - high).astype(bf16).astype(f32)
    low = total - high - middle
    return jnp.where(
        lane == 0, high, jnp.where(lane == 1, middle, jnp.where(lane == 2, low, 0.0))
    ).astype(bf16)


def step_factor(got):
    peers, long, rank = got.shape
    piece = long - TAIL
    lane = lax.broadcasted_iota(jnp.int32, (TAIL, rank), 1)
    row = lax.broadcasted_iota(jnp.int32, (TAIL, rank), 0)
    tail = got[0, piece:, :].astype(f32)
    for j in range(1, peers):
        tail += got[j, piece:, :].astype(f32)
    squares = jnp.sum(jnp.where((row == 0) & (lane < 3), tail, 0.0), keepdims=True)
    return step_rate * jnp.minimum(1.0, clip_norm / jnp.sqrt(squares + 1e-12))


def project_kernel(got_ref, prompts, pay):
    peers, long, rank = pay.shape
    piece = long - TAIL
    blocks = whole_gradient(got_ref, rank)
    tail = make_tail(jnp.sum(sum(b * b for b in blocks), keepdims=True), rank)
    g_down = jnp.concatenate(blocks[:-1], axis=1).astype(bf16)
    proj = dot(prompts[...], g_down, NT).astype(bf16)
    for j in range(peers):
        pay[j, :piece, :] = proj[j * piece : (j + 1) * piece]
        pay[j, piece:, :] = tail


def rows_kernel(got, pa_rows, pay):
    peers, piece, _ = pay.shape
    p_g = got[0, :piece, :].astype(f32)
    for j in range(1, peers):
        p_g += got[j, :piece, :].astype(f32)
    rows = (pa_rows[...].astype(f32) - step_factor(got) * p_g).astype(bf16)
    for j in range(peers):
        pay[j] = rows


def finish_kernel(got, sums, base, base_got, got_g, down_w, up_w, next_down, next_up, keys):
    rank = down_w.shape[1]
    factor = step_factor(sums)
    blocks = whole_gradient(got_g, rank)
    new_up = up_w[...] - factor * blocks[-1]
    next_up[...] = new_up
    keys[...] = (
        base[...]
        + base_got[...].astype(f32)
        + adapter_scale * dot(rejoin(got, 0, got.shape[1]), new_up.astype(bf16))
    ).astype(bf16)
    for c, part in enumerate(blocks[:-1]):
        here = pl.ds(c * rank, rank)
        next_down[here, :] = down_w[here, :] - factor * part.T


def input_kernel(place, near, far, up, down_w, frozen, out, gk):
    rows = out.shape[0]
    lanes = near.shape[1]
    count = near.shape[0] // rows
    for i in range(2 * count):
        ref = near if i < count else far
        block = ref[(i % count) * rows : (i % count + 1) * rows, :]
        owner = place[0] ^ owner_mask(i)
        gk[:, pl.ds(pl.multiple_of(owner * lanes, lanes), lanes)] = block
    a_half = down_w[...].astype(bf16)
    out[...] = (
        dot(gk[...], frozen[...], NT) + adapter_scale * dot(up[...], a_half, NT)
    ).astype(bf16)


def beside_kernel(got, two, other, pa_out, up_out, four):
    count = two.shape[0]
    four[:count, :] = two[...]
    four[count:, :] = other[...]
    peers = got.shape[0]
    piece = pa_out.shape[0]
    up_out[...] = rejoin(got, 0, piece)
    total = got[0, 2 * piece :, :].astype(f32)
    for j in range(1, peers):
        total += got[j, 2 * piece :, :].astype(f32)
    pa_out[...] = total.astype(bf16)


def per_device(acts, output_gradient, lengths, buckets, frozen, down_w, up_w, prompts):
    rows = acts.shape[0]
    width, rank = down_w.shape
    cols = up_w.shape[1]
    n_f = lax.axis_size(FSDP)
    n_near = lax.axis_size(NEAR)
    n_far = lax.axis_size(FAR)
    piece = rows // n_f
    slab = (width + cols) // n_near

    gk, two, pay = call(
        parts_kernel,
        [shape((rows, cols), bf16), shape((2 * rows, cols), bf16), shape((n_f, 2 * piece, rank), bf16)],
        [SMEM, SMEM] + [ANY] * 4,
        (lengths, buckets, acts, output_gradient, down_w, up_w),
        flops=2 * rows * rank * (width + cols),
        out_specs=(HBM, HBM, HBM),
        limit=60,
        scratch_shapes=[
            pltpu.VMEM((rows, width), bf16),
            pltpu.VMEM((rows, cols), bf16),
            pltpu.VMEM((width, rank), f32),
            pltpu.VMEM((rank, cols), f32),
            pltpu.VMEM((rows, cols), bf16),
            pltpu.VMEM((n_f, 2 * piece, rank), bf16),
            pltpu.SemaphoreType.DMA((7,)),
        ],
    )
    got = swap(pay, FSDP)
    other = lax.ppermute(gk, "zlo", Z_PAIRS)
    place = lax.axis_index(FSDP).reshape(1)
    proj, send = call(
        prompts_kernel,
        [shape((rows, rank), bf16), shape((n_f // 2 * rows, cols), bf16)],
        [SMEM] + [VMEM] * 3,
        (place, prompts, frozen, down_w),
        flops=rows * width * (cols * n_f + 2 * rank),
    )
    got, proj, send, other = lax.optimization_barrier((got, proj, send, other))
    (pay,) = call(
        sums_kernel,
        [shape((n_f, 3 * piece, rank), bf16)],
        [VMEM] * 2,
        (got, proj),
        out_specs=(HBM,),
        scratch_shapes=[pltpu.VMEM((n_f, 3 * piece, rank), bf16), pltpu.SemaphoreType.DMA],
    )
    got = swap(pay, FSDP)
    two = lax.dynamic_update_slice(two, other, (rows, 0))
    other = lax.ppermute(two, "x", X_NEAR)
    base_got = lax.ppermute(send, "x", X_FAR)
    got, two = lax.optimization_barrier((got, two))

    (pay,) = call(
        grads_kernel,
        [shape((n_near, slab, rank), bf16)],
        [VMEM] * 3,
        (got, acts, gk),
        flops=2 * rows * rank * (width + cols),
        out_specs=(HBM,),
        scratch_shapes=[pltpu.VMEM((n_near, slab, rank), bf16), pltpu.SemaphoreType.DMA],
    )
    got_g = swap(pay, NEAR)
    pa_rows, up, four = call(
        beside_kernel,
        [
            shape((piece, rank), bf16),
            shape((rows, rank), bf16),
            shape((n_f // 2 * rows, cols), bf16),
        ],
        [VMEM] * 3,
        (got, two, other),
    )
    other = lax.ppermute(four, "x", X_FAR)
    held, send = call(
        own_half_kernel,
        [shape((n_f // 4 * rows, cols), f32), shape((n_f // 4 * rows, cols), bf16)],
        [SMEM] + [VMEM] * 3,
        (place, prompts, frozen, base_got),
        flops=rows * width * cols * n_f,
    )
    got_g, pa_rows, up, held, send = lax.optimization_barrier((got_g, pa_rows, up, held, send))
    base_got = lax.ppermute(send, "x", X_NEAR)
    got = swap(add(got_g, n_far), FAR)
    got_g = swap(add(got, n_near), NEAR)
    (input_gradient,) = call(
        input_kernel,
        [shape((rows, width), bf16)],
        [SMEM] + [VMEM] * 5,
        (place, four, other, up, down_w, frozen),
        flops=2 * rows * width * (cols * n_f + rank),
        scratch_shapes=[pltpu.VMEM((rows, cols * n_f), bf16)],
    )
    base, send = halve(held, base_got)
    base_got = lax.ppermute(send, "zlo", Z_PAIRS)
    got_g, input_gradient, base, base_got = lax.optimization_barrier(
        (got_g, input_gradient, base, base_got)
    )
    (pay,) = call(
        project_kernel,
        [shape((n_f, piece + TAIL, rank), bf16)],
        [VMEM] * 2,
        (got_g, prompts),
        flops=2 * rows * width * rank,
    )
    sums = swap(pay, FSDP)
    (pay,) = call(
        rows_kernel, [shape((n_f, piece, rank), bf16)], [VMEM] * 2, (sums, pa_rows)
    )
    got = swap(pay, FSDP)
    next_down, next_up, keys = call(
        finish_kernel,
        [shape((width, rank), f32), shape((rank, cols), f32), shape((rows, cols), bf16)],
        [VMEM] * 7,
        (got, sums, base, base_got, got_g, down_w, up_w),
        flops=2 * rows * rank * cols,
    )
    return input_gradient, next_down, next_up, keys


def solution(mesh):
    dp, fsdp, section = mesh.devices.shape
    fine = Mesh(mesh.devices.reshape(4, dp // 4, fsdp // 2, 2, section), AXES)
    rows_by_width = P(ROWS, FSDP)
    return jax.shard_map(
        per_device,
        mesh=fine,
        in_specs=(
            rows_by_width,
            rows_by_width,
            P(ROWS),
            P(ROWS),
            P(FSDP, None),
            P(FSDP, None),
            P(None, FSDP),
            rows_by_width,
        ),
        out_specs=(rows_by_width, P(FSDP, None), P(None, FSDP), rows_by_width),
        check_vma=False,
    )
```

```python
import jax
import jax.numpy as jnp
from jax import lax
from jax.experimental import pallas as pl
from jax.experimental.pallas import tpu as pltpu
from jax.sharding import Mesh
from jax.sharding import PartitionSpec as P

adapter_scale = 0.5
step_rate = 16.0
clip_norm = 1.0

AXES = ("zhi", "y", "x", "zlo", "core")
FSDP = ("x", "zlo")
PEERS = ("zlo", "x")
ROWS = ("zhi", "y", "core")
NEAR = ("core", "y")
FAR = "zhi"
TAIL = 16
bf16 = jnp.bfloat16
f32 = jnp.float32

NT = (((1,), (1,)), ((), ()))
TN = (((0,), (0,)), ((), ()))


def dot(a, b, dims=(((1,), (0,)), ((), ()))):
    return lax.dot_general(a, b, dims, preferred_element_type=f32)


Z_PAIRS = ((0, 1), (1, 0))
X_NEAR = ((0, 1), (1, 0), (2, 3), (3, 2))
X_FAR = ((0, 3), (3, 0), (1, 2), (2, 1))


def owner_mask(i):
    return (i & 1) ^ (2 if i & 2 else 0) ^ (6 if i & 4 else 0)


def swap(v, axis):
    return lax.all_to_all(v, axis, 0, 0, tiled=True)


VMEM = None
SMEM = pl.BlockSpec(memory_space=pltpu.SMEM)
ANY = pl.BlockSpec(memory_space=pl.ANY)
HBM = pl.BlockSpec(memory_space=pltpu.HBM)


def block(v):
    zeros = (0,) * len(v.shape)
    return pl.BlockSpec(v.shape, lambda i: zeros)


def call(kernel, outs, ins, args, flops=0, out_specs=None, limit=24, **more):
    moved = sum(a.size * a.dtype.itemsize for a in args) + sum(
        o.size * o.dtype.itemsize for o in outs
    )
    return pl.pallas_call(
        kernel,
        grid=(1,),
        in_specs=[spec or block(a) for spec, a in zip(ins, args, strict=True)],
        out_specs=out_specs or tuple(block(o) for o in outs),
        out_shape=tuple(outs),
        compiler_params=pltpu.CompilerParams(vmem_limit_bytes=limit * 1024 * 1024),
        cost_estimate=pl.CostEstimate(flops=flops, bytes_accessed=moved, transcendentals=0),
        **more,
    )(*args)


def shape(dims, kind):
    return jax.ShapeDtypeStruct(dims, kind)


def parts_kernel(
    lens, buckets, acts, og, down_w, up_w, gk_out, two_out, pay,
    acts_v, og_v, down_v, up_v, gk, parts, sems,
):
    rows = acts.shape[0]
    seqs = lens.shape[0]
    slot = rows // seqs
    peers = pay.shape[0]
    piece = rows // peers
    pairs = ((og, og_v), (up_w, up_v), (down_w, down_v), (acts, acts_v))
    loads = [pltpu.make_async_copy(a, b, sems.at[i]) for i, (a, b) in enumerate(pairs)]
    for c in loads:
        c.start()
    loads[0].wait()
    place = lax.broadcasted_iota(jnp.int32, (slot, 1), 0)
    for s in range(seqs):
        here = pl.ds(s * slot, slot)
        weight = jnp.where(place < lens[s], buckets[s].astype(f32) - 1.5, f32(0.0))
        gk[here, :] = (weight * og_v[here, :].astype(f32)).astype(bf16)
    first = len(pairs)
    stores = [
        pltpu.make_async_copy(gk, gk_out, sems.at[first]),
        pltpu.make_async_copy(gk, two_out.at[pl.ds(0, rows), :], sems.at[first + 1]),
    ]
    for c in stores:
        c.start()

    def put(k, v):
        v = v.astype(bf16)
        for j in range(peers):
            parts[j, k * piece : (k + 1) * piece, :] = v[j * piece : (j + 1) * piece]

    loads[1].wait()
    put(0, dot(gk[...], up_v[...].astype(bf16), NT))
    loads[2].wait()
    a_half = down_v[...].astype(bf16)
    loads[3].wait()
    put(1, dot(acts_v[...], a_half))
    last = pltpu.make_async_copy(parts, pay, sems.at[first + 2])
    last.start()
    for c in stores:
        c.wait()
    last.wait()


def base_part(place, prompts, frozen, i, cols):
    owner = place[0] ^ owner_mask(i)
    return dot(prompts[...], frozen[:, pl.ds(pl.multiple_of(owner * cols, cols), cols)])


def prompts_kernel(place, prompts, frozen, down_w, proj_out, send):
    rows = prompts.shape[0]
    cols = send.shape[1]
    count = send.shape[0] // rows
    for i in range(count):
        send[i * rows : (i + 1) * rows, :] = base_part(
            place, prompts, frozen, count + i, cols
        ).astype(bf16)
    proj_out[...] = dot(prompts[...], down_w[...].astype(bf16)).astype(bf16)


def own_half_kernel(place, prompts, frozen, got, keep, send):
    rows = prompts.shape[0]
    cols = send.shape[1]
    count = send.shape[0] // rows
    for i in range(2 * count):
        part = base_part(place, prompts, frozen, i, cols)
        part += got[i * rows : (i + 1) * rows, :].astype(f32)
        if i < count:
            keep[i * rows : (i + 1) * rows, :] = part
        else:
            send[(i - count) * rows : (i - count + 1) * rows, :] = part.astype(bf16)


def halve_kernel(held, got, keep, send):
    half = keep.shape[0]
    keep[...] = held[:half, :] + got[:half, :].astype(f32)
    send[...] = (held[half:, :] + got[half:, :].astype(f32)).astype(bf16)


def halve(held, got):
    half = held.shape[0] // 2
    dims = (half, held.shape[1])
    return call(halve_kernel, [shape(dims, f32), shape(dims, bf16)], [VMEM] * 2, (held, got))


def sums_kernel(got_ref, proj, pay, pay_v, sem):
    peers, long, _ = pay.shape
    part = got_ref.shape[1]
    piece = long - part
    total = got_ref[0].astype(f32)
    for j in range(1, peers):
        total += got_ref[j].astype(f32)
    total = total.astype(bf16)
    for j in range(peers):
        pay_v[j, :part, :] = total
        pay_v[j, part:, :] = proj[j * piece : (j + 1) * piece, :]
    copy = pltpu.make_async_copy(pay_v, pay, sem)
    copy.start()
    copy.wait()


def rejoin(got_ref, first, piece):
    return jnp.concatenate(
        [got_ref[j, first : first + piece, :] for j in range(got_ref.shape[0])], axis=0
    )


def grads_kernel(got_ref, acts, gk, pay, pay_v, sem):
    rows = acts.shape[0]
    piece = rows // got_ref.shape[0]
    lanes = gk.shape[1]
    up = rejoin(got_ref, 0, piece)
    down = rejoin(got_ref, piece, piece)
    g = adapter_scale * jnp.concatenate([dot(up, acts[...], TN), dot(down, gk[...], TN)], axis=1)
    peers = pay.shape[0]
    step = g.shape[0] // peers
    for j in range(peers):
        pay_v[j] = jnp.concatenate(
            [
                g[j * step : (j + 1) * step, c * lanes : (c + 1) * lanes]
                for c in range(g.shape[1] // lanes)
            ],
            axis=0,
        ).astype(pay.dtype)
    copy = pltpu.make_async_copy(pay_v, pay, sem)
    copy.start()
    copy.wait()


def add_kernel(got_ref, pay, total_v, sems):
    total = got_ref[0].astype(f32)
    for j in range(1, got_ref.shape[0]):
        total += got_ref[j].astype(f32)
    total_v[...] = total.astype(pay.dtype)
    copies = [
        pltpu.make_async_copy(total_v, pay.at[j], sems.at[j]) for j in range(pay.shape[0])
    ]
    for c in copies:
        c.start()
    for c in copies:
        c.wait()


def add(got, peers):
    dims = got.shape[1:]
    (pay,) = call(
        add_kernel,
        [shape((peers,) + dims, bf16)],
        [VMEM],
        (got,),
        out_specs=(HBM,),
        scratch_shapes=[pltpu.VMEM(dims, bf16), pltpu.SemaphoreType.DMA((peers,))],
    )
    return pay


def whole_gradient(got_ref, rank):
    peers, long, _ = got_ref.shape
    step = rank // peers
    got = [got_ref[j].astype(f32) for j in range(peers)]
    return [
        jnp.concatenate([v[c * step : (c + 1) * step] for v in got], axis=0)
        for c in range(long // step)
    ]


def make_tail(total, rank):
    lane = lax.broadcasted_iota(jnp.int32, (TAIL, rank), 1)
    high = total.astype(bf16).astype(f32)
    middle = (total - high).astype(bf16).astype(f32)
    low = total - high - middle
    return jnp.where(
        lane == 0, high, jnp.where(lane == 1, middle, jnp.where(lane == 2, low, 0.0))
    ).astype(bf16)


def step_factor(got):
    peers, long, rank = got.shape
    piece = long - TAIL
    lane = lax.broadcasted_iota(jnp.int32, (TAIL, rank), 1)
    row = lax.broadcasted_iota(jnp.int32, (TAIL, rank), 0)
    tail = got[0, piece:, :].astype(f32)
    for j in range(1, peers):
        tail += got[j, piece:, :].astype(f32)
    squares = jnp.sum(jnp.where((row == 0) & (lane < 3), tail, 0.0), keepdims=True)
    return step_rate * jnp.minimum(1.0, clip_norm / jnp.sqrt(squares + 1e-12))


def project_kernel(got_ref, prompts, pay):
    peers, long, rank = pay.shape
    piece = long - TAIL
    blocks = whole_gradient(got_ref, rank)
    tail = make_tail(jnp.sum(sum(b * b for b in blocks), keepdims=True), rank)
    g_down = jnp.concatenate(blocks[:-1], axis=1).astype(bf16)
    proj = dot(prompts[...], g_down, NT).astype(bf16)
    for j in range(peers):
        pay[j, :piece, :] = proj[j * piece : (j + 1) * piece]
        pay[j, piece:, :] = tail


def rows_kernel(got, pa_rows, pay):
    peers, piece, _ = pay.shape
    p_g = got[0, :piece, :].astype(f32)
    for j in range(1, peers):
        p_g += got[j, :piece, :].astype(f32)
    rows = (pa_rows[...].astype(f32) - step_factor(got) * p_g).astype(bf16)
    for j in range(peers):
        pay[j] = rows


def finish_kernel(got, sums, base, base_got, got_g, down_w, up_w, next_down, next_up, keys):
    rank = down_w.shape[1]
    factor = step_factor(sums)
    blocks = whole_gradient(got_g, rank)
    new_up = up_w[...] - factor * blocks[-1]
    next_up[...] = new_up
    keys[...] = (
        base[...]
        + base_got[...].astype(f32)
        + adapter_scale * dot(rejoin(got, 0, got.shape[1]), new_up.astype(bf16))
    ).astype(bf16)
    for c, part in enumerate(blocks[:-1]):
        here = pl.ds(c * rank, rank)
        next_down[here, :] = down_w[here, :] - factor * part.T


def input_kernel(place, near, far, up, down_w, frozen, out, gk):
    rows = out.shape[0]
    lanes = near.shape[1]
    count = near.shape[0] // rows
    for i in range(2 * count):
        ref = near if i < count else far
        block = ref[(i % count) * rows : (i % count + 1) * rows, :]
        owner = place[0] ^ owner_mask(i)
        gk[:, pl.ds(pl.multiple_of(owner * lanes, lanes), lanes)] = block
    a_half = down_w[...].astype(bf16)
    out[...] = (
        dot(gk[...], frozen[...], NT) + adapter_scale * dot(up[...], a_half, NT)
    ).astype(bf16)


def beside_kernel(got, two, other, pa_out, up_out, four):
    count = two.shape[0]
    four[:count, :] = two[...]
    four[count:, :] = other[...]
    peers = got.shape[0]
    piece = pa_out.shape[0]
    up_out[...] = rejoin(got, 0, piece)
    total = got[0, 2 * piece :, :].astype(f32)
    for j in range(1, peers):
        total += got[j, 2 * piece :, :].astype(f32)
    pa_out[...] = total.astype(bf16)


def per_device(acts, output_gradient, lengths, buckets, frozen, down_w, up_w, prompts):
    rows = acts.shape[0]
    width, rank = down_w.shape
    cols = up_w.shape[1]
    n_f = lax.axis_size(FSDP)
    n_near = lax.axis_size(NEAR)
    n_far = lax.axis_size(FAR)
    piece = rows // n_f
    slab = (width + cols) // n_near

    gk, two, pay = call(
        parts_kernel,
        [shape((rows, cols), bf16), shape((2 * rows, cols), bf16), shape((n_f, 2 * piece, rank), bf16)],
        [SMEM, SMEM] + [ANY] * 4,
        (lengths, buckets, acts, output_gradient, down_w, up_w),
        flops=2 * rows * rank * (width + cols),
        out_specs=(HBM, HBM, HBM),
        limit=60,
        scratch_shapes=[
            pltpu.VMEM((rows, width), bf16),
            pltpu.VMEM((rows, cols), bf16),
            pltpu.VMEM((width, rank), f32),
            pltpu.VMEM((rank, cols), f32),
            pltpu.VMEM((rows, cols), bf16),
            pltpu.VMEM((n_f, 2 * piece, rank), bf16),
            pltpu.SemaphoreType.DMA((7,)),
        ],
    )
    got = swap(pay, PEERS)
    other = lax.ppermute(gk, "zlo", Z_PAIRS)
    place = lax.axis_index(FSDP).reshape(1)
    proj, send = call(
        prompts_kernel,
        [shape((rows, rank), bf16), shape((n_f // 2 * rows, cols), bf16)],
        [SMEM] + [VMEM] * 3,
        (place, prompts, frozen, down_w),
        flops=rows * width * (cols * n_f + 2 * rank),
    )
    got, proj, send, other = lax.optimization_barrier((got, proj, send, other))
    (pay,) = call(
        sums_kernel,
        [shape((n_f, 3 * piece, rank), bf16)],
        [VMEM] * 2,
        (got, proj),
        out_specs=(HBM,),
        scratch_shapes=[pltpu.VMEM((n_f, 3 * piece, rank), bf16), pltpu.SemaphoreType.DMA],
    )
    got = swap(pay, PEERS)
    two = lax.dynamic_update_slice(two, other, (rows, 0))
    other = lax.ppermute(two, "x", X_NEAR)
    base_got = lax.ppermute(send, "x", X_FAR)
    got, two = lax.optimization_barrier((got, two))

    (pay,) = call(
        grads_kernel,
        [shape((n_near, slab, rank), bf16)],
        [VMEM] * 3,
        (got, acts, gk),
        flops=2 * rows * rank * (width + cols),
        out_specs=(HBM,),
        scratch_shapes=[pltpu.VMEM((n_near, slab, rank), bf16), pltpu.SemaphoreType.DMA],
    )
    got_g = swap(pay, NEAR)
    pa_rows, up, four = call(
        beside_kernel,
        [
            shape((piece, rank), bf16),
            shape((rows, rank), bf16),
            shape((n_f // 2 * rows, cols), bf16),
        ],
        [VMEM] * 3,
        (got, two, other),
    )
    other = lax.ppermute(four, "x", X_FAR)
    held, send = call(
        own_half_kernel,
        [shape((n_f // 4 * rows, cols), f32), shape((n_f // 4 * rows, cols), bf16)],
        [SMEM] + [VMEM] * 3,
        (place, prompts, frozen, base_got),
        flops=rows * width * cols * n_f,
    )
    got_g, pa_rows, up, held, send = lax.optimization_barrier((got_g, pa_rows, up, held, send))
    base_got = lax.ppermute(send, "x", X_NEAR)
    got = swap(add(got_g, n_far), FAR)
    got_g = swap(add(got, n_near), NEAR)
    (input_gradient,) = call(
        input_kernel,
        [shape((rows, width), bf16)],
        [SMEM] + [VMEM] * 5,
        (place, four, other, up, down_w, frozen),
        flops=2 * rows * width * (cols * n_f + rank),
        scratch_shapes=[pltpu.VMEM((rows, cols * n_f), bf16)],
    )
    base, send = halve(held, base_got)
    base_got = lax.ppermute(send, "zlo", Z_PAIRS)
    got_g, input_gradient, base, base_got = lax.optimization_barrier(
        (got_g, input_gradient, base, base_got)
    )
    (pay,) = call(
        project_kernel,
        [shape((n_f, piece + TAIL, rank), bf16)],
        [VMEM] * 2,
        (got_g, prompts),
        flops=2 * rows * width * rank,
    )
    sums = swap(pay, PEERS)
    (pay,) = call(
        rows_kernel, [shape((n_f, piece, rank), bf16)], [VMEM] * 2, (sums, pa_rows)
    )
    got = swap(pay, PEERS)
    next_down, next_up, keys = call(
        finish_kernel,
        [shape((width, rank), f32), shape((rank, cols), f32), shape((rows, cols), bf16)],
        [VMEM] * 7,
        (got, sums, base, base_got, got_g, down_w, up_w),
        flops=2 * rows * rank * cols,
    )
    return input_gradient, next_down, next_up, keys


def solution(mesh):
    dp, fsdp, section = mesh.devices.shape
    fine = Mesh(mesh.devices.reshape(4, dp // 4, fsdp // 2, 2, section), AXES)
    rows_by_width = P(ROWS, FSDP)
    return jax.shard_map(
        per_device,
        mesh=fine,
        in_specs=(
            rows_by_width,
            rows_by_width,
            P(ROWS),
            P(ROWS),
            P(FSDP, None),
            P(FSDP, None),
            P(None, FSDP),
            rows_by_width,
        ),
        out_specs=(rows_by_width, P(FSDP, None), P(None, FSDP), rows_by_width),
        check_vma=False,
    )
```

```python
import jax
import jax.numpy as jnp
from jax import lax
from jax.experimental import pallas as pl
from jax.experimental.pallas import tpu as pltpu
from jax.sharding import Mesh
from jax.sharding import PartitionSpec as P

adapter_scale = 0.5
step_rate = 16.0
clip_norm = 1.0

AXES = ("zhi", "y", "x", "zlo", "core")
FSDP = ("x", "zlo")
PEERS = ("zlo", "x")
ROWS = ("zhi", "y", "core")
SUMMED = ("y", "zhi")
TAIL = 16
bf16 = jnp.bfloat16
f32 = jnp.float32

NT = (((1,), (1,)), ((), ()))
TN = (((0,), (0,)), ((), ()))


def dot(a, b, dims=(((1,), (0,)), ((), ()))):
    return lax.dot_general(a, b, dims, preferred_element_type=f32)


CORES = ((0, 1), (1, 0))
Z_PAIRS = ((0, 1), (1, 0))
X_NEAR = ((0, 1), (1, 0), (2, 3), (3, 2))
X_FAR = ((0, 3), (3, 0), (1, 2), (2, 1))


def owner_mask(i):
    return (i & 1) ^ (2 if i & 2 else 0) ^ (6 if i & 4 else 0)


def swap(v, axis):
    return lax.all_to_all(v, axis, 0, 0, tiled=True)


VMEM = None
SMEM = pl.BlockSpec(memory_space=pltpu.SMEM)
ANY = pl.BlockSpec(memory_space=pl.ANY)
HBM = pl.BlockSpec(memory_space=pltpu.HBM)


def block(v):
    zeros = (0,) * len(v.shape)
    return pl.BlockSpec(v.shape, lambda i: zeros)


def call(kernel, outs, ins, args, flops=0, out_specs=None, limit=24, **more):
    moved = sum(a.size * a.dtype.itemsize for a in args) + sum(
        o.size * o.dtype.itemsize for o in outs
    )
    return pl.pallas_call(
        kernel,
        grid=(1,),
        in_specs=[spec or block(a) for spec, a in zip(ins, args, strict=True)],
        out_specs=out_specs or tuple(block(o) for o in outs),
        out_shape=tuple(outs),
        compiler_params=pltpu.CompilerParams(vmem_limit_bytes=limit * 1024 * 1024),
        cost_estimate=pl.CostEstimate(flops=flops, bytes_accessed=moved, transcendentals=0),
        **more,
    )(*args)


def shape(dims, kind):
    return jax.ShapeDtypeStruct(dims, kind)


def parts_kernel(
    lens, buckets, acts, og, down_w, up_w, gk_out, two_out, pay,
    acts_v, og_v, down_v, up_v, gk, parts, sems,
):
    rows = acts.shape[0]
    seqs = lens.shape[0]
    slot = rows // seqs
    peers = pay.shape[0]
    piece = rows // peers
    pairs = ((og, og_v), (up_w, up_v), (down_w, down_v), (acts, acts_v))
    loads = [pltpu.make_async_copy(a, b, sems.at[i]) for i, (a, b) in enumerate(pairs)]
    for c in loads:
        c.start()
    loads[0].wait()
    place = lax.broadcasted_iota(jnp.int32, (slot, 1), 0)
    for s in range(seqs):
        here = pl.ds(s * slot, slot)
        weight = jnp.where(place < lens[s], buckets[s].astype(f32) - 1.5, f32(0.0))
        gk[here, :] = (weight * og_v[here, :].astype(f32)).astype(bf16)
    first = len(pairs)
    stores = [
        pltpu.make_async_copy(gk, gk_out, sems.at[first]),
        pltpu.make_async_copy(gk, two_out.at[pl.ds(0, rows), :], sems.at[first + 1]),
    ]
    for c in stores:
        c.start()

    def put(k, v):
        v = v.astype(bf16)
        for j in range(peers):
            parts[j, k * piece : (k + 1) * piece, :] = v[j * piece : (j + 1) * piece]

    loads[1].wait()
    put(0, dot(gk[...], up_v[...].astype(bf16), NT))
    loads[2].wait()
    a_half = down_v[...].astype(bf16)
    loads[3].wait()
    put(1, dot(acts_v[...], a_half))
    last = pltpu.make_async_copy(parts, pay, sems.at[first + 2])
    last.start()
    for c in stores:
        c.wait()
    last.wait()


def base_part(place, prompts, frozen, i, cols):
    owner = place[0] ^ owner_mask(i)
    return dot(prompts[...], frozen[:, pl.ds(pl.multiple_of(owner * cols, cols), cols)])


def prompts_kernel(place, prompts, frozen, down_w, proj_out, send):
    rows = prompts.shape[0]
    cols = send.shape[1]
    count = send.shape[0] // rows
    for i in range(count):
        send[i * rows : (i + 1) * rows, :] = base_part(
            place, prompts, frozen, count + i, cols
        ).astype(bf16)
    proj_out[...] = dot(prompts[...], down_w[...].astype(bf16)).astype(bf16)


def own_half_kernel(place, prompts, frozen, got, keep, send):
    rows = prompts.shape[0]
    cols = send.shape[1]
    count = send.shape[0] // rows
    for i in range(2 * count):
        part = base_part(place, prompts, frozen, i, cols)
        part += got[i * rows : (i + 1) * rows, :].astype(f32)
        if i < count:
            keep[i * rows : (i + 1) * rows, :] = part
        else:
            send[(i - count) * rows : (i - count + 1) * rows, :] = part.astype(bf16)


def halve_kernel(held, got, keep, send):
    half = keep.shape[0]
    keep[...] = held[:half, :] + got[:half, :].astype(f32)
    send[...] = (held[half:, :] + got[half:, :].astype(f32)).astype(bf16)


def halve(held, got):
    half = held.shape[0] // 2
    dims = (half, held.shape[1])
    return call(halve_kernel, [shape(dims, f32), shape(dims, bf16)], [VMEM] * 2, (held, got))


def sums_kernel(got_ref, proj, pay, pay_v, sem):
    peers, long, _ = pay.shape
    part = got_ref.shape[1]
    piece = long - part
    total = got_ref[0].astype(f32)
    for j in range(1, peers):
        total += got_ref[j].astype(f32)
    total = total.astype(bf16)
    for j in range(peers):
        pay_v[j, :part, :] = total
        pay_v[j, part:, :] = proj[j * piece : (j + 1) * piece, :]
    copy = pltpu.make_async_copy(pay_v, pay, sem)
    copy.start()
    copy.wait()


def rejoin(got_ref, first, piece):
    return jnp.concatenate(
        [got_ref[j, first : first + piece, :] for j in range(got_ref.shape[0])], axis=0
    )


def grads_kernel(got_ref, acts, gk, pay):
    rows = acts.shape[0]
    piece = rows // got_ref.shape[0]
    lanes = gk.shape[1]
    up = rejoin(got_ref, 0, piece)
    down = rejoin(got_ref, piece, piece)
    g = adapter_scale * jnp.concatenate([dot(up, acts[...], TN), dot(down, gk[...], TN)], axis=1)
    peers = pay.shape[0]
    step = g.shape[0] // peers
    for j in range(peers):
        pay[j] = jnp.concatenate(
            [
                g[j * step : (j + 1) * step, c * lanes : (c + 1) * lanes]
                for c in range(g.shape[1] // lanes)
            ],
            axis=0,
        ).astype(pay.dtype)


def add_kernel(got_ref, out):
    total = got_ref[0].astype(f32)
    for j in range(1, got_ref.shape[0]):
        total += got_ref[j].astype(f32)
    out[...] = total


def spread_kernel(mine, got, out, pay, sem):
    total = (mine[...] + got[...]).astype(bf16)
    for j in range(pay.shape[0]):
        pay[j] = total
    copy = pltpu.make_async_copy(pay, out, sem)
    copy.start()
    copy.wait()


def whole_gradient(got_ref, rank):
    peers, long, _ = got_ref.shape
    step = rank // peers
    got = [got_ref[j].astype(f32) for j in range(peers)]
    return [
        jnp.concatenate([v[c * step : (c + 1) * step] for v in got], axis=0)
        for c in range(long // step)
    ]


def make_tail(total, rank):
    lane = lax.broadcasted_iota(jnp.int32, (TAIL, rank), 1)
    high = total.astype(bf16).astype(f32)
    middle = (total - high).astype(bf16).astype(f32)
    low = total - high - middle
    return jnp.where(
        lane == 0, high, jnp.where(lane == 1, middle, jnp.where(lane == 2, low, 0.0))
    ).astype(bf16)


def step_factor(got):
    peers, long, rank = got.shape
    piece = long - TAIL
    lane = lax.broadcasted_iota(jnp.int32, (TAIL, rank), 1)
    row = lax.broadcasted_iota(jnp.int32, (TAIL, rank), 0)
    tail = got[0, piece:, :].astype(f32)
    for j in range(1, peers):
        tail += got[j, piece:, :].astype(f32)
    squares = jnp.sum(jnp.where((row == 0) & (lane < 3), tail, 0.0), keepdims=True)
    return step_rate * jnp.minimum(1.0, clip_norm / jnp.sqrt(squares + 1e-12))


def project_kernel(got_ref, prompts, pay):
    peers, long, rank = pay.shape
    piece = long - TAIL
    blocks = whole_gradient(got_ref, rank)
    tail = make_tail(jnp.sum(sum(b * b for b in blocks), keepdims=True), rank)
    g_down = jnp.concatenate(blocks[:-1], axis=1).astype(bf16)
    proj = dot(prompts[...], g_down, NT).astype(bf16)
    for j in range(peers):
        pay[j, :piece, :] = proj[j * piece : (j + 1) * piece]
        pay[j, piece:, :] = tail


def rows_kernel(got, pa_rows, pay):
    peers, piece, _ = pay.shape
    p_g = got[0, :piece, :].astype(f32)
    for j in range(1, peers):
        p_g += got[j, :piece, :].astype(f32)
    rows = (pa_rows[...].astype(f32) - step_factor(got) * p_g).astype(bf16)
    for j in range(peers):
        pay[j] = rows


def finish_kernel(got, sums, base, base_got, got_g, down_w, up_w, next_down, next_up, keys):
    rank = down_w.shape[1]
    factor = step_factor(sums)
    blocks = whole_gradient(got_g, rank)
    new_up = up_w[...] - factor * blocks[-1]
    next_up[...] = new_up
    keys[...] = (
        base[...]
        + base_got[...].astype(f32)
        + adapter_scale * dot(rejoin(got, 0, got.shape[1]), new_up.astype(bf16))
    ).astype(bf16)
    for c, part in enumerate(blocks[:-1]):
        here = pl.ds(c * rank, rank)
        next_down[here, :] = down_w[here, :] - factor * part.T


def input_kernel(place, near, far, up, down_w, frozen, out, gk):
    rows = out.shape[0]
    lanes = near.shape[1]
    count = near.shape[0] // rows
    for i in range(2 * count):
        ref = near if i < count else far
        block = ref[(i % count) * rows : (i % count + 1) * rows, :]
        owner = place[0] ^ owner_mask(i)
        gk[:, pl.ds(pl.multiple_of(owner * lanes, lanes), lanes)] = block
    a_half = down_w[...].astype(bf16)
    out[...] = (
        dot(gk[...], frozen[...], NT) + adapter_scale * dot(up[...], a_half, NT)
    ).astype(bf16)


def join_kernel(two, other, four):
    count = two.shape[0]
    four[:count, :] = two[...]
    four[count:, :] = other[...]


def beside_kernel(got, pa_out, up_out):
    peers = got.shape[0]
    piece = pa_out.shape[0]
    up_out[...] = rejoin(got, 0, piece)
    total = got[0, 2 * piece :, :].astype(f32)
    for j in range(1, peers):
        total += got[j, 2 * piece :, :].astype(f32)
    pa_out[...] = total.astype(bf16)


def per_device(acts, output_gradient, lengths, buckets, frozen, down_w, up_w, prompts):
    rows = acts.shape[0]
    width, rank = down_w.shape
    cols = up_w.shape[1]
    n_f = lax.axis_size(FSDP)
    n_d = lax.axis_size(SUMMED)
    piece = rows // n_f
    slab = (width + cols) // n_d

    gk, two, pay = call(
        parts_kernel,
        [shape((rows, cols), bf16), shape((2 * rows, cols), bf16), shape((n_f, 2 * piece, rank), bf16)],
        [SMEM, SMEM] + [ANY] * 4,
        (lengths, buckets, acts, output_gradient, down_w, up_w),
        flops=2 * rows * rank * (width + cols),
        out_specs=(HBM, HBM, HBM),
        limit=60,
        scratch_shapes=[
            pltpu.VMEM((rows, width), bf16),
            pltpu.VMEM((rows, cols), bf16),
            pltpu.VMEM((width, rank), f32),
            pltpu.VMEM((rank, cols), f32),
            pltpu.VMEM((rows, cols), bf16),
            pltpu.VMEM((n_f, 2 * piece, rank), bf16),
            pltpu.SemaphoreType.DMA((7,)),
        ],
    )
    got = swap(pay, PEERS)
    other = lax.ppermute(gk, "zlo", Z_PAIRS)
    place = lax.axis_index(FSDP).reshape(1)
    proj, send = call(
        prompts_kernel,
        [shape((rows, rank), bf16), shape((n_f // 2 * rows, cols), bf16)],
        [SMEM] + [VMEM] * 3,
        (place, prompts, frozen, down_w),
        flops=rows * width * (cols * n_f + 2 * rank),
    )
    got, proj, send, other = lax.optimization_barrier((got, proj, send, other))
    (pay,) = call(
        sums_kernel,
        [shape((n_f, 3 * piece, rank), bf16)],
        [VMEM] * 2,
        (got, proj),
        out_specs=(HBM,),
        scratch_shapes=[pltpu.VMEM((n_f, 3 * piece, rank), bf16), pltpu.SemaphoreType.DMA],
    )
    got = swap(pay, PEERS)
    two = lax.dynamic_update_slice(two, other, (rows, 0))
    other = lax.ppermute(two, "x", X_NEAR)
    base_got = lax.ppermute(send, "x", X_FAR)
    got, two = lax.optimization_barrier((got, two))

    (pay,) = call(
        grads_kernel,
        [shape((n_d, slab, rank), bf16)],
        [VMEM] * 3,
        (got, acts, gk),
        flops=2 * rows * rank * (width + cols),
    )
    got_g = swap(pay, SUMMED)
    pa_rows, up = call(
        beside_kernel,
        [shape((piece, rank), bf16), shape((rows, rank), bf16)],
        [VMEM],
        (got,),
    )
    (four,) = call(join_kernel, [shape((n_f // 2 * rows, cols), bf16)], [VMEM] * 2, (two, other))
    far = lax.ppermute(four, "x", X_FAR)
    held, send = call(
        own_half_kernel,
        [shape((n_f // 4 * rows, cols), f32), shape((n_f // 4 * rows, cols), bf16)],
        [SMEM] + [VMEM] * 3,
        (place, prompts, frozen, base_got),
        flops=rows * width * cols * n_f,
    )
    base_got = lax.ppermute(send, "x", X_NEAR)
    got_g, pa_rows, up, held = lax.optimization_barrier((got_g, pa_rows, up, held))
    (mine,) = call(add_kernel, [shape((slab, rank), f32)], [VMEM], (got_g,))
    other = lax.ppermute(mine, "core", CORES)
    dims = (n_d, slab, rank)
    (pay,) = call(
        spread_kernel,
        [shape(dims, bf16)],
        [VMEM] * 2,
        (mine, other),
        out_specs=(HBM,),
        scratch_shapes=[pltpu.VMEM(dims, bf16), pltpu.SemaphoreType.DMA],
    )
    got_g = swap(pay, SUMMED)
    (input_gradient,) = call(
        input_kernel,
        [shape((rows, width), bf16)],
        [SMEM] + [VMEM] * 5,
        (place, four, far, up, down_w, frozen),
        flops=2 * rows * width * (cols * n_f + rank),
        scratch_shapes=[pltpu.VMEM((rows, cols * n_f), bf16)],
    )
    base, send = halve(held, base_got)
    base_got = lax.ppermute(send, "zlo", Z_PAIRS)
    got_g, input_gradient, base, base_got = lax.optimization_barrier(
        (got_g, input_gradient, base, base_got)
    )
    (pay,) = call(
        project_kernel,
        [shape((n_f, piece + TAIL, rank), bf16)],
        [VMEM] * 2,
        (got_g, prompts),
        flops=2 * rows * width * rank,
    )
    sums = swap(pay, PEERS)
    (pay,) = call(
        rows_kernel, [shape((n_f, piece, rank), bf16)], [VMEM] * 2, (sums, pa_rows)
    )
    got = swap(pay, PEERS)
    next_down, next_up, keys = call(
        finish_kernel,
        [shape((width, rank), f32), shape((rank, cols), f32), shape((rows, cols), bf16)],
        [VMEM] * 7,
        (got, sums, base, base_got, got_g, down_w, up_w),
        flops=2 * rows * rank * cols,
    )
    return input_gradient, next_down, next_up, keys


def solution(mesh):
    dp, fsdp, section = mesh.devices.shape
    fine = Mesh(mesh.devices.reshape(4, dp // 4, fsdp // 2, 2, section), AXES)
    rows_by_width = P(ROWS, FSDP)
    return jax.shard_map(
        per_device,
        mesh=fine,
        in_specs=(
            rows_by_width,
            rows_by_width,
            P(ROWS),
            P(ROWS),
            P(FSDP, None),
            P(FSDP, None),
            P(None, FSDP),
            rows_by_width,
        ),
        out_specs=(rows_by_width, P(FSDP, None), P(None, FSDP), rows_by_width),
        check_vma=False,
    )
```

```python
import jax
import jax.numpy as jnp
from jax import lax
from jax.experimental import pallas as pl
from jax.experimental.pallas import tpu as pltpu
from jax.sharding import Mesh
from jax.sharding import PartitionSpec as P

adapter_scale = 0.5
step_rate = 16.0
clip_norm = 1.0

AXES = ("zhi", "y", "x", "zlo", "core")
FSDP = ("x", "zlo")
PEERS = ("zlo", "x")
ROWS = ("zhi", "y", "core")
NEAR = ("core", "y")
FAR = "zhi"
TAIL = 16
bf16 = jnp.bfloat16
f32 = jnp.float32

NT = (((1,), (1,)), ((), ()))
TN = (((0,), (0,)), ((), ()))


def dot(a, b, dims=(((1,), (0,)), ((), ()))):
    return lax.dot_general(a, b, dims, preferred_element_type=f32)


Z_PAIRS = ((0, 1), (1, 0))
X_NEAR = ((0, 1), (1, 0), (2, 3), (3, 2))
X_FAR = ((0, 3), (3, 0), (1, 2), (2, 1))


def owner_mask(i):
    return (i & 1) ^ (2 if i & 2 else 0) ^ (6 if i & 4 else 0)


def swap(v, axis):
    return lax.all_to_all(v, axis, 0, 0, tiled=True)


VMEM = None
SMEM = pl.BlockSpec(memory_space=pltpu.SMEM)
ANY = pl.BlockSpec(memory_space=pl.ANY)
HBM = pl.BlockSpec(memory_space=pltpu.HBM)


def block(v):
    zeros = (0,) * len(v.shape)
    return pl.BlockSpec(v.shape, lambda i: zeros)


def call(kernel, outs, ins, args, flops=0, out_specs=None, limit=24, **more):
    moved = sum(a.size * a.dtype.itemsize for a in args) + sum(
        o.size * o.dtype.itemsize for o in outs
    )
    return pl.pallas_call(
        kernel,
        grid=(1,),
        in_specs=[spec or block(a) for spec, a in zip(ins, args, strict=True)],
        out_specs=out_specs or tuple(block(o) for o in outs),
        out_shape=tuple(outs),
        compiler_params=pltpu.CompilerParams(vmem_limit_bytes=limit * 1024 * 1024),
        cost_estimate=pl.CostEstimate(flops=flops, bytes_accessed=moved, transcendentals=0),
        **more,
    )(*args)


def shape(dims, kind):
    return jax.ShapeDtypeStruct(dims, kind)


def parts_kernel(
    lens, buckets, acts, og, down_w, up_w, gk_out, two_out, pay,
    acts_v, og_v, down_v, up_v, gk, ups, downs, sems,
):
    rows = acts.shape[0]
    seqs = lens.shape[0]
    slot = rows // seqs
    peers = pay.shape[0]
    piece = rows // peers
    half = rows // 2
    pairs = [(og, og_v), (up_w, up_v), (down_w, down_v)] + [
        (acts.at[pl.ds(h * half, half), :], acts_v.at[pl.ds(h * half, half), :]) for h in range(2)
    ]
    loads = [pltpu.make_async_copy(a, b, sems.at[i]) for i, (a, b) in enumerate(pairs)]
    for c in loads:
        c.start()
    loads[0].wait()
    place = lax.broadcasted_iota(jnp.int32, (slot, 1), 0)
    for s in range(seqs):
        here = pl.ds(s * slot, slot)
        weight = jnp.where(place < lens[s], buckets[s].astype(f32) - 1.5, f32(0.0))
        gk[here, :] = (weight * og_v[here, :].astype(f32)).astype(bf16)
    first = len(pairs)
    stores = [
        pltpu.make_async_copy(gk, gk_out, sems.at[first]),
        pltpu.make_async_copy(gk, two_out.at[pl.ds(0, rows), :], sems.at[first + 1]),
    ]
    for c in stores:
        c.start()

    loads[1].wait()
    up = dot(gk[...], up_v[...].astype(bf16), NT).astype(bf16)
    for j in range(peers):
        ups[j] = up[j * piece : (j + 1) * piece]
    stores.append(pltpu.make_async_copy(ups, pay.at[:, pl.ds(0, piece), :], sems.at[first + 2]))
    stores[-1].start()
    loads[2].wait()
    a_half = down_v[...].astype(bf16)
    count = peers // 2
    for h in range(2):
        loads[3 + h].wait()
        down = dot(acts_v[h * half : (h + 1) * half, :], a_half).astype(bf16)
        for j in range(count):
            downs[h * count + j] = down[j * piece : (j + 1) * piece]
        mine = pl.ds(h * count, count)
        stores.append(
            pltpu.make_async_copy(
                downs.at[mine], pay.at[mine, pl.ds(piece, piece), :], sems.at[first + 3 + h]
            )
        )
        stores[-1].start()
    for c in stores:
        c.wait()


def base_part(place, prompts, frozen, i, cols):
    owner = place[0] ^ owner_mask(i)
    return dot(prompts[...], frozen[:, pl.ds(pl.multiple_of(owner * cols, cols), cols)])


def prompts_kernel(place, prompts, frozen, down_w, proj_out, send):
    rows = prompts.shape[0]
    cols = send.shape[1]
    count = send.shape[0] // rows
    for i in range(count):
        send[i * rows : (i + 1) * rows, :] = base_part(
            place, prompts, frozen, count + i, cols
        ).astype(bf16)
    proj_out[...] = dot(prompts[...], down_w[...].astype(bf16)).astype(bf16)


def own_half_kernel(place, prompts, frozen, got, keep, send):
    rows = prompts.shape[0]
    cols = send.shape[1]
    count = send.shape[0] // rows
    for i in range(2 * count):
        part = base_part(place, prompts, frozen, i, cols)
        part += got[i * rows : (i + 1) * rows, :].astype(f32)
        if i < count:
            keep[i * rows : (i + 1) * rows, :] = part
        else:
            send[(i - count) * rows : (i - count + 1) * rows, :] = part.astype(bf16)


def halve_kernel(held, got, keep, send, held_v, got_v, sems):
    loads = [
        pltpu.make_async_copy(held, held_v, sems.at[0]),
        pltpu.make_async_copy(got, got_v, sems.at[1]),
    ]
    for c in loads:
        c.start()
    for c in loads:
        c.wait()
    half = keep.shape[0]
    keep[...] = held_v[:half, :] + got_v[:half, :].astype(f32)
    send[...] = (held_v[half:, :] + got_v[half:, :].astype(f32)).astype(bf16)


def halve(held, got):
    dims = (held.shape[0] // 2, held.shape[1])
    return call(
        halve_kernel,
        [shape(dims, f32), shape(dims, bf16)],
        [HBM] * 2,
        (held, got),
        limit=60,
        scratch_shapes=[
            pltpu.VMEM(held.shape, f32),
            pltpu.VMEM(got.shape, bf16),
            pltpu.SemaphoreType.DMA((2,)),
        ],
    )


def sums_kernel(got_ref, proj, pay, pay_v, sem):
    peers, long, _ = pay.shape
    part = got_ref.shape[1]
    piece = long - part
    total = got_ref[0].astype(f32)
    for j in range(1, peers):
        total += got_ref[j].astype(f32)
    total = total.astype(bf16)
    for j in range(peers):
        pay_v[j, :part, :] = total
        pay_v[j, part:, :] = proj[j * piece : (j + 1) * piece, :]
    copy = pltpu.make_async_copy(pay_v, pay, sem)
    copy.start()
    copy.wait()


def rejoin(got_ref, first, piece):
    return jnp.concatenate(
        [got_ref[j, first : first + piece, :] for j in range(got_ref.shape[0])], axis=0
    )


def grads_kernel(got_ref, acts, gk, pay, pay_v, sem):
    rows = acts.shape[0]
    piece = rows // got_ref.shape[0]
    lanes = gk.shape[1]
    up = rejoin(got_ref, 0, piece)
    down = rejoin(got_ref, piece, piece)
    g = adapter_scale * jnp.concatenate([dot(up, acts[...], TN), dot(down, gk[...], TN)], axis=1)
    peers = pay.shape[0]
    step = g.shape[0] // peers
    for j in range(peers):
        pay_v[j] = jnp.concatenate(
            [
                g[j * step : (j + 1) * step, c * lanes : (c + 1) * lanes]
                for c in range(g.shape[1] // lanes)
            ],
            axis=0,
        ).astype(pay.dtype)
    copy = pltpu.make_async_copy(pay_v, pay, sem)
    copy.start()
    copy.wait()


def add_kernel(got_ref, pay, total_v, sems):
    total = got_ref[0].astype(f32)
    for j in range(1, got_ref.shape[0]):
        total += got_ref[j].astype(f32)
    total_v[...] = total.astype(pay.dtype)
    copies = [
        pltpu.make_async_copy(total_v, pay.at[j], sems.at[j]) for j in range(pay.shape[0])
    ]
    for c in copies:
        c.start()
    for c in copies:
        c.wait()


def add(got, peers):
    dims = got.shape[1:]
    (pay,) = call(
        add_kernel,
        [shape((peers,) + dims, bf16)],
        [VMEM],
        (got,),
        out_specs=(HBM,),
        scratch_shapes=[pltpu.VMEM(dims, bf16), pltpu.SemaphoreType.DMA((peers,))],
    )
    return pay


def whole_gradient(got_ref, rank):
    peers, long, _ = got_ref.shape
    step = rank // peers
    got = [got_ref[j].astype(f32) for j in range(peers)]
    return [
        jnp.concatenate([v[c * step : (c + 1) * step] for v in got], axis=0)
        for c in range(long // step)
    ]


def make_tail(total, rank):
    lane = lax.broadcasted_iota(jnp.int32, (TAIL, rank), 1)
    high = total.astype(bf16).astype(f32)
    middle = (total - high).astype(bf16).astype(f32)
    low = total - high - middle
    return jnp.where(
        lane == 0, high, jnp.where(lane == 1, middle, jnp.where(lane == 2, low, 0.0))
    ).astype(bf16)


def step_factor(got):
    peers, long, rank = got.shape
    piece = long - TAIL
    lane = lax.broadcasted_iota(jnp.int32, (TAIL, rank), 1)
    row = lax.broadcasted_iota(jnp.int32, (TAIL, rank), 0)
    tail = got[0, piece:, :].astype(f32)
    for j in range(1, peers):
        tail += got[j, piece:, :].astype(f32)
    squares = jnp.sum(jnp.where((row == 0) & (lane < 3), tail, 0.0), keepdims=True)
    return step_rate * jnp.minimum(1.0, clip_norm / jnp.sqrt(squares + 1e-12))


def project_kernel(got_ref, prompts, pay):
    peers, long, rank = pay.shape
    piece = long - TAIL
    blocks = whole_gradient(got_ref, rank)
    tail = make_tail(jnp.sum(sum(b * b for b in blocks), keepdims=True), rank)
    g_down = jnp.concatenate(blocks[:-1], axis=1).astype(bf16)
    proj = dot(prompts[...], g_down, NT).astype(bf16)
    for j in range(peers):
        pay[j, :piece, :] = proj[j * piece : (j + 1) * piece]
        pay[j, piece:, :] = tail


def rows_kernel(got, pa_rows, pay):
    peers, piece, _ = pay.shape
    p_g = got[0, :piece, :].astype(f32)
    for j in range(1, peers):
        p_g += got[j, :piece, :].astype(f32)
    rows = (pa_rows[...].astype(f32) - step_factor(got) * p_g).astype(bf16)
    for j in range(peers):
        pay[j] = rows


def finish_kernel(
    got, sums, base, base_got, got_g, down_w, up_w, next_down, next_up, keys,
    down_v, up_v, keys_v, sems,
):
    rank = down_w.shape[1]
    factor = step_factor(sums)
    blocks = whole_gradient(got_g, rank)
    new_up = up_w[...] - factor * blocks[-1]
    up_v[...] = new_up
    copies = [pltpu.make_async_copy(up_v, next_up, sems.at[0])]
    copies[-1].start()
    for c, part in enumerate(blocks[:-1]):
        here = pl.ds(c * rank, rank)
        down_v[here, :] = down_w[here, :] - factor * part.T
        copies.append(pltpu.make_async_copy(down_v.at[here], next_down.at[here], sems.at[2 + c]))
        copies[-1].start()
    keys_v[...] = (
        base[...]
        + base_got[...].astype(f32)
        + adapter_scale * dot(rejoin(got, 0, got.shape[1]), new_up.astype(bf16))
    ).astype(bf16)
    copies.append(pltpu.make_async_copy(keys_v, keys, sems.at[1]))
    copies[-1].start()
    for c in copies:
        c.wait()


def input_kernel(place, near, far, up, down_w, frozen, out, gk):
    rows = out.shape[0]
    lanes = near.shape[1]
    count = near.shape[0] // rows
    for i in range(2 * count):
        ref = near if i < count else far
        block = ref[(i % count) * rows : (i % count + 1) * rows, :]
        owner = place[0] ^ owner_mask(i)
        gk[:, pl.ds(pl.multiple_of(owner * lanes, lanes), lanes)] = block
    a_half = down_w[...].astype(bf16)
    out[...] = (
        dot(gk[...], frozen[...], NT) + adapter_scale * dot(up[...], a_half, NT)
    ).astype(bf16)


def beside_kernel(got, two, other, pa_out, up_out, four):
    count = two.shape[0]
    four[:count, :] = two[...]
    four[count:, :] = other[...]
    peers = got.shape[0]
    piece = pa_out.shape[0]
    up_out[...] = rejoin(got, 0, piece)
    total = got[0, 2 * piece :, :].astype(f32)
    for j in range(1, peers):
        total += got[j, 2 * piece :, :].astype(f32)
    pa_out[...] = total.astype(bf16)


def per_device(acts, output_gradient, lengths, buckets, frozen, down_w, up_w, prompts):
    rows = acts.shape[0]
    width, rank = down_w.shape
    cols = up_w.shape[1]
    n_f = lax.axis_size(FSDP)
    n_near = lax.axis_size(NEAR)
    n_far = lax.axis_size(FAR)
    piece = rows // n_f
    slab = (width + cols) // n_near

    gk, two, pay = call(
        parts_kernel,
        [shape((rows, cols), bf16), shape((2 * rows, cols), bf16), shape((n_f, 2 * piece, rank), bf16)],
        [SMEM, SMEM] + [ANY] * 4,
        (lengths, buckets, acts, output_gradient, down_w, up_w),
        flops=2 * rows * rank * (width + cols),
        out_specs=(HBM, HBM, HBM),
        limit=60,
        scratch_shapes=[
            pltpu.VMEM((rows, width), bf16),
            pltpu.VMEM((rows, cols), bf16),
            pltpu.VMEM((width, rank), f32),
            pltpu.VMEM((rank, cols), f32),
            pltpu.VMEM((rows, cols), bf16),
            pltpu.VMEM((n_f, piece, rank), bf16),
            pltpu.VMEM((n_f, piece, rank), bf16),
            pltpu.SemaphoreType.DMA((10,)),
        ],
    )
    got = swap(pay, PEERS)
    other = lax.ppermute(gk, "zlo", Z_PAIRS)
    place = lax.axis_index(FSDP).reshape(1)
    proj, send = call(
        prompts_kernel,
        [shape((rows, rank), bf16), shape((n_f // 2 * rows, cols), bf16)],
        [SMEM] + [VMEM] * 3,
        (place, prompts, frozen, down_w),
        flops=rows * width * (cols * n_f + 2 * rank),
    )
    got, proj, send, other = lax.optimization_barrier((got, proj, send, other))
    (pay,) = call(
        sums_kernel,
        [shape((n_f, 3 * piece, rank), bf16)],
        [VMEM] * 2,
        (got, proj),
        out_specs=(HBM,),
        scratch_shapes=[pltpu.VMEM((n_f, 3 * piece, rank), bf16), pltpu.SemaphoreType.DMA],
    )
    got = swap(pay, PEERS)
    two = lax.dynamic_update_slice(two, other, (rows, 0))
    other = lax.ppermute(two, "x", X_NEAR)
    _, send = lax.optimization_barrier((two, send))
    base_got = lax.ppermute(send, "x", X_FAR)
    got, two = lax.optimization_barrier((got, two))

    (pay,) = call(
        grads_kernel,
        [shape((n_near, slab, rank), bf16)],
        [VMEM] * 3,
        (got, acts, gk),
        flops=2 * rows * rank * (width + cols),
        out_specs=(HBM,),
        scratch_shapes=[pltpu.VMEM((n_near, slab, rank), bf16), pltpu.SemaphoreType.DMA],
    )
    got_g = swap(pay, NEAR)
    pa_rows, up, four = call(
        beside_kernel,
        [
            shape((piece, rank), bf16),
            shape((rows, rank), bf16),
            shape((n_f // 2 * rows, cols), bf16),
        ],
        [VMEM] * 3,
        (got, two, other),
    )
    other = lax.ppermute(four, "x", X_FAR)
    held, send = call(
        own_half_kernel,
        [shape((n_f // 4 * rows, cols), f32), shape((n_f // 4 * rows, cols), bf16)],
        [SMEM] + [VMEM] * 3,
        (place, prompts, frozen, base_got),
        flops=rows * width * cols * n_f,
    )
    got_g, pa_rows, up, held, send = lax.optimization_barrier((got_g, pa_rows, up, held, send))
    base_got = lax.ppermute(send, "x", X_NEAR)
    got = swap(add(got_g, n_far), FAR)
    got_g = swap(add(got, n_near), NEAR)
    (input_gradient,) = call(
        input_kernel,
        [shape((rows, width), bf16)],
        [SMEM] + [VMEM] * 5,
        (place, four, other, up, down_w, frozen),
        flops=2 * rows * width * (cols * n_f + rank),
        scratch_shapes=[pltpu.VMEM((rows, cols * n_f), bf16)],
    )
    base, send = halve(held, base_got)
    base_got = lax.ppermute(send, "zlo", Z_PAIRS)
    got_g, input_gradient, base, base_got = lax.optimization_barrier(
        (got_g, input_gradient, base, base_got)
    )
    (pay,) = call(
        project_kernel,
        [shape((n_f, piece + TAIL, rank), bf16)],
        [VMEM] * 2,
        (got_g, prompts),
        flops=2 * rows * width * rank,
    )
    sums = swap(pay, PEERS)
    (pay,) = call(
        rows_kernel, [shape((n_f, piece, rank), bf16)], [VMEM] * 2, (sums, pa_rows)
    )
    got = swap(pay, PEERS)
    next_down, next_up, keys = call(
        finish_kernel,
        [shape((width, rank), f32), shape((rank, cols), f32), shape((rows, cols), bf16)],
        [VMEM] * 7,
        (got, sums, base, base_got, got_g, down_w, up_w),
        flops=2 * rows * rank * cols,
        out_specs=(HBM, HBM, HBM),
        scratch_shapes=[
            pltpu.VMEM((width, rank), f32),
            pltpu.VMEM((rank, cols), f32),
            pltpu.VMEM((rows, cols), bf16),
            pltpu.SemaphoreType.DMA((2 + width // rank,)),
        ],
    )
    return input_gradient, next_down, next_up, keys


def solution(mesh):
    dp, fsdp, section = mesh.devices.shape
    fine = Mesh(mesh.devices.reshape(4, dp // 4, fsdp // 2, 2, section), AXES)
    rows_by_width = P(ROWS, FSDP)
    return jax.shard_map(
        per_device,
        mesh=fine,
        in_specs=(
            rows_by_width,
            rows_by_width,
            P(ROWS),
            P(ROWS),
            P(FSDP, None),
            P(FSDP, None),
            P(None, FSDP),
            rows_by_width,
        ),
        out_specs=(rows_by_width, P(FSDP, None), P(None, FSDP), rows_by_width),
        check_vma=False,
    )
```

```python
import jax
import jax.numpy as jnp
from jax import lax
from jax.experimental import pallas as pl
from jax.experimental.pallas import tpu as pltpu
from jax.sharding import Mesh
from jax.sharding import PartitionSpec as P

adapter_scale = 0.5
step_rate = 16.0
clip_norm = 1.0

AXES = ("zhi", "y", "x", "zlo", "core")
FSDP = ("x", "zlo")
PEERS = ("zlo", "x")
ROWS = ("zhi", "y", "core")
NEAR = ("core", "y")
FAR = "zhi"
TAIL = 16
bf16 = jnp.bfloat16
f32 = jnp.float32

NT = (((1,), (1,)), ((), ()))
TN = (((0,), (0,)), ((), ()))


def dot(a, b, dims=(((1,), (0,)), ((), ()))):
    return lax.dot_general(a, b, dims, preferred_element_type=f32)


Z_PAIRS = ((0, 1), (1, 0))
X_NEAR = ((0, 1), (1, 0), (2, 3), (3, 2))
X_FAR = ((0, 3), (3, 0), (1, 2), (2, 1))


def owner_mask(i):
    return (i & 1) ^ (6 if i & 2 else 0) ^ (2 if i & 4 else 0)


def swap(v, axis):
    return lax.all_to_all(v, axis, 0, 0, tiled=True)


VMEM = None
SMEM = pl.BlockSpec(memory_space=pltpu.SMEM)
ANY = pl.BlockSpec(memory_space=pl.ANY)
HBM = pl.BlockSpec(memory_space=pltpu.HBM)


def block(v):
    zeros = (0,) * len(v.shape)
    return pl.BlockSpec(v.shape, lambda i: zeros)


def call(kernel, outs, ins, args, flops=0, out_specs=None, limit=24, **more):
    moved = sum(a.size * a.dtype.itemsize for a in args) + sum(
        o.size * o.dtype.itemsize for o in outs
    )
    return pl.pallas_call(
        kernel,
        grid=(1,),
        in_specs=[spec or block(a) for spec, a in zip(ins, args, strict=True)],
        out_specs=out_specs or tuple(block(o) for o in outs),
        out_shape=tuple(outs),
        compiler_params=pltpu.CompilerParams(vmem_limit_bytes=limit * 1024 * 1024),
        cost_estimate=pl.CostEstimate(flops=flops, bytes_accessed=moved, transcendentals=0),
        **more,
    )(*args)


def shape(dims, kind):
    return jax.ShapeDtypeStruct(dims, kind)


def parts_kernel(
    lens, buckets, acts, og, down_w, up_w, gk_out, two_out, pay,
    acts_v, og_v, down_v, up_v, gk, ups, downs, sems,
):
    rows = acts.shape[0]
    seqs = lens.shape[0]
    slot = rows // seqs
    peers = pay.shape[0]
    piece = rows // peers
    half = rows // 2
    pairs = [(og, og_v), (up_w, up_v), (down_w, down_v)] + [
        (acts.at[pl.ds(h * half, half), :], acts_v.at[pl.ds(h * half, half), :]) for h in range(2)
    ]
    loads = [pltpu.make_async_copy(a, b, sems.at[i]) for i, (a, b) in enumerate(pairs)]
    for c in loads:
        c.start()
    loads[0].wait()
    place = lax.broadcasted_iota(jnp.int32, (slot, 1), 0)
    for s in range(seqs):
        here = pl.ds(s * slot, slot)
        weight = jnp.where(place < lens[s], buckets[s].astype(f32) - 1.5, f32(0.0))
        gk[here, :] = (weight * og_v[here, :].astype(f32)).astype(bf16)
    first = len(pairs)
    stores = [
        pltpu.make_async_copy(gk, gk_out, sems.at[first]),
        pltpu.make_async_copy(gk, two_out.at[pl.ds(0, rows), :], sems.at[first + 1]),
    ]
    for c in stores:
        c.start()

    loads[1].wait()
    up = dot(gk[...], up_v[...].astype(bf16), NT).astype(bf16)
    for j in range(peers):
        ups[j] = up[j * piece : (j + 1) * piece]
    stores.append(pltpu.make_async_copy(ups, pay.at[:, pl.ds(0, piece), :], sems.at[first + 2]))
    stores[-1].start()
    loads[2].wait()
    a_half = down_v[...].astype(bf16)
    count = peers // 2
    for h in range(2):
        loads[3 + h].wait()
        down = dot(acts_v[h * half : (h + 1) * half, :], a_half).astype(bf16)
        for j in range(count):
            downs[h * count + j] = down[j * piece : (j + 1) * piece]
        mine = pl.ds(h * count, count)
        stores.append(
            pltpu.make_async_copy(
                downs.at[mine], pay.at[mine, pl.ds(piece, piece), :], sems.at[first + 3 + h]
            )
        )
        stores[-1].start()
    for c in stores:
        c.wait()


def base_part(place, prompts, frozen, i, cols):
    owner = place[0] ^ owner_mask(i)
    return dot(prompts[...], frozen[:, pl.ds(pl.multiple_of(owner * cols, cols), cols)])


def prompts_kernel(place, prompts, frozen, down_w, proj_out, send):
    rows = prompts.shape[0]
    cols = send.shape[1]
    count = send.shape[0] // rows
    for i in range(count):
        send[i * rows : (i + 1) * rows, :] = base_part(
            place, prompts, frozen, count + i, cols
        ).astype(bf16)
    proj_out[...] = dot(prompts[...], down_w[...].astype(bf16)).astype(bf16)


def own_half_kernel(place, prompts, frozen, got, keep, send):
    rows = prompts.shape[0]
    cols = send.shape[1]
    count = send.shape[0] // rows
    for i in range(2 * count):
        part = base_part(place, prompts, frozen, i, cols)
        part += got[i * rows : (i + 1) * rows, :].astype(f32)
        if i < count:
            keep[i * rows : (i + 1) * rows, :] = part
        else:
            send[(i - count) * rows : (i - count + 1) * rows, :] = part.astype(bf16)


def halve_kernel(held, got, keep, send, held_v, got_v, sems):
    loads = [
        pltpu.make_async_copy(held, held_v, sems.at[0]),
        pltpu.make_async_copy(got, got_v, sems.at[1]),
    ]
    for c in loads:
        c.start()
    for c in loads:
        c.wait()
    half = keep.shape[0]
    keep[...] = held_v[:half, :] + got_v[:half, :].astype(f32)
    send[...] = (held_v[half:, :] + got_v[half:, :].astype(f32)).astype(bf16)


def halve(held, got):
    dims = (held.shape[0] // 2, held.shape[1])
    return call(
        halve_kernel,
        [shape(dims, f32), shape(dims, bf16)],
        [HBM] * 2,
        (held, got),
        limit=60,
        scratch_shapes=[
            pltpu.VMEM(held.shape, f32),
            pltpu.VMEM(got.shape, bf16),
            pltpu.SemaphoreType.DMA((2,)),
        ],
    )


def sums_kernel(got_ref, proj, pay, pay_v, sem):
    peers, long, _ = pay.shape
    part = got_ref.shape[1]
    piece = long - part
    total = got_ref[0].astype(f32)
    for j in range(1, peers):
        total += got_ref[j].astype(f32)
    total = total.astype(bf16)
    for j in range(peers):
        pay_v[j, :part, :] = total
        pay_v[j, part:, :] = proj[j * piece : (j + 1) * piece, :]
    copy = pltpu.make_async_copy(pay_v, pay, sem)
    copy.start()
    copy.wait()


def rejoin(got_ref, first, piece):
    return jnp.concatenate(
        [got_ref[j, first : first + piece, :] for j in range(got_ref.shape[0])], axis=0
    )


def grads_kernel(got_ref, acts, gk, pay, pay_v, sem):
    rows = acts.shape[0]
    piece = rows // got_ref.shape[0]
    lanes = gk.shape[1]
    up = rejoin(got_ref, 0, piece)
    down = rejoin(got_ref, piece, piece)
    g = adapter_scale * jnp.concatenate([dot(up, acts[...], TN), dot(down, gk[...], TN)], axis=1)
    peers = pay.shape[0]
    step = g.shape[0] // peers
    for j in range(peers):
        pay_v[j] = jnp.concatenate(
            [
                g[j * step : (j + 1) * step, c * lanes : (c + 1) * lanes]
                for c in range(g.shape[1] // lanes)
            ],
            axis=0,
        ).astype(pay.dtype)
    copy = pltpu.make_async_copy(pay_v, pay, sem)
    copy.start()
    copy.wait()


def add_kernel(got_ref, pay, total_v, sems):
    total = got_ref[0].astype(f32)
    for j in range(1, got_ref.shape[0]):
        total += got_ref[j].astype(f32)
    total_v[...] = total.astype(pay.dtype)
    copies = [
        pltpu.make_async_copy(total_v, pay.at[j], sems.at[j]) for j in range(pay.shape[0])
    ]
    for c in copies:
        c.start()
    for c in copies:
        c.wait()


def add(got, peers):
    dims = got.shape[1:]
    (pay,) = call(
        add_kernel,
        [shape((peers,) + dims, bf16)],
        [VMEM],
        (got,),
        out_specs=(HBM,),
        scratch_shapes=[pltpu.VMEM(dims, bf16), pltpu.SemaphoreType.DMA((peers,))],
    )
    return pay


def whole_gradient(got_ref, rank):
    peers, long, _ = got_ref.shape
    step = rank // peers
    got = [got_ref[j].astype(f32) for j in range(peers)]
    return [
        jnp.concatenate([v[c * step : (c + 1) * step] for v in got], axis=0)
        for c in range(long // step)
    ]


def make_tail(total, rank):
    lane = lax.broadcasted_iota(jnp.int32, (TAIL, rank), 1)
    high = total.astype(bf16).astype(f32)
    middle = (total - high).astype(bf16).astype(f32)
    low = total - high - middle
    return jnp.where(
        lane == 0, high, jnp.where(lane == 1, middle, jnp.where(lane == 2, low, 0.0))
    ).astype(bf16)


def step_factor(got):
    peers, long, rank = got.shape
    piece = long - TAIL
    lane = lax.broadcasted_iota(jnp.int32, (TAIL, rank), 1)
    row = lax.broadcasted_iota(jnp.int32, (TAIL, rank), 0)
    tail = got[0, piece:, :].astype(f32)
    for j in range(1, peers):
        tail += got[j, piece:, :].astype(f32)
    squares = jnp.sum(jnp.where((row == 0) & (lane < 3), tail, 0.0), keepdims=True)
    return step_rate * jnp.minimum(1.0, clip_norm / jnp.sqrt(squares + 1e-12))


def project_kernel(got_ref, prompts, pay):
    peers, long, rank = pay.shape
    piece = long - TAIL
    blocks = whole_gradient(got_ref, rank)
    tail = make_tail(jnp.sum(sum(b * b for b in blocks), keepdims=True), rank)
    g_down = jnp.concatenate(blocks[:-1], axis=1).astype(bf16)
    proj = dot(prompts[...], g_down, NT).astype(bf16)
    for j in range(peers):
        pay[j, :piece, :] = proj[j * piece : (j + 1) * piece]
        pay[j, piece:, :] = tail


def rows_kernel(got, pa_rows, pay):
    peers, piece, _ = pay.shape
    p_g = got[0, :piece, :].astype(f32)
    for j in range(1, peers):
        p_g += got[j, :piece, :].astype(f32)
    rows = (pa_rows[...].astype(f32) - step_factor(got) * p_g).astype(bf16)
    for j in range(peers):
        pay[j] = rows


def finish_kernel(
    got, sums, base, base_got, got_g, down_w, up_w, next_down, next_up, keys,
    down_v, up_v, keys_v, sems,
):
    rank = down_w.shape[1]
    factor = step_factor(sums)
    blocks = whole_gradient(got_g, rank)
    new_up = up_w[...] - factor * blocks[-1]
    up_v[...] = new_up
    copies = [pltpu.make_async_copy(up_v, next_up, sems.at[0])]
    copies[-1].start()
    for c, part in enumerate(blocks[:-1]):
        here = pl.ds(c * rank, rank)
        down_v[here, :] = down_w[here, :] - factor * part.T
        copies.append(pltpu.make_async_copy(down_v.at[here], next_down.at[here], sems.at[2 + c]))
        copies[-1].start()
    keys_v[...] = (
        base[...]
        + base_got[...].astype(f32)
        + adapter_scale * dot(rejoin(got, 0, got.shape[1]), new_up.astype(bf16))
    ).astype(bf16)
    copies.append(pltpu.make_async_copy(keys_v, keys, sems.at[1]))
    copies[-1].start()
    for c in copies:
        c.wait()


def input_kernel(place, near, far, up, down_w, frozen, out, gk):
    rows = out.shape[0]
    lanes = near.shape[1]
    count = near.shape[0] // rows
    for i in range(2 * count):
        ref = near if i < count else far
        block = ref[(i % count) * rows : (i % count + 1) * rows, :]
        owner = place[0] ^ owner_mask(i)
        gk[:, pl.ds(pl.multiple_of(owner * lanes, lanes), lanes)] = block
    a_half = down_w[...].astype(bf16)
    out[...] = (
        dot(gk[...], frozen[...], NT) + adapter_scale * dot(up[...], a_half, NT)
    ).astype(bf16)


def beside_kernel(got, two, other, pa_out, up_out, four):
    count = two.shape[0]
    four[:count, :] = two[...]
    four[count:, :] = other[...]
    peers = got.shape[0]
    piece = pa_out.shape[0]
    up_out[...] = rejoin(got, 0, piece)
    total = got[0, 2 * piece :, :].astype(f32)
    for j in range(1, peers):
        total += got[j, 2 * piece :, :].astype(f32)
    pa_out[...] = total.astype(bf16)


def per_device(acts, output_gradient, lengths, buckets, frozen, down_w, up_w, prompts):
    rows = acts.shape[0]
    width, rank = down_w.shape
    cols = up_w.shape[1]
    n_f = lax.axis_size(FSDP)
    n_near = lax.axis_size(NEAR)
    n_far = lax.axis_size(FAR)
    piece = rows // n_f
    slab = (width + cols) // n_near

    gk, two, pay = call(
        parts_kernel,
        [shape((rows, cols), bf16), shape((2 * rows, cols), bf16), shape((n_f, 2 * piece, rank), bf16)],
        [SMEM, SMEM] + [ANY] * 4,
        (lengths, buckets, acts, output_gradient, down_w, up_w),
        flops=2 * rows * rank * (width + cols),
        out_specs=(HBM, HBM, HBM),
        limit=60,
        scratch_shapes=[
            pltpu.VMEM((rows, width), bf16),
            pltpu.VMEM((rows, cols), bf16),
            pltpu.VMEM((width, rank), f32),
            pltpu.VMEM((rank, cols), f32),
            pltpu.VMEM((rows, cols), bf16),
            pltpu.VMEM((n_f, piece, rank), bf16),
            pltpu.VMEM((n_f, piece, rank), bf16),
            pltpu.SemaphoreType.DMA((10,)),
        ],
    )
    got = swap(pay, PEERS)
    other = lax.ppermute(gk, "zlo", Z_PAIRS)
    place = lax.axis_index(FSDP).reshape(1)
    proj, send = call(
        prompts_kernel,
        [shape((rows, rank), bf16), shape((n_f // 2 * rows, cols), bf16)],
        [SMEM] + [VMEM] * 3,
        (place, prompts, frozen, down_w),
        flops=rows * width * (cols * n_f + 2 * rank),
    )
    got, proj, send, other = lax.optimization_barrier((got, proj, send, other))
    (pay,) = call(
        sums_kernel,
        [shape((n_f, 3 * piece, rank), bf16)],
        [VMEM] * 2,
        (got, proj),
        out_specs=(HBM,),
        scratch_shapes=[pltpu.VMEM((n_f, 3 * piece, rank), bf16), pltpu.SemaphoreType.DMA],
    )
    got = swap(pay, PEERS)
    two = lax.dynamic_update_slice(two, other, (rows, 0))
    other = lax.ppermute(two, "x", X_FAR)
    _, send = lax.optimization_barrier((two, send))
    base_got = lax.ppermute(send, "x", X_NEAR)
    got, two = lax.optimization_barrier((got, two))

    (pay,) = call(
        grads_kernel,
        [shape((n_near, slab, rank), bf16)],
        [VMEM] * 3,
        (got, acts, gk),
        flops=2 * rows * rank * (width + cols),
        out_specs=(HBM,),
        scratch_shapes=[pltpu.VMEM((n_near, slab, rank), bf16), pltpu.SemaphoreType.DMA],
    )
    got_g = swap(pay, NEAR)
    pa_rows, up, four = call(
        beside_kernel,
        [
            shape((piece, rank), bf16),
            shape((rows, rank), bf16),
            shape((n_f // 2 * rows, cols), bf16),
        ],
        [VMEM] * 3,
        (got, two, other),
    )
    other = lax.ppermute(four, "x", X_NEAR)
    held, send = call(
        own_half_kernel,
        [shape((n_f // 4 * rows, cols), f32), shape((n_f // 4 * rows, cols), bf16)],
        [SMEM] + [VMEM] * 3,
        (place, prompts, frozen, base_got),
        flops=rows * width * cols * n_f,
    )
    got_g, pa_rows, up, held, send = lax.optimization_barrier((got_g, pa_rows, up, held, send))
    base_got = lax.ppermute(send, "x", X_FAR)
    got = swap(add(got_g, n_far), FAR)
    got_g = swap(add(got, n_near), NEAR)
    (input_gradient,) = call(
        input_kernel,
        [shape((rows, width), bf16)],
        [SMEM] + [VMEM] * 5,
        (place, four, other, up, down_w, frozen),
        flops=2 * rows * width * (cols * n_f + rank),
        scratch_shapes=[pltpu.VMEM((rows, cols * n_f), bf16)],
    )
    base, send = halve(held, base_got)
    base_got = lax.ppermute(send, "zlo", Z_PAIRS)
    got_g, input_gradient, base, base_got = lax.optimization_barrier(
        (got_g, input_gradient, base, base_got)
    )
    (pay,) = call(
        project_kernel,
        [shape((n_f, piece + TAIL, rank), bf16)],
        [VMEM] * 2,
        (got_g, prompts),
        flops=2 * rows * width * rank,
    )
    sums = swap(pay, PEERS)
    (pay,) = call(
        rows_kernel, [shape((n_f, piece, rank), bf16)], [VMEM] * 2, (sums, pa_rows)
    )
    got = swap(pay, PEERS)
    next_down, next_up, keys = call(
        finish_kernel,
        [shape((width, rank), f32), shape((rank, cols), f32), shape((rows, cols), bf16)],
        [VMEM] * 7,
        (got, sums, base, base_got, got_g, down_w, up_w),
        flops=2 * rows * rank * cols,
        out_specs=(HBM, HBM, HBM),
        scratch_shapes=[
            pltpu.VMEM((width, rank), f32),
            pltpu.VMEM((rank, cols), f32),
            pltpu.VMEM((rows, cols), bf16),
            pltpu.SemaphoreType.DMA((2 + width // rank,)),
        ],
    )
    return input_gradient, next_down, next_up, keys


def solution(mesh):
    dp, fsdp, section = mesh.devices.shape
    fine = Mesh(mesh.devices.reshape(4, dp // 4, fsdp // 2, 2, section), AXES)
    rows_by_width = P(ROWS, FSDP)
    return jax.shard_map(
        per_device,
        mesh=fine,
        in_specs=(
            rows_by_width,
            rows_by_width,
            P(ROWS),
            P(ROWS),
            P(FSDP, None),
            P(FSDP, None),
            P(None, FSDP),
            rows_by_width,
        ),
        out_specs=(rows_by_width, P(FSDP, None), P(None, FSDP), rows_by_width),
        check_vma=False,
    )
```

```python
import jax
import jax.numpy as jnp
from jax import lax
from jax.experimental import pallas as pl
from jax.experimental.pallas import tpu as pltpu
from jax.sharding import Mesh
from jax.sharding import PartitionSpec as P

adapter_scale = 0.5
step_rate = 16.0
clip_norm = 1.0

AXES = ("zhi", "y", "x", "zlo", "core")
FSDP = ("x", "zlo")
PEERS = ("zlo", "x")
ROWS = ("zhi", "y", "core")
NEAR = ("core", "y")
FAR = "zhi"
TAIL = 16
bf16 = jnp.bfloat16
f32 = jnp.float32

NT = (((1,), (1,)), ((), ()))
TN = (((0,), (0,)), ((), ()))


def dot(a, b, dims=(((1,), (0,)), ((), ()))):
    return lax.dot_general(a, b, dims, preferred_element_type=f32)


Z_PAIRS = ((0, 1), (1, 0))
X_NEAR = ((0, 1), (1, 0), (2, 3), (3, 2))
X_FAR = ((0, 3), (3, 0), (1, 2), (2, 1))


def owner_mask(i):
    return (i & 1) ^ (6 if i & 2 else 0) ^ (2 if i & 4 else 0)


def swap(v, axis):
    return lax.all_to_all(v, axis, 0, 0, tiled=True)


VMEM = None
SMEM = pl.BlockSpec(memory_space=pltpu.SMEM)
ANY = pl.BlockSpec(memory_space=pl.ANY)
HBM = pl.BlockSpec(memory_space=pltpu.HBM)


def block(v):
    zeros = (0,) * len(v.shape)
    return pl.BlockSpec(v.shape, lambda i: zeros)


def call(kernel, outs, ins, args, flops=0, out_specs=None, limit=24, **more):
    moved = sum(a.size * a.dtype.itemsize for a in args) + sum(
        o.size * o.dtype.itemsize for o in outs
    )
    return pl.pallas_call(
        kernel,
        grid=(1,),
        in_specs=[spec or block(a) for spec, a in zip(ins, args, strict=True)],
        out_specs=out_specs or tuple(block(o) for o in outs),
        out_shape=tuple(outs),
        compiler_params=pltpu.CompilerParams(vmem_limit_bytes=limit * 1024 * 1024),
        cost_estimate=pl.CostEstimate(flops=flops, bytes_accessed=moved, transcendentals=0),
        **more,
    )(*args)


def shape(dims, kind):
    return jax.ShapeDtypeStruct(dims, kind)


def parts_kernel(
    lens, buckets, acts, og, down_w, up_w, gk_out, two_out, pay,
    acts_v, og_v, down_v, up_v, gk, ups, downs, sems,
):
    rows = acts.shape[0]
    seqs = lens.shape[0]
    slot = rows // seqs
    peers = pay.shape[0]
    piece = rows // peers
    half = rows // 2
    pairs = [(og, og_v), (up_w, up_v), (down_w, down_v)] + [
        (acts.at[pl.ds(h * half, half), :], acts_v.at[pl.ds(h * half, half), :]) for h in range(2)
    ]
    loads = [pltpu.make_async_copy(a, b, sems.at[i]) for i, (a, b) in enumerate(pairs)]
    for c in loads:
        c.start()
    loads[0].wait()
    place = lax.broadcasted_iota(jnp.int32, (slot, 1), 0)
    for s in range(seqs):
        here = pl.ds(s * slot, slot)
        weight = jnp.where(place < lens[s], buckets[s].astype(f32) - 1.5, f32(0.0))
        gk[here, :] = (weight * og_v[here, :].astype(f32)).astype(bf16)
    first = len(pairs)
    stores = [
        pltpu.make_async_copy(gk, gk_out, sems.at[first]),
        pltpu.make_async_copy(gk, two_out.at[pl.ds(0, rows), :], sems.at[first + 1]),
    ]
    for c in stores:
        c.start()

    loads[1].wait()
    up = dot(gk[...], up_v[...].astype(bf16), NT).astype(bf16)
    for j in range(peers):
        ups[j] = up[j * piece : (j + 1) * piece]
    stores.append(pltpu.make_async_copy(ups, pay.at[:, pl.ds(0, piece), :], sems.at[first + 2]))
    stores[-1].start()
    loads[2].wait()
    a_half = down_v[...].astype(bf16)
    count = peers // 2
    for h in range(2):
        loads[3 + h].wait()
        down = dot(acts_v[h * half : (h + 1) * half, :], a_half).astype(bf16)
        for j in range(count):
            downs[h * count + j] = down[j * piece : (j + 1) * piece]
        mine = pl.ds(h * count, count)
        stores.append(
            pltpu.make_async_copy(
                downs.at[mine], pay.at[mine, pl.ds(piece, piece), :], sems.at[first + 3 + h]
            )
        )
        stores[-1].start()
    for c in stores:
        c.wait()


def base_part(place, prompts, frozen, i, cols):
    owner = place[0] ^ owner_mask(i)
    return dot(prompts[...], frozen[:, pl.ds(pl.multiple_of(owner * cols, cols), cols)])


def prompts_kernel(place, prompts, frozen, down_w, proj_out, send):
    rows = prompts.shape[0]
    cols = send.shape[1]
    count = send.shape[0] // rows
    for i in range(count):
        send[i * rows : (i + 1) * rows, :] = base_part(
            place, prompts, frozen, count + i, cols
        ).astype(bf16)
    proj_out[...] = dot(prompts[...], down_w[...].astype(bf16)).astype(bf16)


def own_half_kernel(place, prompts, frozen, got, keep, send):
    rows = prompts.shape[0]
    cols = send.shape[1]
    count = send.shape[0] // rows
    for i in range(2 * count):
        part = base_part(place, prompts, frozen, i, cols)
        part += got[i * rows : (i + 1) * rows, :].astype(f32)
        if i < count:
            keep[i * rows : (i + 1) * rows, :] = part
        else:
            send[(i - count) * rows : (i - count + 1) * rows, :] = part.astype(bf16)


def halve_kernel(held, got, keep, send, held_v, got_v, sems):
    loads = [
        pltpu.make_async_copy(held, held_v, sems.at[0]),
        pltpu.make_async_copy(got, got_v, sems.at[1]),
    ]
    for c in loads:
        c.start()
    for c in loads:
        c.wait()
    half = keep.shape[0]
    keep[...] = held_v[:half, :] + got_v[:half, :].astype(f32)
    send[...] = (held_v[half:, :] + got_v[half:, :].astype(f32)).astype(bf16)


def halve(held, got):
    dims = (held.shape[0] // 2, held.shape[1])
    return call(
        halve_kernel,
        [shape(dims, f32), shape(dims, bf16)],
        [HBM] * 2,
        (held, got),
        limit=60,
        scratch_shapes=[
            pltpu.VMEM(held.shape, f32),
            pltpu.VMEM(got.shape, bf16),
            pltpu.SemaphoreType.DMA((2,)),
        ],
    )


def sums_kernel(got_ref, proj, pay, pay_v, sem):
    peers, long, _ = pay.shape
    part = got_ref.shape[1]
    piece = long - part
    total = got_ref[0].astype(f32)
    for j in range(1, peers):
        total += got_ref[j].astype(f32)
    total = total.astype(bf16)
    for j in range(peers):
        pay_v[j, :part, :] = total
        pay_v[j, part:, :] = proj[j * piece : (j + 1) * piece, :]
    copy = pltpu.make_async_copy(pay_v, pay, sem)
    copy.start()
    copy.wait()


def rejoin(got_ref, first, piece):
    return jnp.concatenate(
        [got_ref[j, first : first + piece, :] for j in range(got_ref.shape[0])], axis=0
    )


def grads_kernel(got_ref, acts, gk, pay, pay_v, sem):
    rows = acts.shape[0]
    piece = rows // got_ref.shape[0]
    lanes = gk.shape[1]
    up = rejoin(got_ref, 0, piece)
    down = rejoin(got_ref, piece, piece)
    g = adapter_scale * jnp.concatenate([dot(up, acts[...], TN), dot(down, gk[...], TN)], axis=1)
    peers = pay.shape[0]
    step = g.shape[0] // peers
    for j in range(peers):
        pay_v[j] = jnp.concatenate(
            [
                g[j * step : (j + 1) * step, c * lanes : (c + 1) * lanes]
                for c in range(g.shape[1] // lanes)
            ],
            axis=0,
        ).astype(pay.dtype)
    copy = pltpu.make_async_copy(pay_v, pay, sem)
    copy.start()
    copy.wait()


def add_kernel(got_ref, pay, total_v, sems):
    total = got_ref[0].astype(f32)
    for j in range(1, got_ref.shape[0]):
        total += got_ref[j].astype(f32)
    total_v[...] = total.astype(pay.dtype)
    copies = [
        pltpu.make_async_copy(total_v, pay.at[j], sems.at[j]) for j in range(pay.shape[0])
    ]
    for c in copies:
        c.start()
    for c in copies:
        c.wait()


def add(got, peers):
    dims = got.shape[1:]
    (pay,) = call(
        add_kernel,
        [shape((peers,) + dims, bf16)],
        [VMEM],
        (got,),
        out_specs=(HBM,),
        scratch_shapes=[pltpu.VMEM(dims, bf16), pltpu.SemaphoreType.DMA((peers,))],
    )
    return pay


def whole_gradient(got_ref, rank):
    peers, long, _ = got_ref.shape
    step = rank // peers
    got = [got_ref[j].astype(f32) for j in range(peers)]
    return [
        jnp.concatenate([v[c * step : (c + 1) * step] for v in got], axis=0)
        for c in range(long // step)
    ]


def make_tail(total, rank):
    lane = lax.broadcasted_iota(jnp.int32, (TAIL, rank), 1)
    high = total.astype(bf16).astype(f32)
    middle = (total - high).astype(bf16).astype(f32)
    low = total - high - middle
    return jnp.where(
        lane == 0, high, jnp.where(lane == 1, middle, jnp.where(lane == 2, low, 0.0))
    ).astype(bf16)


def step_factor(got):
    peers, long, rank = got.shape
    piece = long - TAIL
    lane = lax.broadcasted_iota(jnp.int32, (TAIL, rank), 1)
    row = lax.broadcasted_iota(jnp.int32, (TAIL, rank), 0)
    tail = got[0, piece:, :].astype(f32)
    for j in range(1, peers):
        tail += got[j, piece:, :].astype(f32)
    squares = jnp.sum(jnp.where((row == 0) & (lane < 3), tail, 0.0), keepdims=True)
    return step_rate * jnp.minimum(1.0, clip_norm / jnp.sqrt(squares + 1e-12))


def project_kernel(got_ref, prompts, pay):
    peers, long, rank = pay.shape
    piece = long - TAIL
    blocks = whole_gradient(got_ref, rank)
    tail = make_tail(jnp.sum(sum(b * b for b in blocks), keepdims=True), rank)
    g_down = jnp.concatenate(blocks[:-1], axis=1).astype(bf16)
    proj = dot(prompts[...], g_down, NT).astype(bf16)
    for j in range(peers):
        pay[j, :piece, :] = proj[j * piece : (j + 1) * piece]
        pay[j, piece:, :] = tail


def rows_kernel(got, pa_rows, pay):
    peers, piece, _ = pay.shape
    p_g = got[0, :piece, :].astype(f32)
    for j in range(1, peers):
        p_g += got[j, :piece, :].astype(f32)
    rows = (pa_rows[...].astype(f32) - step_factor(got) * p_g).astype(bf16)
    for j in range(peers):
        pay[j] = rows


def finish_kernel(
    got, sums, base, base_got, got_g, down_w, up_w, next_down, next_up, keys,
    down_v, up_v, keys_v, sems,
):
    rank = down_w.shape[1]
    factor = step_factor(sums)
    blocks = whole_gradient(got_g, rank)
    new_up = up_w[...] - factor * blocks[-1]
    up_v[...] = new_up
    copies = [pltpu.make_async_copy(up_v, next_up, sems.at[0])]
    copies[-1].start()
    for c, part in enumerate(blocks[:-1]):
        here = pl.ds(c * rank, rank)
        down_v[here, :] = down_w[here, :] - factor * part.T
        copies.append(pltpu.make_async_copy(down_v.at[here], next_down.at[here], sems.at[2 + c]))
        copies[-1].start()
    keys_v[...] = (
        base[...]
        + base_got[...].astype(f32)
        + adapter_scale * dot(rejoin(got, 0, got.shape[1]), new_up.astype(bf16))
    ).astype(bf16)
    copies.append(pltpu.make_async_copy(keys_v, keys, sems.at[1]))
    copies[-1].start()
    for c in copies:
        c.wait()


def input_kernel(place, near, far, up, down_w, frozen, out, gk):
    rows = out.shape[0]
    lanes = near.shape[1]
    count = near.shape[0] // rows
    for i in range(2 * count):
        ref = near if i < count else far
        block = ref[(i % count) * rows : (i % count + 1) * rows, :]
        owner = place[0] ^ owner_mask(i)
        gk[:, pl.ds(pl.multiple_of(owner * lanes, lanes), lanes)] = block
    a_half = down_w[...].astype(bf16)
    out[...] = (
        dot(gk[...], frozen[...], NT) + adapter_scale * dot(up[...], a_half, NT)
    ).astype(bf16)


def beside_kernel(got, two, other, pa_out, up_out, four):
    count = two.shape[0]
    four[:count, :] = two[...]
    four[count:, :] = other[...]
    peers = got.shape[0]
    piece = pa_out.shape[0]
    up_out[...] = rejoin(got, 0, piece)
    total = got[0, 2 * piece :, :].astype(f32)
    for j in range(1, peers):
        total += got[j, 2 * piece :, :].astype(f32)
    pa_out[...] = total.astype(bf16)


def per_device(acts, output_gradient, lengths, buckets, frozen, down_w, up_w, prompts):
    rows = acts.shape[0]
    width, rank = down_w.shape
    cols = up_w.shape[1]
    n_f = lax.axis_size(FSDP)
    n_near = lax.axis_size(NEAR)
    n_far = lax.axis_size(FAR)
    piece = rows // n_f
    slab = (width + cols) // n_near

    gk, two, pay = call(
        parts_kernel,
        [shape((rows, cols), bf16), shape((2 * rows, cols), bf16), shape((n_f, 2 * piece, rank), bf16)],
        [SMEM, SMEM] + [ANY] * 4,
        (lengths, buckets, acts, output_gradient, down_w, up_w),
        flops=2 * rows * rank * (width + cols),
        out_specs=(HBM, HBM, HBM),
        limit=60,
        scratch_shapes=[
            pltpu.VMEM((rows, width), bf16),
            pltpu.VMEM((rows, cols), bf16),
            pltpu.VMEM((width, rank), f32),
            pltpu.VMEM((rank, cols), f32),
            pltpu.VMEM((rows, cols), bf16),
            pltpu.VMEM((n_f, piece, rank), bf16),
            pltpu.VMEM((n_f, piece, rank), bf16),
            pltpu.SemaphoreType.DMA((10,)),
        ],
    )
    got = swap(pay, PEERS)
    other = lax.ppermute(gk, "zlo", Z_PAIRS)
    place = lax.axis_index(FSDP).reshape(1)
    proj, send = call(
        prompts_kernel,
        [shape((rows, rank), bf16), shape((n_f // 2 * rows, cols), bf16)],
        [SMEM] + [VMEM] * 3,
        (place, prompts, frozen, down_w),
        flops=rows * width * (cols * n_f + 2 * rank),
    )
    got, proj, send, other = lax.optimization_barrier((got, proj, send, other))
    (pay,) = call(
        sums_kernel,
        [shape((n_f, 3 * piece, rank), bf16)],
        [VMEM] * 2,
        (got, proj),
        out_specs=(HBM,),
        scratch_shapes=[pltpu.VMEM((n_f, 3 * piece, rank), bf16), pltpu.SemaphoreType.DMA],
    )
    got = swap(pay, PEERS)
    two = lax.dynamic_update_slice(two, other, (rows, 0))
    other = lax.ppermute(two, "x", X_FAR)
    base_got = lax.ppermute(send, "x", X_NEAR)
    got, two = lax.optimization_barrier((got, two))

    (pay,) = call(
        grads_kernel,
        [shape((n_near, slab, rank), bf16)],
        [VMEM] * 3,
        (got, acts, gk),
        flops=2 * rows * rank * (width + cols),
        out_specs=(HBM,),
        scratch_shapes=[pltpu.VMEM((n_near, slab, rank), bf16), pltpu.SemaphoreType.DMA],
    )
    got_g = swap(pay, NEAR)
    pa_rows, up, four = call(
        beside_kernel,
        [
            shape((piece, rank), bf16),
            shape((rows, rank), bf16),
            shape((n_f // 2 * rows, cols), bf16),
        ],
        [VMEM] * 3,
        (got, two, other),
    )
    other = lax.ppermute(four, "x", X_NEAR)
    held, send = call(
        own_half_kernel,
        [shape((n_f // 4 * rows, cols), f32), shape((n_f // 4 * rows, cols), bf16)],
        [SMEM] + [VMEM] * 3,
        (place, prompts, frozen, base_got),
        flops=rows * width * cols * n_f,
    )
    got_g, pa_rows, up, held, send = lax.optimization_barrier((got_g, pa_rows, up, held, send))
    base_got = lax.ppermute(send, "x", X_FAR)
    got = swap(add(got_g, n_far), FAR)
    got_g = swap(add(got, n_near), NEAR)
    (input_gradient,) = call(
        input_kernel,
        [shape((rows, width), bf16)],
        [SMEM] + [VMEM] * 5,
        (place, four, other, up, down_w, frozen),
        flops=2 * rows * width * (cols * n_f + rank),
        scratch_shapes=[pltpu.VMEM((rows, cols * n_f), bf16)],
    )
    base, send = halve(held, base_got)
    base_got = lax.ppermute(send, "zlo", Z_PAIRS)
    got_g, input_gradient, base, base_got = lax.optimization_barrier(
        (got_g, input_gradient, base, base_got)
    )
    (pay,) = call(
        project_kernel,
        [shape((n_f, piece + TAIL, rank), bf16)],
        [VMEM] * 2,
        (got_g, prompts),
        flops=2 * rows * width * rank,
    )
    sums = swap(pay, PEERS)
    (pay,) = call(
        rows_kernel, [shape((n_f, piece, rank), bf16)], [VMEM] * 2, (sums, pa_rows)
    )
    got = swap(pay, PEERS)
    next_down, next_up, keys = call(
        finish_kernel,
        [shape((width, rank), f32), shape((rank, cols), f32), shape((rows, cols), bf16)],
        [VMEM] * 7,
        (got, sums, base, base_got, got_g, down_w, up_w),
        flops=2 * rows * rank * cols,
        out_specs=(HBM, HBM, HBM),
        scratch_shapes=[
            pltpu.VMEM((width, rank), f32),
            pltpu.VMEM((rank, cols), f32),
            pltpu.VMEM((rows, cols), bf16),
            pltpu.SemaphoreType.DMA((2 + width // rank,)),
        ],
    )
    return input_gradient, next_down, next_up, keys


def solution(mesh):
    dp, fsdp, section = mesh.devices.shape
    fine = Mesh(mesh.devices.reshape(4, dp // 4, fsdp // 2, 2, section), AXES)
    rows_by_width = P(ROWS, FSDP)
    return jax.shard_map(
        per_device,
        mesh=fine,
        in_specs=(
            rows_by_width,
            rows_by_width,
            P(ROWS),
            P(ROWS),
            P(FSDP, None),
            P(FSDP, None),
            P(None, FSDP),
            rows_by_width,
        ),
        out_specs=(rows_by_width, P(FSDP, None), P(None, FSDP), rows_by_width),
        check_vma=False,
    )
```
